256 devices in a mesh: band: 8 (over y, core), fft: 32 (over x, z).
Axes of the slice: x: 4, y: 4, z: 8, core: 2. Of those that a mesh axis runs over, the one named last changes fastest.
Arguments:
- current: float32 [2, 64, 98304], P(None, 'band', 'fft'), may hold values from -100 to 100
- h_current: float32 [2, 64, 98304], P(None, 'band', 'fft'), may hold values from -100 to 100
- previous: float32 [2, 64, 98304], P(None, 'band', 'fft'), may hold values from -100 to 100
- h_previous: float32 [2, 64, 98304], P(None, 'band', 'fft'), may hold values from -100 to 100
- eigen_values: float32 [64], P('band'), may hold values from -1 to 3
- potential: float32 [96, 96, 96], P('fft'), may hold values from -3 to 1
- stick_cols: int32 [4096], replicated, may hold values from -1 to 9215, as said below
- g_map: int32 [98304], P('fft'), may hold values from -1 to 12287, as said below
Outputs:
- h_residual: float32 [2, 64, 98304], P(None, 'band', 'fft')
- correlation_matrix: float32 [2, 192, 192], P(None, 'band', 'fft')
- hamiltonian_matrix: float32 [2, 192, 192], P(None, 'band', 'fft')
The draws below stay inside these ranges and needn't reach their ends.
Inputs may be any that keep to these rules, and one draw needn't show every extreme that they name: `stick_cols`: each grid column x * 96 + y whose signed frequencies satisfy x*x + y*y <= 24^2 is named by exactly one slot and all other slots are -1; fft device d owns slots d * 128 to (d + 1) * 128 - 1, its named slots are its last ones, and the numbers of named slots of two devices differ by at most one. `g_map`: the live entries of an fft device come first among its 3072 entries and name each G-vector of its named sticks once: local slot s and grid index z such that the signed frequencies of the stick's column and of z satisfy x*x + y*y + z*z <= 24^2; all other entries are -1.
All inputs are finite; a program needn't handle non-finite values.
Results may differ from the reference program's by a relative error of at most 0.00005.
Values sent between devices are 32-bit elements; how exact they have to be, the bound alone decides.
A program may use at most 64 MiB of HBM per device.

```python
import jax
import jax.numpy as jnp
import numpy as np
from jax import lax

L = 96
NB = 64
NS_DEV = 128
NG_DEV = 3072
NG = 98304
N_FFT = 32


def stick_layout(key):
    frequency = jnp.arange(L, dtype=jnp.int32)
    signed_freq = jnp.where(frequency >= L // 2, frequency - L, frequency)
    radius_sq = L // 4 * (L // 4)
    inside = (signed_freq[:, None] * signed_freq[:, None] + signed_freq[None, :] * signed_freq[None, :] <= radius_sq).reshape(-1)
    inside_count = sum((1 for row_at in range(L) for col_at in range(L) if min(row_at, L - row_at) ** 2 + min(col_at, L - col_at) ** 2 <= radius_sq))
    shuffle = jax.random.permutation(key, L * L).astype(jnp.int32)
    columns = jnp.arange(L * L, dtype=jnp.int32)
    priority = jnp.where(columns == 0, -1, jnp.where(inside, shuffle, L * L + shuffle))
    ordered = jnp.argsort(priority)[:inside_count].astype(jnp.int32)
    position = jnp.arange(inside_count, dtype=jnp.int32)
    owner = position % N_FFT
    within = position // N_FFT
    slots = owner * NS_DEV + NS_DEV - 1 - within
    return jnp.full((NS_DEV * N_FFT,), -1, jnp.int32).at[slots].set(ordered)


def shared_parts(key, scale_low, scale_high):
    scale_key, common_key = jax.random.split(key)
    log_scale = jax.random.uniform(scale_key, (NG,), jnp.float32, np.log(scale_low), np.log(scale_high))
    commons = jnp.clip(jax.random.normal(common_key, (4, 2, NG), jnp.float32), -4.0, 4.0)
    return (jnp.exp(log_scale), commons)


def combine(key, noise, commons, g_scale, spread):
    weights = jax.random.uniform(jax.random.fold_in(key, 2), (4, NB), jnp.float32, -spread, spread)
    values = noise
    for member in range(4):
        values = values + weights[member][None, :, None] * commons[member][:, None, :]
    return values * g_scale[None, None, :]


def draw_stick_cols(key, part):
    layout = stick_layout(key)
    return layout


def draw_g_map(key, part):
    stick_cols = stick_layout(key)
    key = jax.random.fold_in(key, 7)
    frequency = jnp.arange(L, dtype=jnp.int32)
    signed_freq = jnp.where(frequency >= L // 2, frequency - L, frequency)
    columns = stick_cols.reshape(N_FFT, NS_DEV)
    named = columns >= 0
    safe_cols = jnp.where(named, columns, 0)
    x_freq = signed_freq[safe_cols // L]
    y_freq = signed_freq[safe_cols % L]
    radial = x_freq * x_freq + y_freq * y_freq
    radius_sq = L // 4 * (L // 4)
    live_cells = named[:, :, None] & (radial[:, :, None] + (signed_freq * signed_freq)[None, None, :] <= radius_sq)
    flat_live = live_cells.reshape(N_FFT, NS_DEV * L)
    packed = jnp.cumsum(flat_live.astype(jnp.int32), axis=1) - 1
    target = jnp.where(flat_live, packed, NG_DEV)
    local_index = jnp.arange(NS_DEV * L, dtype=jnp.int32)

    def fill_device(targets):
        return jnp.full((NG_DEV,), -1, jnp.int32).at[targets].set(local_index, mode='drop')
    return jax.vmap(fill_device)(target).reshape(-1)


def draw_current(key, part):
    g_scale, commons = shared_parts(key, 0.4, 4.0)
    key = jax.random.fold_in(key, 3)
    noise = jnp.clip(jax.random.normal(jax.random.fold_in(key, 1), (2, NB, NG), jnp.float32), -4.0, 4.0)
    return combine(key, noise, commons, g_scale, 0.7)


def draw_h_current(key, part):
    g_scale, commons = shared_parts(key, 0.4, 4.0)
    key = jax.random.fold_in(key, 4)
    noise = jnp.clip(jax.random.normal(jax.random.fold_in(key, 1), (2, NB, NG), jnp.float32), -4.0, 4.0)
    return combine(key, noise, commons, g_scale, 0.7)


def draw_previous(key, part):
    g_scale, commons = shared_parts(key, 0.4, 4.0)
    key = jax.random.fold_in(key, 5)
    noise = jnp.clip(jax.random.normal(jax.random.fold_in(key, 1), (2, NB, NG), jnp.float32), -4.0, 4.0)
    return combine(key, noise, commons, g_scale, 0.7)


def draw_h_previous(key, part):
    g_scale, commons = shared_parts(key, 0.4, 4.0)
    key = jax.random.fold_in(key, 6)
    noise = jnp.clip(jax.random.normal(jax.random.fold_in(key, 1), (2, NB, NG), jnp.float32), -4.0, 4.0)
    return combine(key, noise, commons, g_scale, 0.7)


def shard_levels(rng, extent, shards, smallest, largest):
    gain, own = 1.0, jax.random.fold_in(rng, 6)
    for dim, blocks in shards:
        draws = jnp.exp(jax.random.uniform(jax.random.fold_in(own, dim), (blocks,), jnp.float32, smallest / len(shards), largest / len(shards)))
        gain = gain * jnp.repeat(draws, extent[dim] // blocks).reshape([-1 if axis == dim else 1 for axis in range(len(extent))])
    return gain


def setup_inputs(seed: int = 0) -> dict:
    key_of = jax.random.split(jax.random.key(seed), 9)
    return {
        "current": draw_current(jax.random.fold_in(key_of[8], 71), 0),
        "h_current": draw_h_current(jax.random.fold_in(key_of[8], 71), 0),
        "previous": draw_previous(jax.random.fold_in(key_of[8], 71), 0),
        "h_previous": draw_h_previous(jax.random.fold_in(key_of[8], 71), 0),
        "eigen_values": jnp.clip(-1.0 + 4.0 * jax.random.uniform(key_of[4], (NB,), jnp.float32) ** shard_levels(key_of[4], (NB,), ((0, 8),), -0.2, 0.2), -1.0, 3.0),
        "potential": jnp.clip(-3.0 + 4.0 * jax.random.uniform(key_of[5], (L, L, L), jnp.float32) ** shard_levels(key_of[5], (L, L, L), ((0, 32),), -0.2, 0.2), -3.0, 1.0),
        "stick_cols": draw_stick_cols(jax.random.fold_in(key_of[8], 71), 0),
        "g_map": draw_g_map(jax.random.fold_in(key_of[8], 71), 0),
    }


def signed_index(values):
    return jnp.where(values >= L // 2, values - L, values)


def slot_geometry(stick_cols, g_map):
    device_rows = g_map.reshape(N_FFT, NG_DEV)
    live_mask = device_rows >= 0
    safe_rows = jnp.where(live_mask, device_rows, 0).astype(jnp.int32)
    offsets = (jnp.arange(N_FFT, dtype=jnp.int32) * NS_DEV)[:, None]
    stick_index = (offsets + safe_rows // L).astype(jnp.int32)
    z_index = safe_rows % L
    column = jnp.where(live_mask, stick_cols[stick_index], 0).astype(jnp.int32)
    x_freq = signed_index(column // L)
    y_freq = signed_index(column % L)
    z_freq = signed_index(z_index)
    norm_sq = x_freq * x_freq + y_freq * y_freq + z_freq * z_freq
    kinetic = jnp.where(live_mask, 64.0 * norm_sq.astype(jnp.float32) / float(L * L), 0.0).astype(jnp.float32)
    cell = jnp.where(live_mask, z_index * (L * L) + column, L * L * L).astype(jnp.int32)
    return live_mask.reshape(-1), kinetic.reshape(-1), cell.reshape(-1)


def potential_on_band(pair, cell, live_mask, potential):
    spectrum = lax.complex(pair[0], pair[1])
    grid_cells = jnp.zeros((L * L * L,), spectrum.dtype).at[cell].set(spectrum, mode="drop")
    real_field = jnp.fft.ifftn(grid_cells.reshape(L, L, L)) * potential
    result_grid = jnp.fft.fftn(real_field).reshape(-1)
    picked = result_grid[jnp.minimum(cell, L * L * L - 1)]
    return jnp.stack([jnp.where(live_mask, picked.real, 0.0), jnp.where(live_mask, picked.imag, 0.0)])


def hermitian(left_block, right_block):
    real_part = jnp.dot(left_block[0], right_block[0].T, precision=lax.Precision.HIGHEST, preferred_element_type=jnp.float32)
    real_part = real_part + jnp.dot(left_block[1], right_block[1].T, precision=lax.Precision.HIGHEST, preferred_element_type=jnp.float32)
    imag_part = jnp.dot(left_block[0], right_block[1].T, precision=lax.Precision.HIGHEST, preferred_element_type=jnp.float32)
    imag_part = imag_part - jnp.dot(left_block[1], right_block[0].T, precision=lax.Precision.HIGHEST, preferred_element_type=jnp.float32)
    return jnp.stack([real_part, imag_part])


def reference(current, h_current, previous, h_previous, eigen_values, potential, stick_cols, g_map):
    live_mask, kinetic, cell = slot_geometry(stick_cols, g_map)
    residual = jnp.where(live_mask, (h_current - eigen_values[None, :, None] * current) / (1.0 + kinetic), 0.0)

    def one_band(pair):
        return potential_on_band(pair, cell, live_mask, potential)

    potential_term = jnp.transpose(lax.map(one_band, jnp.transpose(residual, (1, 0, 2))), (1, 0, 2))
    h_residual = jnp.where(live_mask, kinetic * residual + potential_term, 0.0)
    basis = jnp.concatenate([jnp.where(live_mask, current, 0.0), residual, jnp.where(live_mask, previous, 0.0)], axis=1)
    h_basis = jnp.concatenate([jnp.where(live_mask, h_current, 0.0), h_residual, jnp.where(live_mask, h_previous, 0.0)], axis=1)
    gram_scale = 8.0 / float(L ** 3)
    correlation_matrix = hermitian(basis, basis) * gram_scale
    hamiltonian_matrix = hermitian(basis, h_basis) * gram_scale
    return h_residual, correlation_matrix, hamiltonian_matrix
```

```python
import functools
import math

import jax
import jax.numpy as jnp
import ml_dtypes
import numpy as np
from jax import lax
from jax.experimental import pallas as pl
from jax.experimental.pallas import tpu as pltpu
from jax.sharding import PartitionSpec as P

L = 96
CUT = 24
F32 = jnp.float32
BF16 = jnp.bfloat16
NF = 32
NBD = 8
GT = 24
NPAIR = 25
MESH = pl.DeviceIdType.MESH
VM = pl.BlockSpec(memory_space=pltpu.VMEM)
SM = pl.BlockSpec(memory_space=pltpu.SMEM)


def split_np(table):
    high = table.astype(ml_dtypes.bfloat16)
    low = (table - high.astype(np.float64)).astype(ml_dtypes.bfloat16)
    return high, low


def tables():
    zout = (np.arange(NF)[None, :] * 3 + np.arange(3)[:, None]).reshape(-1)
    wz = np.zeros((2, 2, L, 2, 32))
    for par in range(2):
        zi = 2 * np.arange(32) + par
        ok = zi <= 2 * CUT
        ang = 2 * math.pi / L * ((zout[:, None] * (zi - CUT)[None, :]) % L)
        c, s = np.cos(ang) * ok, np.sin(ang) * ok
        wz[par, 0, :, 0], wz[par, 0, :, 1] = c, -s
        wz[par, 1, :, 0], wz[par, 1, :, 1] = s, c
    zh, zl = split_np(wz.reshape(384, 64))
    wz = np.concatenate([zh, zh, zl], axis=1)
    n = np.arange(L)
    k = np.arange(49) - CUT
    ang = 2 * math.pi / L * ((k[:, None] * n[None, :]) % L)
    c, s = np.cos(ang), np.sin(ang)
    wy = np.zeros((2, 64, 2, 128))
    wy[0, :49, 0, :L], wy[0, :49, 1, :L] = c, s
    wy[1, :49, 0, :L], wy[1, :49, 1, :L] = -s, c
    yh, yl = split_np(wy.reshape(128, 256))
    wy = np.concatenate([yh, yh, yl], axis=0)
    wx = np.zeros((2, L, 2, 56))
    wx[0, :, 0, :49], wx[0, :, 1, :49] = c.T, -s.T
    wx[1, :, 0, :49], wx[1, :, 1, :49] = s.T, c.T
    xh, xl = split_np(wx.reshape(192, 112))
    wxa = np.concatenate([xh, xh], axis=1)
    wxb = xl
    vx = np.zeros((2, 56, 2, L))
    vx[0, :49, 0], vx[0, :49, 1] = c, s
    vx[1, :49, 0], vx[1, :49, 1] = -s, c
    vh, vl = split_np(vx.reshape(112, 192))
    vx = np.concatenate([vh, vl], axis=0)
    vy = np.zeros((2, 128, 2, 64))
    vy[0, :L, 0, :49], vy[0, :L, 1, :49] = c.T, -s.T
    vy[1, :L, 0, :49], vy[1, :L, 1, :49] = s.T, c.T
    vyh, vyl = split_np(vy.reshape(256, 128))
    vy = np.concatenate([vyh, vyl], axis=1)
    vz = np.zeros((2, 64, L))
    ang = 2 * math.pi / L * ((k[:, None] * zout[None, :]) % L)
    vz[0, :49], vz[1, :49] = np.cos(ang), np.sin(ang)
    zbh, zbl = split_np(vz.reshape(128, L))
    vza = np.concatenate([zbh, zbh], axis=1)
    return dict(wz=wz, wy=wy, wxa=wxa, wxb=wxb, vx=vx, vy=vy, vza=vza, vzb=zbl)


def dot(a, b):
    return jnp.dot(a, b, preferred_element_type=F32)


def dot_nt(a, b):
    return lax.dot_general(a, b, (((1,), (1,)), ((), ())), preferred_element_type=F32)


def halves(x):
    hi = x.astype(BF16)
    return hi, (x - hi.astype(F32)).astype(BF16)


def low_lanes(shape):
    return lax.broadcasted_iota(jnp.int32, shape, len(shape) - 1) < 64


def swap(x):
    return pltpu.roll(x, 64, 1)


def div96(v):
    return (v * 43691) >> 22


def signed(v):
    return jnp.where(v >= L // 2, v - L, v)


def lanes_of(x, index):
    return jnp.take_along_axis(x, index, axis=1, mode="promise_in_bounds")


def slot_facts(m, cols):
    live = m >= 0
    ms = jnp.maximum(m, 0)
    slot = div96(ms)
    z = signed(ms - slot * L)
    col = jnp.where(live, lanes_of(cols, slot), 0)
    xc = div96(col)
    x = signed(xc)
    y = signed(col - xc * L)
    norm = x * x + y * y + z * z
    kin = jnp.where(live, 64.0 * norm.astype(F32) / float(L * L), 0.0)
    zi = z + CUT
    pair = jnp.where(live, zi >> 1, -1)
    lane = jnp.where(live, (zi & 1) * 64 + slot - 64, 0)
    return live, kin, pair, lane


def sticks_kernel(ev, cur, hcur, prev, hprev, gm, scols, wz, res, send, bsend, rt, inv, oh_l, oh_r, y):
    me = lax.axis_index("fft")
    cols = jnp.broadcast_to(scols[pl.ds(me, 1), :], (8, 128))
    row = lax.broadcasted_iota(jnp.int32, (8, 128), 0)
    evc = jnp.zeros((8, 128), F32)
    for b in range(8):
        evc = jnp.where(row == b, ev[b], evc)
    rows32 = lax.broadcasted_iota(jnp.int32, (32, 128), 0)
    rows128 = lax.broadcasted_iota(jnp.int32, (128, 128), 0)
    glo = lax.broadcasted_iota(jnp.int32, (32, 128), 1)
    for k in range(GT):
        at = pl.ds(128 * k, 128)
        d, lo = k // 3, (k % 3) * 128
        live, kin, pair, lane = slot_facts(jnp.broadcast_to(gm[:, at], (8, 128)), cols)
        den = 1.0 + kin
        for c in range(2):
            x, h = cur[c, :, at], hcur[c, :, at]
            r = jnp.where(live, (h - evc * x) / den, 0.0)
            rt[k, 8 * c : 8 * c + 8, :] = r
            res[8 * c : 8 * c + 8, at] = r
            bsend[d, c, :, lo : lo + 128] = jnp.where(live, x, 0.0)
            bsend[d, 2 + c, :, lo : lo + 128] = r
            bsend[d, 4 + c, :, lo : lo + 128] = jnp.where(live, prev[c, :, at], 0.0)
            bsend[d, 6 + c, :, lo : lo + 128] = jnp.where(live, h, 0.0)
            bsend[d, 8 + c, :, lo : lo + 128] = jnp.where(live, hprev[c, :, at], 0.0)
        hit = jnp.broadcast_to(pair[:1], (32, 128)) == rows32
        oh_l[0:32, at] = jnp.where(hit, float(k + 1), 0.0).astype(BF16)
        oh_l[32:64, at] = jnp.where(hit, glo.astype(F32), 0.0).astype(BF16)
        key = jnp.where(live, lane, -1)
        oh_r[:, at] = jnp.where(jnp.broadcast_to(key[:1], (128, 128)) == rows128, 1.0, 0.0).astype(BF16)
    inv[...] = dot_nt(oh_l[...], oh_r[...]).astype(jnp.int32)
    y[400:512, :] = jnp.zeros((112, 128), F32)

    def place(t, carry):
        hi = jnp.broadcast_to(inv[pl.ds(t, 1), :], (16, 128))
        lo = jnp.broadcast_to(inv[pl.ds(t + 32, 1), :], (16, 128))
        acc = jnp.zeros((16, 128), F32)
        for k in range(GT):
            acc = jnp.where(hi == k + 1, lanes_of(rt[k], lo), acc)
        y[pl.ds(pl.multiple_of(t * 16, 16), 16), :] = acc
        return carry

    lax.fori_loop(0, NPAIR, place, 0)
    low = low_lanes((192, 128))
    low96 = low_lanes((96, 128))
    for b2 in range(4):
        parts = []
        for b in (2 * b2, 2 * b2 + 1):
            s = jnp.concatenate([y[pl.ds(c * 8 + b, 32, stride=16), :] for c in range(2)], axis=0)
            hi, lo = halves(s)
            parts.append(jnp.concatenate([hi, lo, hi], axis=0))
        out = dot(wz[...], jnp.concatenate(parts, axis=1))
        for i in range(2):
            o = out[:, 128 * i : 128 * i + 128]
            w = jnp.where(low, o[:192], o[192:])
            w = w + swap(w)
            w = jnp.where(low96, w[:96], w[96:])
            for zl in range(3):
                send[pl.ds((2 * b2 + i) * 3 + zl, 32, stride=24), :] = w[32 * zl : 32 * zl + 32]


def everyone_in(peers_f, peers_b):
    f, b = lax.axis_index("fft"), lax.axis_index("band")
    barrier = pltpu.get_barrier_semaphore()
    if peers_f:
        def greet(i, c):
            pl.semaphore_signal(barrier, inc=1, device_id=(b, lax.rem(f + i, NF)), device_id_type=MESH)
            return c
        lax.fori_loop(1, NF, greet, 0)
    if peers_b:
        def greet_b(i, c):
            pl.semaphore_signal(barrier, inc=1, device_id=(lax.rem(b + i, NBD), f), device_id_type=MESH)
            return c
        lax.fori_loop(1, NBD, greet_b, 0)
    pl.semaphore_wait(barrier, (NF - 1) * peers_f + (NBD - 1) * peers_b)


class FftExchange:
    def __init__(self, src, dst, ssem, rsem, n):
        self.a = (src, dst, ssem, rsem, n)

    def copy(self, to, frm, i):
        src, dst, ssem, rsem, n = self.a
        return pltpu.make_async_remote_copy(
            src_ref=src.at[pl.ds(pl.multiple_of(to * n, 8), n), :],
            dst_ref=dst.at[pl.ds(pl.multiple_of(frm * n, 8), n), :],
            send_sem=ssem.at[i], recv_sem=rsem.at[i],
            device_id=(lax.axis_index("band"), to), device_id_type=MESH)

    def start(self):
        src, dst, ssem, rsem, n = self.a
        f = lax.axis_index("fft")
        def go(i, c):
            self.copy(lax.rem(f + i, NF), f, i).start()
            return c
        lax.fori_loop(1, NF, go, 0)
        own = pl.ds(pl.multiple_of(f * n, 8), n)
        pltpu.make_async_copy(src.at[own, :], dst.at[own, :], rsem.at[0]).start()

    def wait(self):
        src, dst, ssem, rsem, n = self.a
        f = lax.axis_index("fft")
        own = pl.ds(pl.multiple_of(f * n, 8), n)
        pltpu.make_async_copy(src.at[own, :], dst.at[own, :], rsem.at[0]).wait()
        def done(i, c):
            self.copy(lax.rem(f + i, NF), lax.rem(f + NF - i, NF), i).wait()
            return c
        lax.fori_loop(1, NF, done, 0)


class BandExchange:
    def __init__(self, src, dst, place, ssem, rsem):
        self.a = (src, dst, place, ssem, rsem)

    def copy(self, to, frm, i):
        src, dst, place, ssem, rsem = self.a
        return pltpu.make_async_remote_copy(
            src_ref=src.at[to], dst_ref=place(dst, frm), send_sem=ssem.at[i], recv_sem=rsem.at[i],
            device_id=(to, lax.axis_index("fft")), device_id_type=MESH)

    def start(self):
        src, dst, place, ssem, rsem = self.a
        b = lax.axis_index("band")
        for i in range(1, NBD):
            self.copy(lax.rem(b + i, NBD), b, i).start()
        pltpu.make_async_copy(src.at[b], place(dst, b), rsem.at[0]).start()

    def wait(self):
        src, dst, place, ssem, rsem = self.a
        b = lax.axis_index("band")
        pltpu.make_async_copy(src.at[b], place(dst, b), rsem.at[0]).wait()
        for i in range(1, NBD):
            self.copy(lax.rem(b + i, NBD), lax.rem(b + NBD - i, NBD), i).wait()


def band_rows(dst, frm):
    return dst.at[:, pl.ds(pl.multiple_of(frm * 8, 8), 8), :]


def band_slot(dst, frm):
    return dst.at[frm]


def out_kernel(send, bsend, recv, brecv, ssem, rsem, bssem, brsem):
    everyone_in(True, True)
    fx = FftExchange(send, recv, ssem, rsem, 24)
    bx = BandExchange(bsend, brecv, band_rows, bssem, brsem)
    fx.start()
    bx.start()
    fx.wait()
    bx.wait()


def plane_kernel(recv, scols, pot, wy, wxa, wxb, vx, vy, send, q, oh_l, oh_r, inv, pick, pm, tt, potp, gg, gt):
    low1 = low_lanes((1, 128))
    rows32 = lax.broadcasted_iota(jnp.int32, (32, 128), 0)
    rows128 = lax.broadcasted_iota(jnp.int32, (128, 128), 0)
    glo = lax.broadcasted_iota(jnp.int32, (32, 128), 1).astype(F32)
    low = low_lanes((24, 128))
    for k in range(16):
        col = jnp.where(low1, swap(scols[2 * k : 2 * k + 1, :]), scols[2 * k + 1 : 2 * k + 2, :])
        live = col >= 0
        colp = jnp.maximum(col, 0)
        xc = div96(colp)
        xi = signed(xc) + CUT
        yi = signed(colp - xc * L) + CUT
        pair = jnp.where(live, xi >> 1, -1)
        lane = jnp.where(live, (xi & 1) * 64 + yi, -1)
        pick[k : k + 1, :] = pair
        pick[16 + k : 17 + k, :] = jnp.maximum(lane, 0)
        at = pl.ds(128 * k, 128)
        hit = jnp.broadcast_to(pair, (32, 128)) == rows32
        oh_l[0:32, at] = jnp.where(hit, float(k + 1), 0.0).astype(BF16)
        oh_l[32:64, at] = jnp.where(hit, glo, 0.0).astype(BF16)
        oh_r[:, at] = jnp.where(jnp.broadcast_to(lane, (128, 128)) == rows128, 1.0, 0.0).astype(BF16)
        r0, r1 = recv[48 * k : 48 * k + 24, :], recv[48 * k + 24 : 48 * k + 48, :]
        q[k, 0:24, :] = jnp.where(low, r0, swap(r1))
        q[k, 24:48, :] = jnp.where(low, swap(r0), r1)
    inv[...] = dot_nt(oh_l[...], oh_r[...]).astype(jnp.int32)
    potp[...] = jnp.zeros((3, L, 128), F32)
    potp[:, :, 0:L] = pot[...]

    def place(t, carry):
        hi = jnp.broadcast_to(inv[pl.ds(t, 1), :], (48, 128))
        lo = jnp.broadcast_to(inv[pl.ds(t + 32, 1), :], (48, 128))
        acc = jnp.zeros((48, 128), F32)
        for k in range(16):
            acc = jnp.where(hi == k + 1, lanes_of(q[k], lo), acc)
        re, im = acc[:24], acc[24:]
        base = pl.multiple_of(t * 48, 16)
        pm[pl.ds(base, 24), :] = jnp.where(low, re, swap(im))
        pm[pl.ds(base + 24, 24), :] = jnp.where(low, swap(re), im)
        return carry

    lax.fori_loop(0, NPAIR, place, 0)

    def along_y(i, carry):
        at = pl.ds(pl.multiple_of(i * 240, 16), 240)
        hi, lo = halves(pm[at, :])
        out = dot(jnp.concatenate([hi, lo], axis=1), wy[0:256, :]) + dot(hi, wy[256:384, :])
        tt[0, at, :] = out[:, 0:128]
        tt[1, at, :] = out[:, 128:256]
        return carry

    lax.fori_loop(0, 5, along_y, 0)
    tt[:, 1200:1344, :] = jnp.zeros((2, 144, 128), F32)

    def along_x(i, carry):
        his, los = [], []
        for j in range(2):
            s = jnp.concatenate([tt[c, pl.ds(2 * i + j, 56, stride=24), :] for c in range(2)], axis=0)
            hi, lo = halves(s)
            his.append(hi)
            los.append(lo)
        hi = jnp.concatenate(his, axis=1)
        lo = jnp.concatenate(los, axis=1)
        u = dot(wxa[...], jnp.concatenate([hi, lo], axis=0)) + dot(wxb[...], hi)
        pv = jnp.concatenate([potp[lax.rem(2 * i + j, 3)] for j in range(2)], axis=1)
        u = u * jnp.concatenate([pv, pv], axis=0)
        hi, lo = halves(u)
        a = dot(vx[...], hi)
        t = a[0:112] + a[112:224] + dot(vx[0:112, :], lo)
        row = jnp.concatenate(
            [jnp.concatenate([t[0:56, 128 * j : 128 * j + 128], t[56:112, 128 * j : 128 * j + 128]], axis=1) for j in range(2)],
            axis=0)
        hi, lo = halves(row)
        a = dot(hi, vy[...])
        g = a[:, 0:128] + a[:, 128:256] + dot(lo, vy[:, 0:128])
        for j in range(2):
            gg[pl.ds(2 * i + j, 56, stride=24), :] = g[56 * j : 56 * j + 56]
        return carry

    lax.fori_loop(0, 12, along_x, 0)

    def pair_up(t, carry):
        base = pl.multiple_of(t * 48, 16)
        g0, g1 = gg[pl.ds(base, 24), :], gg[pl.ds(base + 24, 24), :]
        gt[t, 0:24, :] = jnp.where(low, g0, swap(g1))
        gt[t, 24:48, :] = jnp.where(low, swap(g0), g1)
        return carry

    lax.fori_loop(0, NPAIR, pair_up, 0)

    def collect(k, carry):
        hi = jnp.broadcast_to(pick[pl.ds(k, 1), :], (48, 128))
        lo = jnp.broadcast_to(pick[pl.ds(k + 16, 1), :], (48, 128))
        acc = jnp.zeros((48, 128), F32)
        for t in range(NPAIR):
            acc = jnp.where(hi == t, lanes_of(gt[t], lo), acc)
        re, im = acc[:24], acc[24:]
        base = pl.multiple_of(k * 48, 16)
        send[pl.ds(base, 24), :] = jnp.where(low, re, swap(im))
        send[pl.ds(base + 24, 24), :] = jnp.where(low, swap(re), im)
        return carry

    lax.fori_loop(0, 16, collect, 0)


def row_side(brecv, qs):
    zero = jnp.zeros((8, 768), F32)
    for d in range(NBD):
        for j in range(3):
            g8 = 3 * d + j
            ty, r0 = g8 // 8, (g8 % 8) * 8
            re, im = brecv[2 * ty, r0 : r0 + 8, :], brecv[2 * ty + 1, r0 : r0 + 8, :]
            o = 64 * d + 8 * j
            qs[o : o + 8, 0:384] = re
            qs[o : o + 8, 384:768] = im
            qs[o + 32 : o + 40, 0:384] = -im
            qs[o + 32 : o + 40, 384:768] = re
        qs[64 * d + 24 : 64 * d + 32, :] = zero
        qs[64 * d + 56 : 64 * d + 64, :] = zero


def back_kernel(send, brecv, recv, early, qs, flat, ks, esend, erecv, ssem, rsem, bssem, brsem):
    everyone_in(True, True)
    fx = FftExchange(send, recv, ssem, rsem, 24)
    fx.start()
    row_side(brecv, qs)
    for m in range(2):
        for ty in range(3):
            at = 64 * ty
            if m == 1 and ty == 1:
                flat[at : at + 64, :] = jnp.zeros((64, 768), F32)
                continue
            src = 2 * ty if m == 0 else (6 if ty == 0 else 8)
            flat[at : at + 64, 0:384] = brecv[src]
            flat[at : at + 64, 384:768] = brecv[src + 1]
        ks[256 * m : 256 * m + 256, :] = jnp.zeros((256, 768), F32)
        for f in range(NF):
            ks[256 * m + 8 * f : 256 * m + 8 * f + 6, :] = flat[6 * f : 6 * f + 6, :]
    khi, klo = halves(ks[...])
    low = low_lanes((256, 128))
    for n in range(2):
        qhi, qlo = halves(qs[256 * n : 256 * n + 256, :])
        g = dot_nt(khi, qhi) + dot_nt(klo, qhi) + dot_nt(khi, qlo)
        for j in range(2):
            c, h = g[0:256, 128 * j : 128 * j + 128], g[256:512, 128 * j : 128 * j + 128]
            esend[4 * n + 2 * j] = jnp.where(low, c, swap(h))
            esend[4 * n + 2 * j + 1] = jnp.where(low, swap(c), h)
    bx = BandExchange(esend, erecv, band_slot, bssem, brsem)
    bx.start()
    bx.wait()
    total = erecv[0]
    for d in range(1, NBD):
        total = total + erecv[d]
    early[...] = total
    fx.wait()


def term_kernel(recv, res, gm, scols, vza, vzb, hres, hsend, z, zt):
    for b2 in range(4):
        his, los = [], []
        for b in (2 * b2, 2 * b2 + 1):
            s = jnp.concatenate([recv[pl.ds(3 * b + zl, 32, stride=24), :] for zl in range(3)], axis=0)
            hi, lo = halves(s)
            his.append(hi)
            los.append(lo)
        hi = jnp.concatenate(his, axis=1)
        lo = jnp.concatenate(los, axis=1)
        out = dot(vza[...], jnp.concatenate([hi, lo], axis=0)) + dot(vzb[...], hi)
        low = low_lanes((64, 128))
        for i in range(2):
            o = out[:, 128 * i : 128 * i + 128]
            other = swap(o[64:128])
            z[pl.ds(2 * b2 + i, 64, stride=8), :] = o[0:64] + jnp.where(low, other, -other)
    low = low_lanes((8, 128))
    for t in range(NPAIR):
        z0, z1 = z[16 * t : 16 * t + 8, :], z[16 * t + 8 : 16 * t + 16, :]
        zt[t, 0:8, :] = jnp.where(low, z0, swap(z1))
        zt[t, 8:16, :] = jnp.where(low, swap(z0), z1)
    me = lax.axis_index("fft")
    cols = jnp.broadcast_to(scols[pl.ds(me, 1), :], (8, 128))
    for k in range(GT):
        at = pl.ds(128 * k, 128)
        live, kin, pair, lane = slot_facts(jnp.broadcast_to(gm[:, at], (8, 128)), cols)
        hi = jnp.concatenate([pair, pair], axis=0)
        lo = jnp.concatenate([lane, lane], axis=0)
        acc = jnp.zeros((16, 128), F32)
        for t in range(NPAIR):
            acc = jnp.where(hi == t, lanes_of(zt[t], lo), acc)
        for c in range(2):
            v = kin * res[8 * c : 8 * c + 8, at] + acc[8 * c : 8 * c + 8] * (1.0 / float(L**3))
            v = jnp.where(live, v, 0.0)
            hres[c, :, at] = v
            hsend[k // 3, c, :, (k % 3) * 128 : (k % 3) * 128 + 128] = v


F0, F1 = 10, 22


def late_kernel(hsend, brecv, early, out, hrecv, qs, flat, ks, lsend, lrecv, fsend, frecv,
                hssem, hrsem, bssem, brsem, ssem, rsem):
    everyone_in(True, True)
    hx = BandExchange(hsend, hrecv, band_rows, hssem, hrsem)
    hx.start()
    row_side(brecv, qs)
    ks[...] = jnp.zeros((96, 768), F32)
    hx.wait()
    flat[:, 0:384] = hrecv[0]
    flat[:, 384:768] = hrecv[1]
    for f in range(F0, F1):
        k0, k1 = max(6 * f, 64), min(6 * f + 6, 128)
        o = 8 * (f - F0) + k0 - 6 * f
        ks[o : o + k1 - k0, :] = flat[k0 - 64 : k1 - 64, :]
    khi, klo = halves(ks[...])
    low = low_lanes((48, 128))
    for n in range(2):
        qhi, qlo = halves(qs[256 * n : 256 * n + 256, :])
        g = dot_nt(khi, qhi) + dot_nt(klo, qhi) + dot_nt(khi, qlo)
        for j in range(2):
            a, b = g[0:48, 128 * j : 128 * j + 128], g[48:96, 128 * j : 128 * j + 128]
            lsend[4 * n + 2 * j] = jnp.where(low, a, swap(b))
            lsend[4 * n + 2 * j + 1] = jnp.where(low, swap(a), b)
    bx = BandExchange(lsend, lrecv, band_slot, bssem, brsem)
    bx.start()
    fsend[...] = early[...]
    bx.wait()
    total = lrecv[0]
    for d in range(1, NBD):
        total = total + lrecv[d]
    fsend[8 * F0 : 8 * F0 + 48, :] = fsend[8 * F0 : 8 * F0 + 48, :] + jnp.where(low, 0.0, swap(total))
    fsend[8 * F0 + 48 : 8 * F0 + 96, :] = fsend[8 * F0 + 48 : 8 * F0 + 96, :] + jnp.where(low, 0.0, total)
    fx = FftExchange(fsend, frecv, ssem, rsem, 8)
    fx.start()
    fx.wait()
    total = frecv[0:8, :]
    for d in range(1, NF):
        total = total + frecv[8 * d : 8 * d + 8, :]
    out[...] = total * (8.0 / float(L**3))


def sds(*shape):
    return jax.ShapeDtypeStruct(shape, F32)


DMA = pltpu.SemaphoreType.DMA
BIG = 48 * 1024 * 1024


def local(current, h_current, previous, h_previous, eigen_values, potential, stick_cols, g_map):
    w = tables()
    gm = g_map.reshape(1, 3072)
    sc = stick_cols.reshape(NF, 128)
    params = functools.partial(pltpu.CompilerParams, vmem_limit_bytes=BIG)
    res, send, bsend = pl.pallas_call(
        sticks_kernel,
        out_shape=(sds(16, 3072), sds(768, 128), sds(8, 10, 8, 384)),
        in_specs=[SM] + [VM] * 7, out_specs=(VM, VM, VM),
        scratch_shapes=[
            pltpu.VMEM((24, 16, 128), F32), pltpu.VMEM((64, 128), jnp.int32),
            pltpu.VMEM((64, 3072), BF16), pltpu.VMEM((128, 3072), BF16), pltpu.VMEM((512, 128), F32)],
        compiler_params=params(), name="sticks",
    )(eigen_values, current, h_current, previous, h_previous, gm, sc, w["wz"])
    recv, brecv = pl.pallas_call(
        out_kernel, out_shape=(sds(768, 128), sds(10, 64, 384)), in_specs=[VM, VM], out_specs=(VM, VM),
        scratch_shapes=[DMA((NF,)), DMA((NF,)), DMA((NBD,)), DMA((NBD,))],
        compiler_params=params(collective_id=0, has_side_effects=True), name="outward",
    )(send, bsend)
    send2 = pl.pallas_call(
        plane_kernel, out_shape=sds(768, 128), in_specs=[VM] * 8, out_specs=VM,
        scratch_shapes=[
            pltpu.VMEM((16, 48, 128), F32), pltpu.VMEM((64, 2048), BF16), pltpu.VMEM((128, 2048), BF16),
            pltpu.VMEM((64, 128), jnp.int32), pltpu.VMEM((32, 128), jnp.int32), pltpu.VMEM((1200, 128), F32),
            pltpu.VMEM((2, 1344, 128), F32), pltpu.VMEM((3, L, 128), F32), pltpu.VMEM((1344, 128), F32),
            pltpu.VMEM((NPAIR, 48, 128), F32)],
        compiler_params=params(), name="planes",
    )(recv, sc, potential, w["wy"], w["wxa"], w["wxb"], w["vx"], w["vy"])
    recv2, early = pl.pallas_call(
        back_kernel, out_shape=(sds(768, 128), sds(256, 128)), in_specs=[VM, VM], out_specs=(VM, VM),
        scratch_shapes=[
            pltpu.VMEM((512, 768), F32), pltpu.VMEM((192, 768), F32), pltpu.VMEM((512, 768), F32),
            pltpu.VMEM((8, 256, 128), F32), pltpu.VMEM((8, 256, 128), F32),
            DMA((NF,)), DMA((NF,)), DMA((NBD,)), DMA((NBD,))],
        compiler_params=params(collective_id=1, has_side_effects=True), name="inward",
    )(send2, brecv)
    hres, hsend = pl.pallas_call(
        term_kernel, out_shape=(sds(2, 8, 3072), sds(8, 2, 8, 384)), in_specs=[VM] * 6, out_specs=(VM, VM),
        scratch_shapes=[pltpu.VMEM((512, 128), F32), pltpu.VMEM((NPAIR, 16, 128), F32)],
        compiler_params=params(), name="term",
    )(recv2, res, gm, sc, w["vza"], w["vzb"])
    tile = pl.pallas_call(
        late_kernel, out_shape=sds(8, 128), in_specs=[VM] * 3, out_specs=VM,
        scratch_shapes=[
            pltpu.VMEM((2, 64, 384), F32), pltpu.VMEM((512, 768), F32), pltpu.VMEM((64, 768), F32),
            pltpu.VMEM((96, 768), F32), pltpu.VMEM((8, 48, 128), F32), pltpu.VMEM((8, 48, 128), F32),
            pltpu.VMEM((256, 128), F32), pltpu.VMEM((256, 128), F32),
            DMA((NBD,)), DMA((NBD,)), DMA((NBD,)), DMA((NBD,)), DMA((NF,)), DMA((NF,))],
        compiler_params=params(collective_id=2, has_side_effects=True), name="late",
    )(hsend, brecv, early)
    mats = jnp.transpose(tile[0:6].reshape(6, 4, 32)[:, :, 0:24], (1, 2, 0))
    return hres, mats[0:2], mats[2:4]


def solution(mesh):
    bf = P(None, "band", "fft")
    in_specs = (bf, bf, bf, bf, P("band"), P("fft", None, None), P(), P("fft"))
    return jax.shard_map(local, mesh=mesh, in_specs=in_specs, out_specs=(bf, bf, bf), check_vma=False)
```

```python
import math

import jax
import jax.numpy as jnp
import ml_dtypes
import numpy as np
from jax import lax
from jax.experimental import pallas as pl
from jax.experimental.pallas import tpu as pltpu
from jax.sharding import PartitionSpec as P

L = 96
CUT = 24
F32 = jnp.float32
BF16 = jnp.bfloat16
NF = 32
NBD = 8
GT = 24
NPAIR = 25
MESH = pl.DeviceIdType.MESH
VM = pl.BlockSpec(memory_space=pltpu.VMEM)
HB = pl.BlockSpec(memory_space=pltpu.HBM)
SM = pl.BlockSpec(memory_space=pltpu.SMEM)


def split_np(table):
    high = table.astype(ml_dtypes.bfloat16)
    low = (table - high.astype(np.float64)).astype(ml_dtypes.bfloat16)
    return high, low


def tables():
    zout = (np.arange(NF)[None, :] * 3 + np.arange(3)[:, None]).reshape(-1)
    wz = np.zeros((2, 2, L, 2, 32))
    for par in range(2):
        zi = 2 * np.arange(32) + par
        ok = zi <= 2 * CUT
        ang = 2 * math.pi / L * ((zout[:, None] * (zi - CUT)[None, :]) % L)
        c, s = np.cos(ang) * ok, np.sin(ang) * ok
        wz[par, 0, :, 0], wz[par, 0, :, 1] = c, -s
        wz[par, 1, :, 0], wz[par, 1, :, 1] = s, c
    zh, zl = split_np(wz.reshape(384, 64))
    wz = np.concatenate([zh, zh, zl], axis=1)
    n = np.arange(L)
    k = np.arange(49) - CUT
    ang = 2 * math.pi / L * ((k[:, None] * n[None, :]) % L)
    c, s = np.cos(ang), np.sin(ang)
    wy = np.zeros((2, 64, 2, 128))
    wy[0, :49, 0, :L], wy[0, :49, 1, :L] = c, s
    wy[1, :49, 0, :L], wy[1, :49, 1, :L] = -s, c
    yh, yl = split_np(wy.reshape(128, 256))
    wy = np.concatenate([yh, yh, yl], axis=0)
    wx = np.zeros((2, L, 2, 56))
    wx[0, :, 0, :49], wx[0, :, 1, :49] = c.T, -s.T
    wx[1, :, 0, :49], wx[1, :, 1, :49] = s.T, c.T
    xh, xl = split_np(wx.reshape(192, 112))
    wxa = np.concatenate([xh, xh], axis=1)
    wxb = xl
    vx = np.zeros((2, 56, 2, L))
    vx[0, :49, 0], vx[0, :49, 1] = c, s
    vx[1, :49, 0], vx[1, :49, 1] = -s, c
    vh, vl = split_np(vx.reshape(112, 192))
    vx = np.concatenate([vh, vl], axis=0)
    vy = np.zeros((2, 128, 2, 64))
    vy[0, :L, 0, :49], vy[0, :L, 1, :49] = c.T, -s.T
    vy[1, :L, 0, :49], vy[1, :L, 1, :49] = s.T, c.T
    vyh, vyl = split_np(vy.reshape(256, 128))
    vy = np.concatenate([vyh, vyl], axis=1)
    vz = np.zeros((2, 64, L))
    ang = 2 * math.pi / L * ((k[:, None] * zout[None, :]) % L)
    vz[0, :49], vz[1, :49] = np.cos(ang), np.sin(ang)
    zbh, zbl = split_np(vz.reshape(128, L))
    vza = np.concatenate([zbh, zbh], axis=1)
    return dict(wz=wz, wy=wy, wxa=wxa, wxb=wxb, vx=vx, vy=vy, vza=vza, vzb=zbl)


def dot(a, b):
    return jnp.dot(a, b, preferred_element_type=F32)


def dot_nt(a, b):
    return lax.dot_general(a, b, (((1,), (1,)), ((), ())), preferred_element_type=F32)


def halves(x):
    hi = x.astype(BF16)
    return hi, (x - hi.astype(F32)).astype(BF16)


def low_lanes(shape):
    return lax.broadcasted_iota(jnp.int32, shape, len(shape) - 1) < 64


def swap(x):
    return pltpu.roll(x, 64, 1)


def div96(v):
    return (v * 43691) >> 22


def signed(v):
    return jnp.where(v >= L // 2, v - L, v)


def lanes_of(x, index):
    return jnp.take_along_axis(x, index, axis=1, mode="promise_in_bounds")


def slot_facts(m, cols):
    live = m >= 0
    ms = jnp.maximum(m, 0)
    slot = div96(ms)
    z = signed(ms - slot * L)
    col = jnp.where(live, lanes_of(cols, slot), 0)
    xc = div96(col)
    x = signed(xc)
    y = signed(col - xc * L)
    norm = x * x + y * y + z * z
    kin = jnp.where(live, 64.0 * norm.astype(F32) / float(L * L), 0.0)
    zi = z + CUT
    pair = jnp.where(live, zi >> 1, -1)
    lane = jnp.where(live, (zi & 1) * 64 + slot - 64, 0)
    return live, kin, pair, lane


def sticks_kernel(ev, cur, hcur, prev, hprev, gm, scols, wz, res, send, bsend, rt, inv, oh_l, oh_r, y):
    me = lax.axis_index("fft")
    cols = jnp.broadcast_to(scols[pl.ds(me, 1), :], (8, 128))
    row = lax.broadcasted_iota(jnp.int32, (8, 128), 0)
    evc = jnp.zeros((8, 128), F32)
    for b in range(8):
        evc = jnp.where(row == b, ev[b], evc)
    rows32 = lax.broadcasted_iota(jnp.int32, (32, 128), 0)
    rows128 = lax.broadcasted_iota(jnp.int32, (128, 128), 0)
    glo = lax.broadcasted_iota(jnp.int32, (32, 128), 1)
    for k in range(GT):
        at = pl.ds(128 * k, 128)
        d, lo = k // 3, (k % 3) * 128
        live, kin, pair, lane = slot_facts(jnp.broadcast_to(gm[:, at], (8, 128)), cols)
        den = 1.0 + kin
        for c in range(2):
            x, h = cur[c, :, at], hcur[c, :, at]
            r = jnp.where(live, (h - evc * x) / den, 0.0)
            rt[k, 8 * c : 8 * c + 8, :] = r
            res[8 * c : 8 * c + 8, at] = r
            bsend[d, c, :, lo : lo + 128] = jnp.where(live, x, 0.0)
            bsend[d, 2 + c, :, lo : lo + 128] = r
            bsend[d, 4 + c, :, lo : lo + 128] = jnp.where(live, prev[c, :, at], 0.0)
            bsend[d, 6 + c, :, lo : lo + 128] = jnp.where(live, h, 0.0)
            bsend[d, 8 + c, :, lo : lo + 128] = jnp.where(live, hprev[c, :, at], 0.0)
        hit = jnp.broadcast_to(pair[:1], (32, 128)) == rows32
        oh_l[0:32, at] = jnp.where(hit, float(k + 1), 0.0).astype(BF16)
        oh_l[32:64, at] = jnp.where(hit, glo.astype(F32), 0.0).astype(BF16)
        key = jnp.where(live, lane, -1)
        oh_r[:, at] = jnp.where(jnp.broadcast_to(key[:1], (128, 128)) == rows128, 1.0, 0.0).astype(BF16)
    inv[...] = dot_nt(oh_l[...], oh_r[...]).astype(jnp.int32)
    y[400:512, :] = jnp.zeros((112, 128), F32)

    def place(t, carry):
        hi = jnp.broadcast_to(inv[pl.ds(t, 1), :], (16, 128))
        lo = jnp.broadcast_to(inv[pl.ds(t + 32, 1), :], (16, 128))
        acc = jnp.zeros((16, 128), F32)
        for k in range(GT):
            acc = jnp.where(hi == k + 1, lanes_of(rt[k], lo), acc)
        y[pl.ds(pl.multiple_of(t * 16, 16), 16), :] = acc
        return carry

    lax.fori_loop(0, NPAIR, place, 0)
    low = low_lanes((192, 128))
    low96 = low_lanes((96, 128))
    for b2 in range(4):
        parts = []
        for b in (2 * b2, 2 * b2 + 1):
            s = jnp.concatenate([y[pl.ds(c * 8 + b, 32, stride=16), :] for c in range(2)], axis=0)
            hi, lo = halves(s)
            parts.append(jnp.concatenate([hi, lo, hi], axis=0))
        out = dot(wz[...], jnp.concatenate(parts, axis=1))
        for i in range(2):
            o = out[:, 128 * i : 128 * i + 128]
            w = jnp.where(low, o[:192], o[192:])
            w = w + swap(w)
            w = jnp.where(low96, w[:96], w[96:])
            for zl in range(3):
                send[pl.ds((2 * b2 + i) * 3 + zl, 32, stride=24), :] = w[32 * zl : 32 * zl + 32]


def greet_everyone():
    f, b = lax.axis_index("fft"), lax.axis_index("band")
    barrier = pltpu.get_barrier_semaphore()

    def greet(i, c):
        pl.semaphore_signal(barrier, inc=1, device_id=(b, lax.rem(f + i, NF)), device_id_type=MESH)
        return c

    def greet_b(i, c):
        pl.semaphore_signal(barrier, inc=1, device_id=(lax.rem(b + i, NBD), f), device_id_type=MESH)
        return c

    lax.fori_loop(1, NF, greet, 0)
    lax.fori_loop(1, NBD, greet_b, 0)


def everyone_in():
    pl.semaphore_wait(pltpu.get_barrier_semaphore(), NF - 1 + NBD - 1)


class FftExchange:
    def __init__(self, src, dst, ssem, rsem, n):
        self.a = (src, dst, ssem, rsem, n)

    def copy(self, to, frm, i):
        src, dst, ssem, rsem, n = self.a
        return pltpu.make_async_remote_copy(
            src_ref=src.at[pl.ds(pl.multiple_of(to * n, 8), n), :],
            dst_ref=dst.at[pl.ds(pl.multiple_of(frm * n, 8), n), :],
            send_sem=ssem.at[i], recv_sem=rsem.at[i],
            device_id=(lax.axis_index("band"), to), device_id_type=MESH)

    def start(self):
        src, dst, ssem, rsem, n = self.a
        f = lax.axis_index("fft")
        def go(i, c):
            self.copy(lax.rem(f + i, NF), f, i).start()
            return c
        lax.fori_loop(1, NF, go, 0)
        own = pl.ds(pl.multiple_of(f * n, 8), n)
        pltpu.make_async_copy(src.at[own, :], dst.at[own, :], rsem.at[0]).start()

    def wait(self):
        src, dst, ssem, rsem, n = self.a
        f = lax.axis_index("fft")
        own = pl.ds(pl.multiple_of(f * n, 8), n)
        pltpu.make_async_copy(src.at[own, :], dst.at[own, :], rsem.at[0]).wait()
        def done(i, c):
            self.copy(lax.rem(f + i, NF), lax.rem(f + NF - i, NF), i).wait()
            return c
        lax.fori_loop(1, NF, done, 0)


class BandExchange:
    def __init__(self, src, dst, place, ssem, rsem):
        self.a = (src, dst, place, ssem, rsem)

    def copy(self, to, frm, i):
        src, dst, place, ssem, rsem = self.a
        return pltpu.make_async_remote_copy(
            src_ref=src.at[to], dst_ref=place(dst, frm), send_sem=ssem.at[i], recv_sem=rsem.at[i],
            device_id=(to, lax.axis_index("fft")), device_id_type=MESH)

    def start(self):
        src, dst, place, ssem, rsem = self.a
        b = lax.axis_index("band")
        for i in range(1, NBD):
            self.copy(lax.rem(b + i, NBD), b, i).start()
        pltpu.make_async_copy(src.at[b], place(dst, b), rsem.at[0]).start()

    def wait(self):
        src, dst, place, ssem, rsem = self.a
        b = lax.axis_index("band")
        pltpu.make_async_copy(src.at[b], place(dst, b), rsem.at[0]).wait()
        for i in range(1, NBD):
            self.copy(lax.rem(b + i, NBD), lax.rem(b + NBD - i, NBD), i).wait()


def band_rows(dst, frm):
    return dst.at[:, pl.ds(pl.multiple_of(frm * 8, 8), 8), :]


def band_slot(dst, frm):
    return dst.at[frm]


def plane_maps(scols, pot, oh_l, oh_r, inv, pick, potp):
    low1 = low_lanes((1, 128))
    rows32 = lax.broadcasted_iota(jnp.int32, (32, 128), 0)
    rows128 = lax.broadcasted_iota(jnp.int32, (128, 128), 0)
    glo = lax.broadcasted_iota(jnp.int32, (32, 128), 1).astype(F32)
    for k in range(16):
        col = jnp.where(low1, swap(scols[2 * k : 2 * k + 1, :]), scols[2 * k + 1 : 2 * k + 2, :])
        live = col >= 0
        colp = jnp.maximum(col, 0)
        xc = div96(colp)
        xi = signed(xc) + CUT
        yi = signed(colp - xc * L) + CUT
        pair = jnp.where(live, xi >> 1, -1)
        lane = jnp.where(live, (xi & 1) * 64 + yi, -1)
        pick[k : k + 1, :] = pair
        pick[16 + k : 17 + k, :] = jnp.maximum(lane, 0)
        at = pl.ds(128 * k, 128)
        hit = jnp.broadcast_to(pair, (32, 128)) == rows32
        oh_l[0:32, at] = jnp.where(hit, float(k + 1), 0.0).astype(BF16)
        oh_l[32:64, at] = jnp.where(hit, glo, 0.0).astype(BF16)
        oh_r[:, at] = jnp.where(jnp.broadcast_to(lane, (128, 128)) == rows128, 1.0, 0.0).astype(BF16)
    inv[...] = dot_nt(oh_l[...], oh_r[...]).astype(jnp.int32)
    potp[...] = jnp.zeros((3, L, 128), F32)
    potp[:, :, 0:L] = pot[...]


def planes(recv, wy, wxa, wxb, vx, vy, send, q, inv, pick, pm, tt, potp, gg, gt):
    low = low_lanes((24, 128))
    for k in range(16):
        r0, r1 = recv[48 * k : 48 * k + 24, :], recv[48 * k + 24 : 48 * k + 48, :]
        q[k, 0:24, :] = jnp.where(low, r0, swap(r1))
        q[k, 24:48, :] = jnp.where(low, swap(r0), r1)

    def place(t, carry):
        hi = jnp.broadcast_to(inv[pl.ds(t, 1), :], (48, 128))
        lo = jnp.broadcast_to(inv[pl.ds(t + 32, 1), :], (48, 128))
        acc = jnp.zeros((48, 128), F32)
        for k in range(16):
            acc = jnp.where(hi == k + 1, lanes_of(q[k], lo), acc)
        re, im = acc[:24], acc[24:]
        base = pl.multiple_of(t * 48, 16)
        pm[pl.ds(base, 24), :] = jnp.where(low, re, swap(im))
        pm[pl.ds(base + 24, 24), :] = jnp.where(low, swap(re), im)
        return carry

    lax.fori_loop(0, NPAIR, place, 0)

    def along_y(i, carry):
        at = pl.ds(pl.multiple_of(i * 240, 16), 240)
        hi, lo = halves(pm[at, :])
        out = dot(jnp.concatenate([hi, lo], axis=1), wy[0:256, :]) + dot(hi, wy[256:384, :])
        tt[0, at, :] = out[:, 0:128]
        tt[1, at, :] = out[:, 128:256]
        return carry

    lax.fori_loop(0, 5, along_y, 0)
    tt[:, 1200:1344, :] = jnp.zeros((2, 144, 128), F32)

    def along_x(i, carry):
        his, los = [], []
        for j in range(2):
            s = jnp.concatenate([tt[c, pl.ds(2 * i + j, 56, stride=24), :] for c in range(2)], axis=0)
            hi, lo = halves(s)
            his.append(hi)
            los.append(lo)
        hi = jnp.concatenate(his, axis=1)
        lo = jnp.concatenate(los, axis=1)
        u = dot(wxa[...], jnp.concatenate([hi, lo], axis=0)) + dot(wxb[...], hi)
        pv = jnp.concatenate([potp[lax.rem(2 * i + j, 3)] for j in range(2)], axis=1)
        u = u * jnp.concatenate([pv, pv], axis=0)
        hi, lo = halves(u)
        a = dot(vx[...], hi)
        t = a[0:112] + a[112:224] + dot(vx[0:112, :], lo)
        row = jnp.concatenate(
            [jnp.concatenate([t[0:56, 128 * j : 128 * j + 128], t[56:112, 128 * j : 128 * j + 128]], axis=1) for j in range(2)],
            axis=0)
        hi, lo = halves(row)
        a = dot(hi, vy[...])
        g = a[:, 0:128] + a[:, 128:256] + dot(lo, vy[:, 0:128])
        for j in range(2):
            gg[pl.ds(2 * i + j, 56, stride=24), :] = g[56 * j : 56 * j + 56]
        return carry

    lax.fori_loop(0, 12, along_x, 0)

    def pair_up(t, carry):
        base = pl.multiple_of(t * 48, 16)
        g0, g1 = gg[pl.ds(base, 24), :], gg[pl.ds(base + 24, 24), :]
        gt[t, 0:24, :] = jnp.where(low, g0, swap(g1))
        gt[t, 24:48, :] = jnp.where(low, swap(g0), g1)
        return carry

    lax.fori_loop(0, NPAIR, pair_up, 0)

    def collect(k, carry):
        hi = jnp.broadcast_to(pick[pl.ds(k, 1), :], (48, 128))
        lo = jnp.broadcast_to(pick[pl.ds(k + 16, 1), :], (48, 128))
        acc = jnp.zeros((48, 128), F32)
        for t in range(NPAIR):
            acc = jnp.where(hi == t, lanes_of(gt[t], lo), acc)
        re, im = acc[:24], acc[24:]
        base = pl.multiple_of(k * 48, 16)
        send[pl.ds(base, 24), :] = jnp.where(low, re, swap(im))
        send[pl.ds(base + 24, 24), :] = jnp.where(low, swap(re), im)
        return carry

    lax.fori_loop(0, 16, collect, 0)


def row_side(brecv, qs):
    zero = jnp.zeros((8, 768), F32)
    for d in range(NBD):
        for j in range(3):
            g8 = 3 * d + j
            ty, r0 = g8 // 8, (g8 % 8) * 8
            re, im = brecv[2 * ty, r0 : r0 + 8, :], brecv[2 * ty + 1, r0 : r0 + 8, :]
            o = 64 * d + 8 * j
            qs[o : o + 8, 0:384] = re
            qs[o : o + 8, 384:768] = im
            qs[o + 32 : o + 40, 0:384] = -im
            qs[o + 32 : o + 40, 384:768] = re
        qs[64 * d + 24 : 64 * d + 32, :] = zero
        qs[64 * d + 56 : 64 * d + 64, :] = zero


def early_gram(brecv, qs, flat, ks, esend):
    for m in range(2):
        for ty in range(3):
            at = 64 * ty
            if m == 1 and ty == 1:
                flat[at : at + 64, :] = jnp.zeros((64, 768), F32)
                continue
            src = 2 * ty if m == 0 else (6 if ty == 0 else 8)
            flat[at : at + 64, 0:384] = brecv[src]
            flat[at : at + 64, 384:768] = brecv[src + 1]
        ks[256 * m : 256 * m + 256, :] = jnp.zeros((256, 768), F32)
        for f in range(NF):
            ks[256 * m + 8 * f : 256 * m + 8 * f + 6, :] = flat[6 * f : 6 * f + 6, :]
    khi, klo = halves(ks[...])
    low = low_lanes((256, 128))
    for n in range(2):
        qhi, qlo = halves(qs[256 * n : 256 * n + 256, :])
        g = dot_nt(khi, qhi) + dot_nt(klo, qhi) + dot_nt(khi, qlo)
        for j in range(2):
            c, h = g[0:256, 128 * j : 128 * j + 128], g[256:512, 128 * j : 128 * j + 128]
            esend[4 * n + 2 * j] = jnp.where(low, c, swap(h))
            esend[4 * n + 2 * j + 1] = jnp.where(low, swap(c), h)

def term_kernel(recv, res, gm, scols, vza, vzb, hres, hsend, z, zt):
    for b2 in range(4):
        his, los = [], []
        for b in (2 * b2, 2 * b2 + 1):
            s = jnp.concatenate([recv[pl.ds(3 * b + zl, 32, stride=24), :] for zl in range(3)], axis=0)
            hi, lo = halves(s)
            his.append(hi)
            los.append(lo)
        hi = jnp.concatenate(his, axis=1)
        lo = jnp.concatenate(los, axis=1)
        out = dot(vza[...], jnp.concatenate([hi, lo], axis=0)) + dot(vzb[...], hi)
        low = low_lanes((64, 128))
        for i in range(2):
            o = out[:, 128 * i : 128 * i + 128]
            other = swap(o[64:128])
            z[pl.ds(2 * b2 + i, 64, stride=8), :] = o[0:64] + jnp.where(low, other, -other)
    low = low_lanes((8, 128))
    for t in range(NPAIR):
        z0, z1 = z[16 * t : 16 * t + 8, :], z[16 * t + 8 : 16 * t + 16, :]
        zt[t, 0:8, :] = jnp.where(low, z0, swap(z1))
        zt[t, 8:16, :] = jnp.where(low, swap(z0), z1)
    me = lax.axis_index("fft")
    cols = jnp.broadcast_to(scols[pl.ds(me, 1), :], (8, 128))
    for k in range(GT):
        at = pl.ds(128 * k, 128)
        live, kin, pair, lane = slot_facts(jnp.broadcast_to(gm[:, at], (8, 128)), cols)
        hi = jnp.concatenate([pair, pair], axis=0)
        lo = jnp.concatenate([lane, lane], axis=0)
        acc = jnp.zeros((16, 128), F32)
        for t in range(NPAIR):
            acc = jnp.where(hi == t, lanes_of(zt[t], lo), acc)
        for c in range(2):
            v = kin * res[8 * c : 8 * c + 8, at] + acc[8 * c : 8 * c + 8] * (1.0 / float(L**3))
            v = jnp.where(live, v, 0.0)
            hres[c, :, at] = v
            hsend[k // 3, c, :, (k % 3) * 128 : (k % 3) * 128 + 128] = v


F0, F1 = 10, 22


def late_gram(hrecv, qs, flat, ks, lsend):
    ks[...] = jnp.zeros((96, 768), F32)
    flat[0:64, 0:384] = hrecv[0]
    flat[0:64, 384:768] = hrecv[1]
    for f in range(F0, F1):
        k0, k1 = max(6 * f, 64), min(6 * f + 6, 128)
        o = 8 * (f - F0) + k0 - 6 * f
        ks[o : o + k1 - k0, :] = flat[k0 - 64 : k1 - 64, :]
    khi, klo = halves(ks[...])
    low = low_lanes((48, 128))
    for n in range(2):
        qhi, qlo = halves(qs[256 * n : 256 * n + 256, :])
        g = dot_nt(khi, qhi) + dot_nt(klo, qhi) + dot_nt(khi, qlo)
        for j in range(2):
            a, b = g[0:48, 128 * j : 128 * j + 128], g[48:96, 128 * j : 128 * j + 128]
            lsend[4 * n + 2 * j] = jnp.where(low, a, swap(b))
            lsend[4 * n + 2 * j + 1] = jnp.where(low, swap(a), b)


def step_kernel(ev, cur_h, hcur_h, prev_h, hprev_h, gm_h, scols_h, pot_h, wz_h, wy_h, wxa_h, wxb_h, vx_h, vy_h,
                vza_h, vzb_h, hres_h, out,
                cur, hcur, prev, hprev, gm, scols, pot, wz, wy, wxa, wxb, vx, vy, vza, vzb, hres,
                res, send, bsend, rt, zinv, zoh_l, zoh_r, y,
                recv, brecv, oh_l, oh_r, inv, pick, potp, q, pm, tt, gg, gt, send2, recv2,
                qs, flat, ks, esend, erecv, z, zt, hsend, hrecv, lks, lsend, lrecv, fsend, frecv,
                s1, r1, s2, r2, s3, r3, s4, r4, s5, r5, s6, r6, s7, r7, load):
    pairs = [(gm_h, gm), (scols_h, scols), (cur_h, cur), (hcur_h, hcur), (prev_h, prev), (hprev_h, hprev), (wz_h, wz),
             (pot_h, pot), (wy_h, wy), (wxa_h, wxa), (wxb_h, wxb), (vx_h, vx), (vy_h, vy), (vza_h, vza), (vzb_h, vzb)]
    loads = [pltpu.make_async_copy(a, b, load.at[i]) for i, (a, b) in enumerate(pairs)]
    for copy in loads:
        copy.start()
    greet_everyone()
    for copy in loads[:7]:
        copy.wait()
    sticks_kernel(ev, cur, hcur, prev, hprev, gm, scols, wz, res, send, bsend, rt, zinv, zoh_l, zoh_r, y)
    everyone_in()
    x1 = FftExchange(send, recv, s1, r1, 24)
    x2 = BandExchange(bsend, brecv, band_rows, s2, r2)
    x3 = FftExchange(send2, recv2, s3, r3, 24)
    x4 = BandExchange(esend, erecv, band_slot, s4, r4)
    x5 = BandExchange(hsend, hrecv, band_rows, s5, r5)
    x6 = BandExchange(lsend, lrecv, band_slot, s6, r6)
    x7 = FftExchange(fsend, frecv, s7, r7, 8)
    x1.start()
    x2.start()
    for copy in loads[7:]:
        copy.wait()
    plane_maps(scols, pot, oh_l, oh_r, inv, pick, potp)
    x1.wait()
    planes(recv, wy, wxa, wxb, vx, vy, send2, q, inv, pick, pm, tt, potp, gg, gt)
    x3.start()
    x2.wait()
    row_side(brecv, qs)
    early_gram(brecv, qs, flat, ks, esend)
    x4.start()
    x3.wait()
    term_kernel(recv2, res, gm, scols, vza, vzb, hres, hsend, z, zt)
    x5.start()
    store = pltpu.make_async_copy(hres, hres_h, load.at[15])
    store.start()
    x4.wait()
    total = erecv[0]
    for d in range(1, NBD):
        total = total + erecv[d]
    fsend[...] = total
    x5.wait()
    late_gram(hrecv, qs, flat, lks, lsend)
    x6.start()
    x6.wait()
    low = low_lanes((48, 128))
    total = lrecv[0]
    for d in range(1, NBD):
        total = total + lrecv[d]
    fsend[8 * F0 : 8 * F0 + 48, :] = fsend[8 * F0 : 8 * F0 + 48, :] + jnp.where(low, 0.0, swap(total))
    fsend[8 * F0 + 48 : 8 * F0 + 96, :] = fsend[8 * F0 + 48 : 8 * F0 + 96, :] + jnp.where(low, 0.0, total)
    x7.start()
    x7.wait()
    total = frecv[0:8, :]
    for d in range(1, NF):
        total = total + frecv[8 * d : 8 * d + 8, :]
    out[...] = total * (8.0 / float(L**3))
    store.wait()


def sds(*shape):
    return jax.ShapeDtypeStruct(shape, F32)


DMA = pltpu.SemaphoreType.DMA
BIG = 64 * 1024 * 1024


def local(current, h_current, previous, h_previous, eigen_values, potential, stick_cols, g_map):
    w = tables()
    gm = g_map.reshape(1, 3072)
    sc = stick_cols.reshape(NF, 128)
    vm = lambda *shape: pltpu.VMEM(shape, F32)
    v16 = lambda *shape: pltpu.VMEM(shape, BF16)
    vi = lambda *shape: pltpu.VMEM(shape, jnp.int32)
    sems = []
    for n in (NF, NBD, NF, NBD, NBD, NBD, NF):
        sems += [DMA((n,)), DMA((n,))]
    hres, tile = pl.pallas_call(
        step_kernel, out_shape=(sds(2, 8, 3072), sds(8, 128)), in_specs=[SM] + [HB] * 15, out_specs=(HB, VM),
        scratch_shapes=[
            vm(2, 8, 3072), vm(2, 8, 3072), vm(2, 8, 3072), vm(2, 8, 3072), vi(1, 3072), vi(NF, 128), vm(3, L, L),
            v16(384, 192), v16(384, 256), v16(192, 224), v16(192, 112), v16(224, 192), v16(256, 256), v16(128, 192),
            v16(128, 96), vm(2, 8, 3072),
            vm(16, 3072), vm(768, 128), vm(8, 10, 8, 384), vm(24, 16, 128), vi(64, 128), v16(64, 3072),
            v16(128, 3072), vm(512, 128),
            vm(768, 128), vm(10, 64, 384), v16(64, 2048), v16(128, 2048), vi(64, 128), vi(32, 128), vm(3, L, 128),
            vm(16, 48, 128), vm(1200, 128), vm(2, 1344, 128), vm(1344, 128), vm(NPAIR, 48, 128), vm(768, 128),
            vm(768, 128),
            vm(512, 768), vm(192, 768), vm(512, 768), vm(8, 256, 128), vm(8, 256, 128), vm(512, 128),
            vm(NPAIR, 16, 128), vm(8, 2, 8, 384), vm(2, 64, 384), vm(96, 768), vm(8, 48, 128), vm(8, 48, 128),
            vm(256, 128), vm(256, 128)] + sems + [DMA((16,))],
        compiler_params=pltpu.CompilerParams(collective_id=0, has_side_effects=True, vmem_limit_bytes=BIG), name="step",
    )(eigen_values, current, h_current, previous, h_previous, gm, sc, potential,
      w["wz"], w["wy"], w["wxa"], w["wxb"], w["vx"], w["vy"], w["vza"], w["vzb"])
    mats = jnp.transpose(tile[0:6].reshape(6, 4, 32)[:, :, 0:24], (1, 2, 0))
    return hres, mats[0:2], mats[2:4]


def solution(mesh):
    bf = P(None, "band", "fft")
    in_specs = (bf, bf, bf, bf, P("band"), P("fft", None, None), P(), P("fft"))
    return jax.shard_map(local, mesh=mesh, in_specs=in_specs, out_specs=(bf, bf, bf), check_vma=False)
```

```python
import math

import jax
import jax.numpy as jnp
import ml_dtypes
import numpy as np
from jax import lax
from jax.experimental import pallas as pl
from jax.experimental.pallas import tpu as pltpu
from jax.sharding import PartitionSpec as P

L = 96
CUT = 24
F32 = jnp.float32
BF16 = jnp.bfloat16
NF = 32
NBD = 8
GT = 24
NT = 13
MESH = pl.DeviceIdType.MESH
VM = pl.BlockSpec(memory_space=pltpu.VMEM)
HB = pl.BlockSpec(memory_space=pltpu.HBM)
SM = pl.BlockSpec(memory_space=pltpu.SMEM)


def split_np(table):
    high = table.astype(ml_dtypes.bfloat16)
    low = (table - high.astype(np.float64)).astype(ml_dtypes.bfloat16)
    return high, low


def tables():
    zout = (np.arange(NF)[None, :] * 3 + np.arange(3)[:, None]).reshape(-1)
    wz = np.zeros((2, 2, L, 2, 32))
    for par in range(2):
        zi = 2 * np.arange(32) + par
        ok = zi <= 2 * CUT
        ang = 2 * math.pi / L * ((zout[:, None] * (zi - CUT)[None, :]) % L)
        c, s = np.cos(ang) * ok, np.sin(ang) * ok
        wz[par, 0, :, 0], wz[par, 0, :, 1] = c, -s
        wz[par, 1, :, 0], wz[par, 1, :, 1] = s, c
    zh, zl = split_np(wz.reshape(384, 64))
    wz = np.concatenate([zh, zh, zl], axis=1)
    n = np.arange(L)
    k = np.arange(49) - CUT
    ang = 2 * math.pi / L * ((k[:, None] * n[None, :]) % L)
    c, s = np.cos(ang), np.sin(ang)
    wy = np.zeros((2, 64, 2, 128))
    wy[0, :49, 0, :L], wy[0, :49, 1, :L] = c, s
    wy[1, :49, 0, :L], wy[1, :49, 1, :L] = -s, c
    yh, yl = split_np(wy.reshape(128, 256))
    wy = np.concatenate([yh, yh, yl], axis=0)
    wx = np.zeros((2, L, 2, 56))
    wx[0, :, 0, :49], wx[0, :, 1, :49] = c.T, -s.T
    wx[1, :, 0, :49], wx[1, :, 1, :49] = s.T, c.T
    xh, xl = split_np(wx.reshape(192, 112))
    wx = np.concatenate([xh, xh, xl], axis=1)
    vx = np.zeros((2, 56, 2, L))
    vx[0, :49, 0], vx[0, :49, 1] = c, s
    vx[1, :49, 0], vx[1, :49, 1] = -s, c
    vh, vl = split_np(vx.reshape(112, 192))
    vx = np.concatenate([vh, vh, vl], axis=1)
    vy = np.zeros((2, 128, 2, 64))
    vy[0, :L, 0, :49], vy[0, :L, 1, :49] = c.T, -s.T
    vy[1, :L, 0, :49], vy[1, :L, 1, :49] = s.T, c.T
    vyh, vyl = split_np(vy.reshape(256, 128))
    vy = np.concatenate([vyh, vyl], axis=1)
    vz = np.zeros((2, 64, L))
    ang = 2 * math.pi / L * ((k[:, None] * zout[None, :]) % L)
    vz[0, :49], vz[1, :49] = np.cos(ang), np.sin(ang)
    zbh, zbl = split_np(vz.reshape(128, L))
    vz = np.concatenate([zbh, zbh, zbl], axis=1)
    return dict(wz=wz, wy=wy, wx=wx, vx=vx, vy=vy, vz=vz)


def dot(a, b):
    return jnp.dot(a, b, preferred_element_type=F32)


def dot_nt(a, b):
    return lax.dot_general(a, b, (((1,), (1,)), ((), ())), preferred_element_type=F32)


def halves(x):
    hi = x.astype(BF16)
    return hi, (x - hi.astype(F32)).astype(BF16)


def low_lanes(shape):
    return lax.broadcasted_iota(jnp.int32, shape, len(shape) - 1) < 64


def swap(x):
    return pltpu.roll(x, 64, 1)


def div96(v):
    return (v * 43691) >> 22


def signed(v):
    return jnp.where(v >= L // 2, v - L, v)


def lanes_of(x, index):
    return jnp.take_along_axis(x, index, axis=1, mode="promise_in_bounds")


def slot_facts(m, cols):
    live = m >= 0
    ms = jnp.maximum(m, 0)
    slot = div96(ms)
    z = signed(ms - slot * L)
    col = jnp.where(live, lanes_of(cols, slot), 0)
    xc = div96(col)
    x = signed(xc)
    y = signed(col - xc * L)
    norm = x * x + y * y + z * z
    kin = jnp.where(live, 64.0 * norm.astype(F32) / float(L * L), 0.0)
    zi = z + CUT
    four = jnp.where(live, zi >> 2, -1)
    lane = jnp.where(live, (zi & 3) * 64 + slot - 64, -1)
    return live, kin, four, lane


def one_hot_rows(key, rows):
    return jnp.where(jnp.broadcast_to(key, (256, 128)) == rows, 1.0, 0.0).astype(BF16)


def four_masks(four):
    wide = jnp.broadcast_to(four, (16, 128))
    return [jnp.where(wide == t, 1.0, 0.0).astype(BF16) for t in range(NT)]


def residual(ev, cur, hcur, gm, scols, res, lhs, hit, kinr, fourr, liver):
    me = lax.axis_index("fft")
    cols = jnp.broadcast_to(scols[pl.ds(me, 1), :], (8, 128))
    row = lax.broadcasted_iota(jnp.int32, (8, 128), 0)
    evc = jnp.zeros((8, 128), F32)
    for b in range(8):
        evc = jnp.where(row == b, ev[b], evc)
    rows = lax.broadcasted_iota(jnp.int32, (256, 128), 0)

    for k in range(GT):
        at = pl.ds(128 * k, 128)
        live, kin, four, lane = slot_facts(jnp.broadcast_to(gm[:, at], (8, 128)), cols)
        kinr[:, at] = kin
        fourr[:, at] = four
        liver[:, at] = live.astype(F32)
        den = 1.0 + kin
        r = jnp.concatenate(
            [jnp.where(live, (hcur[c, :, at] - evc * cur[c, :, at]) / den, 0.0) for c in range(2)], axis=0)
        res[:, at] = r
        hi, lo = halves(r)
        hit[:, at] = one_hot_rows(lane[:1], rows)
        for t, m in enumerate(four_masks(four[:1])):
            lhs[32 * t : 32 * t + 16, at] = hi * m
            lhs[32 * t + 16 : 32 * t + 32, at] = lo * m


def sticks(lhs, hit, wz, send, y):
    out = dot_nt(lhs[...], hit[...])
    y[416:512, :] = jnp.zeros((96, 128), F32)
    for t in range(NT):
        o = out[32 * t : 32 * t + 16] + out[32 * t + 16 : 32 * t + 32]
        for h in range(2):
            y[32 * t + 16 * h : 32 * t + 16 * h + 16, :] = o[:, 128 * h : 128 * h + 128]
    low = low_lanes((192, 128))
    low96 = low_lanes((96, 128))
    parts = []
    for b in range(8):
        x = jnp.concatenate([y[pl.ds(c * 8 + b, 32, stride=16), :] for c in range(2)], axis=0)
        hi, lo = halves(x)
        parts.append(jnp.concatenate([hi, lo, hi], axis=0))
    out = dot(wz[...], jnp.concatenate(parts, axis=1))
    for b in range(8):
        o = out[:, 128 * b : 128 * b + 128]
        w = jnp.where(low, o[:192], o[192:])
        w = w + swap(w)
        w = jnp.where(low96, w[:96], w[96:])
        for zl in range(3):
            send[pl.ds(256 * zl + b, 32, stride=8), :] = w[32 * zl : 32 * zl + 32]


def basis_rows(cur, hcur, prev, hprev, res, liver, bsend):
    def tile(d, carry):
        at = pl.ds(pl.multiple_of(384 * d, 128), 384)
        live = liver[:, at] > 0.0
        for c in range(2):
            bsend[d, c] = jnp.where(live, cur[c, :, at], 0.0)
            bsend[d, 2 + c] = res[8 * c : 8 * c + 8, at]
            bsend[d, 4 + c] = jnp.where(live, prev[c, :, at], 0.0)
            bsend[d, 6 + c] = jnp.where(live, hcur[c, :, at], 0.0)
            bsend[d, 8 + c] = jnp.where(live, hprev[c, :, at], 0.0)
        return carry

    lax.fori_loop(0, NBD, tile, 0)


def greet_everyone():
    f, b = lax.axis_index("fft"), lax.axis_index("band")
    barrier = pltpu.get_barrier_semaphore()

    def greet(i, c):
        pl.semaphore_signal(barrier, inc=1, device_id=(b, lax.rem(f + i, NF)), device_id_type=MESH)
        return c

    def greet_b(i, c):
        pl.semaphore_signal(barrier, inc=1, device_id=(lax.rem(b + i, NBD), f), device_id_type=MESH)
        return c

    lax.fori_loop(1, NF, greet, 0)
    lax.fori_loop(1, NBD, greet_b, 0)


def everyone_in():
    pl.semaphore_wait(pltpu.get_barrier_semaphore(), NF - 1 + NBD - 1)


FAR_FIRST = sorted(
    [(dx, dz) for dx in range(4) for dz in range(8) if dx or dz], key=lambda o: -min(o[0], 4 - o[0]) - min(o[1], 8 - o[1]))


def whole(ref, sem):
    pltpu.make_async_copy(ref, ref, sem).wait()


class FftExchange:
    def __init__(self, src, dst, ssem, rsem):
        self.a = (src, dst, ssem, rsem)

    def start(self, g=0):
        src, dst, ssem, rsem = self.a
        f, b = lax.axis_index("fft"), lax.axis_index("band")
        to_me = dst.at[pl.ds(pl.multiple_of(256 * g + 8 * f, 8), 8), :]

        for dx, dz in FAR_FIRST:
            to = lax.rem(f // 8 + dx, 4) * 8 + lax.rem(f + dz, 8)
            pltpu.make_async_remote_copy(
                src_ref=src.at[pl.ds(pl.multiple_of(256 * g + 8 * to, 8), 8), :], dst_ref=to_me,
                send_sem=ssem.at[g], recv_sem=rsem.at[g], device_id=(b, to), device_id_type=MESH).start()
        own = src.at[pl.ds(pl.multiple_of(256 * g + 8 * f, 8), 8), :]
        pltpu.make_async_copy(own, to_me, rsem.at[g]).start()

    def wait(self, g=0):
        src, dst, ssem, rsem = self.a
        whole(dst.at[pl.ds(pl.multiple_of(256 * g, 256), 256), :], rsem.at[g])

    def sent(self, g=0):
        src, dst, ssem, rsem = self.a
        whole(src.at[pl.ds(256 * g, 248), :], ssem.at[g])


class BandExchange:
    def __init__(self, src, dst, place, ssem, rsem):
        self.a = (src, dst, place, ssem, rsem)

    def start(self):
        src, dst, place, ssem, rsem = self.a
        f, b = lax.axis_index("fft"), lax.axis_index("band")
        for i in range(1, NBD):
            to = lax.rem(b + i, NBD)
            pltpu.make_async_remote_copy(
                src_ref=src.at[to], dst_ref=place(dst, b), send_sem=ssem, recv_sem=rsem,
                device_id=(to, f), device_id_type=MESH).start()
        pltpu.make_async_copy(src.at[b], place(dst, b), rsem).start()

    def wait(self):
        src, dst, place, ssem, rsem = self.a
        whole(dst, rsem)

    def sent(self):
        src, dst, place, ssem, rsem = self.a
        whole(src.at[pl.ds(0, NBD - 1)], ssem)


class BandSum:
    def __init__(self, src, got, mid, dst, sems):
        self.a = (src, got, mid, dst, sems)
        b = lax.axis_index("band")
        self.y, self.c = b // 2, lax.rem(b, 2)

    def first(self):
        src, got, mid, dst, sems = self.a
        pltpu.make_async_remote_copy(
            src_ref=src.at[1 - self.c], dst_ref=got, send_sem=sems.at[0], recv_sem=sems.at[1],
            device_id=(2 * self.y + 1 - self.c, lax.axis_index("fft")), device_id_type=MESH).start()

    def second(self):
        src, got, mid, dst, sems = self.a
        whole(got, sems.at[1])
        mid[...] = src[self.c] + got[...]
        for i in (2, 1, 3):
            to = lax.rem(self.y + i, 4)
            pltpu.make_async_remote_copy(
                src_ref=mid.at[to], dst_ref=dst.at[self.y], send_sem=sems.at[2], recv_sem=sems.at[3],
                device_id=(2 * to + self.c, lax.axis_index("fft")), device_id_type=MESH).start()
        pltpu.make_async_copy(mid.at[self.y], dst.at[self.y], sems.at[3]).start()

    def total(self):
        src, got, mid, dst, sems = self.a
        whole(dst, sems.at[3])
        return (dst[0] + dst[1]) + (dst[2] + dst[3])

    def sent(self):
        src, got, mid, dst, sems = self.a
        whole(got, sems.at[0])
        whole(mid.at[pl.ds(0, 3)], sems.at[2])


def band_rows(dst, frm):
    return dst.at[:, pl.ds(pl.multiple_of(frm * 8, 8), 8), :]


def plane_maps(scols, pot, hit, mask, fourr, potp):
    low1 = low_lanes((1, 128))
    rows = lax.broadcasted_iota(jnp.int32, (256, 128), 0)
    for k in range(16):
        col = jnp.where(low1, swap(scols[2 * k : 2 * k + 1, :]), scols[2 * k + 1 : 2 * k + 2, :])
        live = col >= 0
        colp = jnp.maximum(col, 0)
        xc = div96(colp)
        xi = signed(xc) + CUT
        yi = signed(colp - xc * L) + CUT
        four = jnp.where(live, xi >> 2, -1)
        at = pl.ds(128 * k, 128)
        fourr[:, at] = jnp.broadcast_to(four, (8, 128))
        hit[:, at] = one_hot_rows(jnp.where(live, (xi & 3) * 64 + yi, -1), rows)
        for t, m in enumerate(four_masks(four)):
            mask[16 * t : 16 * t + 16, at] = m
    potp[...] = jnp.zeros((3, L, 128), F32)
    potp[:, :, 0:L] = pot[...]


def place(g, recv, hit, mask, lhs, pm):
    low = low_lanes((8, 128))
    for k in range(16):
        at = pl.ds(128 * k, 128)
        base = pl.multiple_of(256 * g + 16 * k, 16)
        r0, r1 = recv[pl.ds(base, 8), :], recv[pl.ds(base + 8, 8), :]
        hi, lo = halves(jnp.concatenate([jnp.where(low, r0, swap(r1)), jnp.where(low, swap(r0), r1)], axis=0))
        for t in range(NT):
            m = mask[16 * t : 16 * t + 16, at]
            lhs[32 * t : 32 * t + 16, at] = hi * m
            lhs[32 * t + 16 : 32 * t + 32, at] = lo * m
    out = dot_nt(lhs[...], hit[...])
    for t in range(NT):
        o = out[32 * t : 32 * t + 16] + out[32 * t + 16 : 32 * t + 32]
        for h in range(2):
            re, im = o[:8, 128 * h : 128 * h + 128], o[8:, 128 * h : 128 * h + 128]
            base = 32 * t + 16 * h
            pm[base : base + 8, :] = jnp.where(low, re, swap(im))
            pm[base + 8 : base + 16, :] = jnp.where(low, swap(re), im)


def along_y(pm, wy, tt):
    hi, lo = halves(pm[0:416, :])
    out = dot(jnp.concatenate([hi, lo], axis=1), wy[0:256, :]) + dot(hi, wy[256:384, :])
    tt[0, 0:416, :] = out[:, 0:128]
    tt[1, 0:416, :] = out[:, 128:256]
    tt[:, 416:448, :] = jnp.zeros((2, 32, 128), F32)


def along_x(g, tt, potp, wx, vx, vy, gg):
    pv = potp[g]
    pv = jnp.concatenate([pv] * 8, axis=1)
    pv = jnp.concatenate([pv, pv], axis=0)
    his, los = [], []
    for b in range(8):
        hi, lo = halves(jnp.concatenate([tt[c, pl.ds(b, 56, stride=8), :] for c in range(2)], axis=0))
        his.append(hi)
        los.append(lo)
    hi = jnp.concatenate(his, axis=1)
    u = dot(wx[...], jnp.concatenate([hi, jnp.concatenate(los, axis=1), hi], axis=0))
    hi, lo = halves(u * pv)
    t = dot(vx[...], jnp.concatenate([hi, lo, hi], axis=0))
    hi, lo = halves(jnp.concatenate(
        [jnp.concatenate([t[56 * c : 56 * c + 56, 128 * b : 128 * b + 128] for c in range(2)], axis=1) for b in range(8)],
        axis=0))
    a = dot(hi, vy[...])
    q = a[:, 0:128] + a[:, 128:256] + dot(lo, vy[:, 0:128])
    for b in range(8):
        gg[pl.ds(b, 56, stride=8), :] = q[56 * b : 56 * b + 56]


def fours(src, low):
    blocks = []
    for t in range(NT):
        cols = []
        for h in range(2):
            base = 32 * t + 16 * h
            g0, g1 = src[base : base + 8, :], src[base + 8 : base + 16, :]
            cols.append(jnp.concatenate([jnp.where(low, g0, swap(g1)), jnp.where(low, swap(g0), g1)], axis=0))
        blocks.append(jnp.concatenate(cols, axis=1))
    hi, lo = halves(jnp.concatenate(blocks, axis=0))
    return jnp.concatenate([hi, lo], axis=1)


def pick(lhs, hit, fourr, n, width):
    at = pl.ds(n * width, width)
    d = hit[:, at]
    out = dot(lhs, jnp.concatenate([d, d], axis=0))
    f = fourr[:, at]
    f = jnp.concatenate([f, f], axis=0)
    acc = jnp.zeros((16, width), F32)
    for t in range(NT):
        acc = jnp.where(f == t, out[16 * t : 16 * t + 16], acc)
    return acc


def collect(g, gg, hit, fourr, gl, send):
    low = low_lanes((8, 128))
    gl[...] = fours(gg, low)
    for n in range(8):
        acc = pick(gl[...], hit, fourr, n, 256)
        for k in range(2):
            re, im = acc[0:8, 128 * k : 128 * k + 128], acc[8:16, 128 * k : 128 * k + 128]
            base = pl.multiple_of(256 * g + 32 * n + 16 * k, 16)
            send[pl.ds(base, 8), :] = jnp.where(low, re, swap(im))
            send[pl.ds(base + 8, 8), :] = jnp.where(low, swap(re), im)


def row_side(brecv, qs):
    zero = jnp.zeros((8, 768), F32)
    for d in range(NBD):
        for j in range(3):
            g8 = 3 * d + j
            ty, r0 = g8 // 8, (g8 % 8) * 8
            re, im = brecv[2 * ty, r0 : r0 + 8, :], brecv[2 * ty + 1, r0 : r0 + 8, :]
            o = 64 * d + 8 * j
            qs[o : o + 8, 0:384] = re
            qs[o : o + 8, 384:768] = im
            qs[o + 32 : o + 40, 0:384] = -im
            qs[o + 32 : o + 40, 384:768] = re
        qs[64 * d + 24 : 64 * d + 32, :] = zero
        qs[64 * d + 56 : 64 * d + 64, :] = zero


def early_gram(brecv, qs, flat, ks, esend):
    for m in range(2):
        for ty in range(3):
            at = 64 * ty
            if m == 1 and ty == 1:
                flat[at : at + 64, :] = jnp.zeros((64, 768), F32)
                continue
            src = 2 * ty if m == 0 else (6 if ty == 0 else 8)
            flat[at : at + 64, 0:384] = brecv[src]
            flat[at : at + 64, 384:768] = brecv[src + 1]
        ks[256 * m : 256 * m + 256, :] = jnp.zeros((256, 768), F32)
        for f in range(NF):
            ks[256 * m + 8 * f : 256 * m + 8 * f + 6, :] = flat[6 * f : 6 * f + 6, :]
    khi, klo = halves(ks[...])
    low = low_lanes((256, 128))
    for n in range(2):
        qhi, qlo = halves(qs[256 * n : 256 * n + 256, :])
        g = dot_nt(khi, qhi) + dot_nt(klo, qhi) + dot_nt(khi, qlo)
        for j in range(2):
            c, h = g[0:256, 128 * j : 128 * j + 128], g[256:512, 128 * j : 128 * j + 128]
            esend[0, 2 * n + j] = jnp.where(low, c, swap(h))
            esend[1, 2 * n + j] = jnp.where(low, swap(c), h)

def term(recv, res, hit, fourr, kinr, liver, vz, hres, hsend, z, zl_):
    his, los = [], []
    for b in range(8):
        hi, lo = halves(jnp.concatenate([recv[pl.ds(256 * zl + b, 32, stride=8), :] for zl in range(3)], axis=0))
        his.append(hi)
        los.append(lo)
    hi = jnp.concatenate(his, axis=1)
    out = dot(vz[...], jnp.concatenate([hi, jnp.concatenate(los, axis=1), hi], axis=0))
    low = low_lanes((64, 128))
    for b in range(8):
        o = out[:, 128 * b : 128 * b + 128]
        other = swap(o[64:128])
        z[pl.ds(b, 64, stride=8), :] = o[0:64] + jnp.where(low, other, -other)
    zl_[...] = fours(z, low_lanes((8, 128)))
    for n in range(12):
        at = pl.ds(256 * n, 256)
        acc = pick(zl_[...], hit, fourr, n, 256)
        live = liver[:, at] > 0.0
        for c in range(2):
            v = kinr[:, at] * res[8 * c : 8 * c + 8, at] + acc[8 * c : 8 * c + 8] * (1.0 / float(L**3))
            v = jnp.where(live, v, 0.0)
            hres[c, :, at] = v
            for k in range(2):
                q = 2 * n + k
                hsend[q // 3, c, :, (q % 3) * 128 : (q % 3) * 128 + 128] = v[:, 128 * k : 128 * k + 128]


F0, F1 = 10, 22


def late_gram(hrecv, qs, flat, ks, lsend):
    ks[...] = jnp.zeros((96, 768), F32)
    flat[0:64, 0:384] = hrecv[0]
    flat[0:64, 384:768] = hrecv[1]
    for f in range(F0, F1):
        k0, k1 = max(6 * f, 64), min(6 * f + 6, 128)
        o = 8 * (f - F0) + k0 - 6 * f
        ks[o : o + k1 - k0, :] = flat[k0 - 64 : k1 - 64, :]
    khi, klo = halves(ks[...])
    low = low_lanes((48, 128))
    for n in range(2):
        qhi, qlo = halves(qs[256 * n : 256 * n + 256, :])
        g = dot_nt(khi, qhi) + dot_nt(klo, qhi) + dot_nt(khi, qlo)
        for j in range(2):
            a, b = g[0:48, 128 * j : 128 * j + 128], g[48:96, 128 * j : 128 * j + 128]
            lsend[0, 2 * n + j] = jnp.where(low, a, swap(b))
            lsend[1, 2 * n + j] = jnp.where(low, swap(a), b)


def step_kernel(ev, cur_h, hcur_h, prev_h, hprev_h, gm_h, scols_h, pot_h, wz_h, wy_h, wx_h, vx_h, vy_h,
                vz_h, hres_h, out,
                cur, hcur, prev, hprev, gm, scols, pot, wz, wy, wx, vx, vy, vz, hres,
                res, kinr, gfour, liver, ghit, glhs, y, send, bsend,
                recv, brecv, shit, smask, sfour, slhs, potp, pm, tt, gg, gl, send2, recv2,
                qs, flat, ks, esend, egot, emid, erecv, z, zl, hsend, hrecv, lks,
                lsend, lgot, lmid, lrecv, fsend, frecv, s1, r1, s3, r3, s4, s6, sems, load):
    pairs = [(gm_h, gm), (scols_h, scols), (cur_h, cur), (hcur_h, hcur), (wz_h, wz), (prev_h, prev), (hprev_h, hprev),
             (pot_h, pot), (wy_h, wy), (wx_h, wx), (vx_h, vx), (vy_h, vy), (vz_h, vz)]
    loads = [pltpu.make_async_copy(a, b, load.at[i]) for i, (a, b) in enumerate(pairs)]
    for copy in loads:
        copy.start()
    greet_everyone()
    for copy in loads[:5]:
        copy.wait()
    x1 = FftExchange(send, recv, s1, r1)
    x2 = BandExchange(bsend, brecv, band_rows, sems.at[0], sems.at[1])
    x3 = FftExchange(send2, recv2, s3, r3)
    x4 = BandSum(esend, egot, emid, erecv, s4)
    x5 = BandExchange(hsend, hrecv, band_rows, sems.at[4], sems.at[5])
    x6 = BandSum(lsend, lgot, lmid, lrecv, s6)
    x7 = FftExchange(fsend, frecv, sems.at[pl.ds(8, 1)], sems.at[pl.ds(9, 1)])
    residual(ev, cur, hcur, gm, scols, res, glhs, ghit, kinr, gfour, liver)
    sticks(glhs, ghit, wz, send, y)
    everyone_in()
    for g in range(3):
        x1.start(g)
    for copy in loads[5:]:
        copy.wait()
    basis_rows(cur, hcur, prev, hprev, res, liver, bsend)
    plane_maps(scols, pot, shit, smask, sfour, potp)

    def plane(g, carry):
        x1.wait(g)
        pl.when(g == 0)(x2.start)
        place(g, recv, shit, smask, slhs, pm)
        along_y(pm, wy, tt)
        along_x(g, tt, potp, wx, vx, vy, gg)
        collect(g, gg, shit, sfour, gl, send2)
        x3.start(g)
        return carry

    lax.fori_loop(0, 3, plane, 0)
    x2.wait()
    row_side(brecv, qs)
    early_gram(brecv, qs, flat, ks, esend)
    x4.first()
    x4.second()
    for g in range(3):
        x3.wait(g)
    term(recv2, res, ghit, gfour, kinr, liver, vz, hres, hsend, z, zl)
    x5.start()
    store = pltpu.make_async_copy(hres, hres_h, load.at[15])
    store.start()
    fsend[...] = x4.total()
    x5.wait()
    late_gram(hrecv, qs, flat, lks, lsend)
    x6.first()
    x6.second()
    low = low_lanes((48, 128))
    total = x6.total()
    fsend[8 * F0 : 8 * F0 + 48, :] = fsend[8 * F0 : 8 * F0 + 48, :] + jnp.where(low, 0.0, swap(total))
    fsend[8 * F0 + 48 : 8 * F0 + 96, :] = fsend[8 * F0 + 48 : 8 * F0 + 96, :] + jnp.where(low, 0.0, total)
    x7.start()
    x7.wait()
    total = frecv[0:8, :]
    for d in range(1, NF):
        total = total + frecv[8 * d : 8 * d + 8, :]
    out[...] = total * (8.0 / float(L**3))
    store.wait()
    for g in range(3):
        x1.sent(g)
        x3.sent(g)
    for x in (x2, x4, x5, x6, x7):
        x.sent()


def sds(*shape):
    return jax.ShapeDtypeStruct(shape, F32)


DMA = pltpu.SemaphoreType.DMA
BIG = 64 * 1024 * 1024


def local(current, h_current, previous, h_previous, eigen_values, potential, stick_cols, g_map):
    w = tables()
    gm = g_map.reshape(1, 3072)
    sc = stick_cols.reshape(NF, 128)
    vm = lambda *shape: pltpu.VMEM(shape, F32)
    v16 = lambda *shape: pltpu.VMEM(shape, BF16)
    vi = lambda *shape: pltpu.VMEM(shape, jnp.int32)
    hres, tile = pl.pallas_call(
        step_kernel, out_shape=(sds(2, 8, 3072), sds(8, 128)), in_specs=[SM] + [HB] * 13, out_specs=(HB, VM),
        scratch_shapes=[
            vm(2, 8, 3072), vm(2, 8, 3072), vm(2, 8, 3072), vm(2, 8, 3072), vi(1, 3072), vi(NF, 128), vm(3, L, L),
            v16(384, 192), v16(384, 256), v16(192, 336), v16(112, 576), v16(256, 256), v16(128, 288),
            vm(2, 8, 3072),
            vm(16, 3072), vm(8, 3072), vi(8, 3072), vm(8, 3072), v16(256, 3072), v16(416, 3072), vm(512, 128),
            vm(768, 128), vm(8, 10, 8, 384),
            vm(768, 128), vm(10, 64, 384), v16(256, 2048), v16(208, 2048), vi(8, 2048), v16(416, 2048),
            vm(3, L, 128), vm(416, 128), vm(2, 448, 128), vm(448, 128), v16(208, 512), vm(768, 128), vm(768, 128),
            vm(512, 768), vm(192, 768), vm(512, 768), vm(2, 4, 256, 128), vm(4, 256, 128), vm(4, 256, 128),
            vm(4, 256, 128), vm(512, 128),
            v16(208, 512), vm(8, 2, 8, 384), vm(2, 64, 384), vm(96, 768), vm(2, 4, 48, 128), vm(4, 48, 128), vm(4, 48, 128), vm(4, 48, 128),
            vm(256, 128), vm(256, 128), DMA((3,)), DMA((3,)), DMA((3,)), DMA((3,)), DMA((4,)), DMA((4,)), DMA((10,)), DMA((16,))],
        compiler_params=pltpu.CompilerParams(collective_id=0, has_side_effects=True, vmem_limit_bytes=BIG), name="step",
    )(eigen_values, current, h_current, previous, h_previous, gm, sc, potential,
      w["wz"], w["wy"], w["wx"], w["vx"], w["vy"], w["vz"])
    mats = jnp.transpose(tile[0:6].reshape(6, 4, 32)[:, :, 0:24], (1, 2, 0))
    return hres, mats[0:2], mats[2:4]


def solution(mesh):
    bf = P(None, "band", "fft")
    in_specs = (bf, bf, bf, bf, P("band"), P("fft", None, None), P(), P("fft"))
    return jax.shard_map(local, mesh=mesh, in_specs=in_specs, out_specs=(bf, bf, bf), check_vma=False)
```

```python
import math

import jax
import jax.numpy as jnp
import ml_dtypes
import numpy as np
from jax import lax
from jax.experimental import pallas as pl
from jax.experimental.pallas import tpu as pltpu
from jax.sharding import PartitionSpec as P

L = 96
CUT = 24
F32 = jnp.float32
BF16 = jnp.bfloat16
NF = 32
NBD = 8
GT = 24
NT = 13
MESH = pl.DeviceIdType.MESH
VM = pl.BlockSpec(memory_space=pltpu.VMEM)
HB = pl.BlockSpec(memory_space=pltpu.HBM)
SM = pl.BlockSpec(memory_space=pltpu.SMEM)


def split_np(table):
    high = table.astype(ml_dtypes.bfloat16)
    low = (table - high.astype(np.float64)).astype(ml_dtypes.bfloat16)
    return high, low


def tables():
    zout = (np.arange(NF)[None, :] * 3 + np.arange(3)[:, None]).reshape(-1)
    wz = np.zeros((2, 2, L, 2, 32))
    for par in range(2):
        zi = 2 * np.arange(32) + par
        ok = zi <= 2 * CUT
        ang = 2 * math.pi / L * ((zout[:, None] * (zi - CUT)[None, :]) % L)
        c, s = np.cos(ang) * ok, np.sin(ang) * ok
        wz[par, 0, :, 0], wz[par, 0, :, 1] = c, -s
        wz[par, 1, :, 0], wz[par, 1, :, 1] = s, c
    zh, zl = split_np(wz.reshape(384, 64))
    wz = np.concatenate([zh, zh, zl], axis=1)
    n = np.arange(L)
    k = np.arange(49) - CUT
    ang = 2 * math.pi / L * ((k[:, None] * n[None, :]) % L)
    c, s = np.cos(ang), np.sin(ang)
    wy = np.zeros((2, 64, 2, 128))
    wy[0, :49, 0, :L], wy[0, :49, 1, :L] = c, s
    wy[1, :49, 0, :L], wy[1, :49, 1, :L] = -s, c
    yh, yl = split_np(wy.reshape(128, 256))
    wy = np.concatenate([yh, yh, yl], axis=0)
    wx = np.zeros((2, L, 2, 56))
    wx[0, :, 0, :49], wx[0, :, 1, :49] = c.T, -s.T
    wx[1, :, 0, :49], wx[1, :, 1, :49] = s.T, c.T
    xh, xl = split_np(wx.reshape(192, 112))
    wx = np.concatenate([xh, xh, xl], axis=1)
    vx = np.zeros((2, 56, 2, L))
    vx[0, :49, 0], vx[0, :49, 1] = c, s
    vx[1, :49, 0], vx[1, :49, 1] = -s, c
    vh, vl = split_np(vx.reshape(112, 192))
    vx = np.concatenate([vh, vh, vl], axis=1)
    vy = np.zeros((2, 128, 2, 64))
    vy[0, :L, 0, :49], vy[0, :L, 1, :49] = c.T, -s.T
    vy[1, :L, 0, :49], vy[1, :L, 1, :49] = s.T, c.T
    vyh, vyl = split_np(vy.reshape(256, 128))
    vy = np.concatenate([vyh, vyl], axis=1)
    vz = np.zeros((2, 64, L))
    ang = 2 * math.pi / L * ((k[:, None] * zout[None, :]) % L)
    vz[0, :49], vz[1, :49] = np.cos(ang), np.sin(ang)
    zbh, zbl = split_np(vz.reshape(128, L))
    vz = np.concatenate([zbh, zbh, zbl], axis=1)
    return dict(wz=wz, wy=wy, wx=wx, vx=vx, vy=vy, vz=vz)


def dot(a, b):
    return jnp.dot(a, b, preferred_element_type=F32)


def dot_nt(a, b):
    return lax.dot_general(a, b, (((1,), (1,)), ((), ())), preferred_element_type=F32)


def halves(x):
    hi = x.astype(BF16)
    return hi, (x - hi.astype(F32)).astype(BF16)


def low_lanes(shape):
    return lax.broadcasted_iota(jnp.int32, shape, len(shape) - 1) < 64


def swap(x):
    return pltpu.roll(x, 64, 1)


def div96(v):
    return (v * 43691) >> 22


def signed(v):
    return jnp.where(v >= L // 2, v - L, v)


def lanes_of(x, index):
    return jnp.take_along_axis(x, index, axis=1, mode="promise_in_bounds")


def slot_facts(m, cols):
    live = m >= 0
    ms = jnp.maximum(m, 0)
    slot = div96(ms)
    z = signed(ms - slot * L)
    col = jnp.where(live, lanes_of(cols, slot), 0)
    xc = div96(col)
    x = signed(xc)
    y = signed(col - xc * L)
    norm = x * x + y * y + z * z
    kin = jnp.where(live, 64.0 * norm.astype(F32) / float(L * L), 0.0)
    zi = z + CUT
    four = jnp.where(live, zi >> 2, -1)
    lane = jnp.where(live, (zi & 3) * 64 + slot - 64, -1)
    return live, kin, four, lane


def one_hot_rows(key, rows):
    return jnp.where(jnp.broadcast_to(key, (256, 128)) == rows, 1.0, 0.0).astype(BF16)


def four_masks(four):
    wide = jnp.broadcast_to(four, (16, 128))
    return [jnp.where(wide == t, 1.0, 0.0).astype(BF16) for t in range(NT)]


def residual(ev, cur, hcur, gm, scols, res, lhs, hit, kinr, fourr, liver):
    me = lax.axis_index("fft")
    cols = jnp.broadcast_to(scols[pl.ds(me, 1), :], (8, 128))
    row = lax.broadcasted_iota(jnp.int32, (8, 128), 0)
    evc = jnp.zeros((8, 128), F32)
    for b in range(8):
        evc = jnp.where(row == b, ev[b], evc)
    rows = lax.broadcasted_iota(jnp.int32, (256, 128), 0)

    for k in range(GT):
        at = pl.ds(128 * k, 128)
        live, kin, four, lane = slot_facts(jnp.broadcast_to(gm[:, at], (8, 128)), cols)
        kinr[:, at] = kin
        fourr[:, at] = four
        liver[:, at] = live.astype(F32)
        den = 1.0 + kin
        r = jnp.concatenate(
            [jnp.where(live, (hcur[c, :, at] - evc * cur[c, :, at]) / den, 0.0) for c in range(2)], axis=0)
        res[:, at] = r
        hi, lo = halves(r)
        hit[:, at] = one_hot_rows(lane[:1], rows)
        for t, m in enumerate(four_masks(four[:1])):
            lhs[32 * t : 32 * t + 16, at] = hi * m
            lhs[32 * t + 16 : 32 * t + 32, at] = lo * m


def sticks(lhs, hit, wz, send, y):
    out = dot_nt(lhs[...], hit[...])
    y[416:512, :] = jnp.zeros((96, 128), F32)
    for t in range(NT):
        o = out[32 * t : 32 * t + 16] + out[32 * t + 16 : 32 * t + 32]
        for h in range(2):
            y[32 * t + 16 * h : 32 * t + 16 * h + 16, :] = o[:, 128 * h : 128 * h + 128]
    low = low_lanes((192, 128))
    low96 = low_lanes((96, 128))
    parts = []
    for b in range(8):
        x = jnp.concatenate([y[pl.ds(c * 8 + b, 32, stride=16), :] for c in range(2)], axis=0)
        hi, lo = halves(x)
        parts.append(jnp.concatenate([hi, lo, hi], axis=0))
    out = dot(wz[...], jnp.concatenate(parts, axis=1))
    for b in range(8):
        o = out[:, 128 * b : 128 * b + 128]
        w = jnp.where(low, o[:192], o[192:])
        w = w + swap(w)
        w = jnp.where(low96, w[:96], w[96:])
        for zl in range(3):
            send[pl.ds(256 * zl + b, 32, stride=8), :] = w[32 * zl : 32 * zl + 32]


def basis_rows(cur, hcur, prev, hprev, res, liver, bsend):
    def tile(d, carry):
        at = pl.ds(pl.multiple_of(384 * d, 128), 384)
        live = liver[:, at] > 0.0
        for c in range(2):
            bsend[d, c] = jnp.where(live, cur[c, :, at], 0.0)
            bsend[d, 2 + c] = res[8 * c : 8 * c + 8, at]
            bsend[d, 4 + c] = jnp.where(live, prev[c, :, at], 0.0)
            bsend[d, 6 + c] = jnp.where(live, hcur[c, :, at], 0.0)
            bsend[d, 8 + c] = jnp.where(live, hprev[c, :, at], 0.0)
        return carry

    lax.fori_loop(0, NBD, tile, 0)


def greet_everyone():
    f, b = lax.axis_index("fft"), lax.axis_index("band")
    barrier = pltpu.get_barrier_semaphore()

    def greet(i, c):
        pl.semaphore_signal(barrier, inc=1, device_id=(b, lax.rem(f + i, NF)), device_id_type=MESH)
        return c

    def greet_b(i, c):
        pl.semaphore_signal(barrier, inc=1, device_id=(lax.rem(b + i, NBD), f), device_id_type=MESH)
        return c

    lax.fori_loop(1, NF, greet, 0)
    lax.fori_loop(1, NBD, greet_b, 0)


def everyone_in():
    pl.semaphore_wait(pltpu.get_barrier_semaphore(), NF - 1 + NBD - 1)


FAR_FIRST = sorted(
    [(dx, dz) for dx in range(4) for dz in range(8) if dx or dz], key=lambda o: -min(o[0], 4 - o[0]) - min(o[1], 8 - o[1]))


def whole(ref, sem):
    pltpu.make_async_copy(ref, ref, sem).wait()


class FftExchange:
    def __init__(self, src, dst, ssem, rsem):
        self.a = (src, dst, ssem, rsem)

    def start(self, g=0):
        src, dst, ssem, rsem = self.a
        f, b = lax.axis_index("fft"), lax.axis_index("band")
        to_me = dst.at[pl.ds(pl.multiple_of(256 * g + 8 * f, 8), 8), :]

        for dx, dz in FAR_FIRST:
            to = lax.rem(f // 8 + dx, 4) * 8 + lax.rem(f + dz, 8)
            pltpu.make_async_remote_copy(
                src_ref=src.at[pl.ds(pl.multiple_of(256 * g + 8 * to, 8), 8), :], dst_ref=to_me,
                send_sem=ssem.at[g], recv_sem=rsem.at[g], device_id=(b, to), device_id_type=MESH).start()
        own = src.at[pl.ds(pl.multiple_of(256 * g + 8 * f, 8), 8), :]
        pltpu.make_async_copy(own, to_me, rsem.at[g]).start()

    def wait(self, g=0):
        src, dst, ssem, rsem = self.a
        whole(dst.at[pl.ds(pl.multiple_of(256 * g, 256), 256), :], rsem.at[g])

    def sent(self, g=0):
        src, dst, ssem, rsem = self.a
        whole(src.at[pl.ds(256 * g, 248), :], ssem.at[g])


class BandExchange:
    def __init__(self, src, dst, place, ssem, rsem):
        self.a = (src, dst, place, ssem, rsem)

    def start(self):
        src, dst, place, ssem, rsem = self.a
        f, b = lax.axis_index("fft"), lax.axis_index("band")
        for i in range(1, NBD):
            to = lax.rem(b + i, NBD)
            pltpu.make_async_remote_copy(
                src_ref=src.at[to], dst_ref=place(dst, b), send_sem=ssem, recv_sem=rsem,
                device_id=(to, f), device_id_type=MESH).start()
        pltpu.make_async_copy(src.at[b], place(dst, b), rsem).start()

    def wait(self):
        src, dst, place, ssem, rsem = self.a
        whole(dst, rsem)

    def sent(self):
        src, dst, place, ssem, rsem = self.a
        whole(src.at[pl.ds(0, NBD - 1)], ssem)


class BandSum:
    def __init__(self, src, got, mid, dst, sems):
        self.a = (src, got, mid, dst, sems)
        b = lax.axis_index("band")
        self.y, self.c = b // 2, lax.rem(b, 2)

    def first(self):
        src, got, mid, dst, sems = self.a
        pltpu.make_async_remote_copy(
            src_ref=src.at[1 - self.c], dst_ref=got, send_sem=sems.at[0], recv_sem=sems.at[1],
            device_id=(2 * self.y + 1 - self.c, lax.axis_index("fft")), device_id_type=MESH).start()

    def second(self):
        src, got, mid, dst, sems = self.a
        whole(got, sems.at[1])
        mid[...] = src[self.c] + got[...]
        for i in (2, 1, 3):
            to = lax.rem(self.y + i, 4)
            pltpu.make_async_remote_copy(
                src_ref=mid.at[to], dst_ref=dst.at[self.y], send_sem=sems.at[2], recv_sem=sems.at[3],
                device_id=(2 * to + self.c, lax.axis_index("fft")), device_id_type=MESH).start()
        pltpu.make_async_copy(mid.at[self.y], dst.at[self.y], sems.at[3]).start()

    def total(self):
        src, got, mid, dst, sems = self.a
        whole(dst, sems.at[3])
        return (dst[0] + dst[1]) + (dst[2] + dst[3])

    def sent(self):
        src, got, mid, dst, sems = self.a
        whole(got, sems.at[0])
        whole(mid.at[pl.ds(0, 3)], sems.at[2])


def band_rows(dst, frm):
    return dst.at[:, pl.ds(pl.multiple_of(frm * 8, 8), 8), :]


def plane_maps(scols, pot, hit, mask, fourr, potp):
    low1 = low_lanes((1, 128))
    rows = lax.broadcasted_iota(jnp.int32, (256, 128), 0)
    for k in range(16):
        col = jnp.where(low1, swap(scols[2 * k : 2 * k + 1, :]), scols[2 * k + 1 : 2 * k + 2, :])
        live = col >= 0
        colp = jnp.maximum(col, 0)
        xc = div96(colp)
        xi = signed(xc) + CUT
        yi = signed(colp - xc * L) + CUT
        four = jnp.where(live, xi >> 2, -1)
        at = pl.ds(128 * k, 128)
        fourr[:, at] = jnp.broadcast_to(four, (8, 128))
        hit[:, at] = one_hot_rows(jnp.where(live, (xi & 3) * 64 + yi, -1), rows)
        for t, m in enumerate(four_masks(four)):
            mask[16 * t : 16 * t + 16, at] = m
    potp[...] = jnp.zeros((3, L, 128), F32)
    potp[:, :, 0:L] = pot[...]


def place(g, recv, hit, mask, lhs, pm):
    low = low_lanes((8, 128))
    for k in range(16):
        at = pl.ds(128 * k, 128)
        base = pl.multiple_of(256 * g + 16 * k, 16)
        r0, r1 = recv[pl.ds(base, 8), :], recv[pl.ds(base + 8, 8), :]
        hi, lo = halves(jnp.concatenate([jnp.where(low, r0, swap(r1)), jnp.where(low, swap(r0), r1)], axis=0))
        for t in range(NT):
            m = mask[16 * t : 16 * t + 16, at]
            lhs[32 * t : 32 * t + 16, at] = hi * m
            lhs[32 * t + 16 : 32 * t + 32, at] = lo * m
    out = dot_nt(lhs[...], hit[...])
    for t in range(NT):
        o = out[32 * t : 32 * t + 16] + out[32 * t + 16 : 32 * t + 32]
        for h in range(2):
            re, im = o[:8, 128 * h : 128 * h + 128], o[8:, 128 * h : 128 * h + 128]
            base = 32 * t + 16 * h
            pm[base : base + 8, :] = jnp.where(low, re, swap(im))
            pm[base + 8 : base + 16, :] = jnp.where(low, swap(re), im)


def along_y(pm, wy, tt):
    hi, lo = halves(pm[0:416, :])
    out = dot(jnp.concatenate([hi, lo], axis=1), wy[0:256, :]) + dot(hi, wy[256:384, :])
    tt[0, 0:416, :] = out[:, 0:128]
    tt[1, 0:416, :] = out[:, 128:256]
    tt[:, 416:448, :] = jnp.zeros((2, 32, 128), F32)


def along_x(g, tt, potp, wx, vx, vy, gg):
    pv = potp[g]
    pv = jnp.concatenate([pv] * 8, axis=1)
    pv = jnp.concatenate([pv, pv], axis=0)
    his, los = [], []
    for b in range(8):
        hi, lo = halves(jnp.concatenate([tt[c, pl.ds(b, 56, stride=8), :] for c in range(2)], axis=0))
        his.append(hi)
        los.append(lo)
    hi = jnp.concatenate(his, axis=1)
    u = dot(wx[...], jnp.concatenate([hi, jnp.concatenate(los, axis=1), hi], axis=0))
    hi, lo = halves(u * pv)
    t = dot(vx[...], jnp.concatenate([hi, lo, hi], axis=0))
    hi, lo = halves(jnp.concatenate(
        [jnp.concatenate([t[56 * c : 56 * c + 56, 128 * b : 128 * b + 128] for c in range(2)], axis=1) for b in range(8)],
        axis=0))
    a = dot(hi, vy[...])
    q = a[:, 0:128] + a[:, 128:256] + dot(lo, vy[:, 0:128])
    for b in range(8):
        gg[pl.ds(b, 56, stride=8), :] = q[56 * b : 56 * b + 56]


def fours(src, low):
    blocks = []
    for t in range(NT):
        cols = []
        for h in range(2):
            base = 32 * t + 16 * h
            g0, g1 = src[base : base + 8, :], src[base + 8 : base + 16, :]
            cols.append(jnp.concatenate([jnp.where(low, g0, swap(g1)), jnp.where(low, swap(g0), g1)], axis=0))
        blocks.append(jnp.concatenate(cols, axis=1))
    hi, lo = halves(jnp.concatenate(blocks, axis=0))
    return jnp.concatenate([hi, lo], axis=1)


def pick(lhs, hit, fourr, n, width):
    at = pl.ds(n * width, width)
    d = hit[:, at]
    out = dot(lhs, jnp.concatenate([d, d], axis=0))
    f = fourr[:, at]
    f = jnp.concatenate([f, f], axis=0)
    acc = jnp.zeros((16, width), F32)
    for t in range(NT):
        acc = jnp.where(f == t, out[16 * t : 16 * t + 16], acc)
    return acc


def collect(g, gg, hit, fourr, gl, send):
    low = low_lanes((8, 128))
    gl[...] = fours(gg, low)
    for n in range(8):
        acc = pick(gl[...], hit, fourr, n, 256)
        for k in range(2):
            re, im = acc[0:8, 128 * k : 128 * k + 128], acc[8:16, 128 * k : 128 * k + 128]
            base = pl.multiple_of(256 * g + 32 * n + 16 * k, 16)
            send[pl.ds(base, 8), :] = jnp.where(low, re, swap(im))
            send[pl.ds(base + 8, 8), :] = jnp.where(low, swap(re), im)


def row_side(brecv, qs):
    zero = jnp.zeros((8, 768), F32)
    for d in range(NBD):
        for j in range(3):
            g8 = 3 * d + j
            ty, r0 = g8 // 8, (g8 % 8) * 8
            re, im = brecv[2 * ty, r0 : r0 + 8, :], brecv[2 * ty + 1, r0 : r0 + 8, :]
            o = 64 * (4 * (d % 2) + d // 2) + 8 * j
            qs[o : o + 8, 0:384] = re
            qs[o : o + 8, 384:768] = im
            qs[o + 32 : o + 40, 0:384] = -im
            qs[o + 32 : o + 40, 384:768] = re
        qs[64 * d + 24 : 64 * d + 32, :] = zero
        qs[64 * d + 56 : 64 * d + 64, :] = zero


def early_gram(brecv, qs, qcat, flat, esend):
    hi, lo = halves(qs[...])
    qcat[...] = jnp.concatenate([hi, hi, lo], axis=1)
    for i in range(5):
        flat[64 * i : 64 * i + 64, 0:384] = brecv[2 * i]
        flat[64 * i : 64 * i + 64, 384:768] = brecv[2 * i + 1]
    hi, lo = halves(flat[...])
    out = dot_nt(jnp.concatenate([hi, lo, hi], axis=1), qcat[...])
    low = low_lanes((192, 128))
    zero = jnp.zeros((64, 128), F32)
    for n in range(4):
        o = out[:, 128 * n : 128 * n + 128]
        c, h = o[0:192], jnp.concatenate([o[192:256], zero, o[256:320]], axis=0)
        esend[n // 2, 2 * (n % 2)] = jnp.where(low, c, swap(h))
        esend[n // 2, 2 * (n % 2) + 1] = jnp.where(low, swap(c), h)


def term(recv, res, hit, fourr, kinr, liver, vz, hres, hsend, z, zl_):
    his, los = [], []
    for b in range(8):
        hi, lo = halves(jnp.concatenate([recv[pl.ds(256 * zl + b, 32, stride=8), :] for zl in range(3)], axis=0))
        his.append(hi)
        los.append(lo)
    hi = jnp.concatenate(his, axis=1)
    out = dot(vz[...], jnp.concatenate([hi, jnp.concatenate(los, axis=1), hi], axis=0))
    low = low_lanes((64, 128))
    for b in range(8):
        o = out[:, 128 * b : 128 * b + 128]
        other = swap(o[64:128])
        z[pl.ds(b, 64, stride=8), :] = o[0:64] + jnp.where(low, other, -other)
    zl_[...] = fours(z, low_lanes((8, 128)))
    for n in range(12):
        at = pl.ds(256 * n, 256)
        acc = pick(zl_[...], hit, fourr, n, 256)
        live = liver[:, at] > 0.0
        for c in range(2):
            v = kinr[:, at] * res[8 * c : 8 * c + 8, at] + acc[8 * c : 8 * c + 8] * (1.0 / float(L**3))
            v = jnp.where(live, v, 0.0)
            hres[c, :, at] = v
            for k in range(2):
                q = 2 * n + k
                hsend[q // 3, c, :, (q % 3) * 128 : (q % 3) * 128 + 128] = v[:, 128 * k : 128 * k + 128]


F0, F1 = 10, 22


def late_gram(hrecv, qcat, flat, lsend, start):
    flat[0:64, 0:384] = hrecv[0]
    flat[0:64, 384:768] = hrecv[1]
    hi, lo = halves(flat[0:64, :])
    cat = jnp.concatenate([hi, lo, hi], axis=1)
    low = low_lanes((32, 128))
    mine = lax.rem(lax.axis_index("band"), 2)
    for core in (1 - mine, mine):
        out = dot_nt(cat, qcat[pl.ds(pl.multiple_of(256 * core, 256), 256), :])
        for n in range(2):
            a, b = out[0:32, 128 * n : 128 * n + 128], out[32:64, 128 * n : 128 * n + 128]
            lsend[core, 2 * n] = jnp.where(low, a, swap(b))
            lsend[core, 2 * n + 1] = jnp.where(low, swap(a), b)
        if core is not mine:
            start()


def late_tiles(total, la, lb, fl):
    other = swap(total)
    la[8:40, :], la[40:72, :] = total, other
    lb[8:40, :], lb[40:72, :] = other, total
    low = low_lanes((3, 128))
    for i in range(F1 - F0):
        r = 8 + 6 * (F0 + i) - 64
        fl[8 * i : 8 * i + 3, :] = jnp.where(low, la[r : r + 3, :], lb[r + 3 : r + 6, :])


class LateExchange:
    def __init__(self, src, dst, ssem, rsem):
        self.a = (src, dst, ssem, rsem)
        self.f = lax.axis_index("fft")
        self.owner = jnp.logical_and(self.f >= F0, self.f < F1)

    def start(self):
        src, dst, ssem, rsem = self.a
        f, b = self.f, lax.axis_index("band")
        to_me = dst.at[pl.ds(pl.multiple_of(8 * f, 8), 4), :]
        for i in range(F1 - F0):
            n = lax.rem(f + i, F1 - F0)
            part = src.at[pl.ds(pl.multiple_of(8 * n, 8), 4), :]

            @pl.when(n + F0 != f)
            def _():
                pltpu.make_async_remote_copy(
                    src_ref=part, dst_ref=to_me, send_sem=ssem, recv_sem=rsem, device_id=(b, n + F0),
                    device_id_type=MESH).start()

        @pl.when(self.owner)
        def _():
            own = src.at[pl.ds(pl.multiple_of(8 * (f - F0), 8), 4), :]
            pltpu.make_async_copy(own, to_me, rsem).start()

    def add(self, out, scale):
        src, dst, ssem, rsem = self.a

        @pl.when(self.owner)
        def _():
            whole(dst.at[pl.ds(0, 4 * NF), :], rsem)
            total = dst[0:4, :]
            for d in range(1, NF):
                total = total + dst[8 * d : 8 * d + 4, :]
            total = total[0:3] * scale
            low = low_lanes((3, 128))
            out[0:3, :] = out[0:3, :] + jnp.where(low, 0.0, swap(total))
            out[3:6, :] = out[3:6, :] + jnp.where(low, 0.0, total)

    def sent(self):
        src, dst, ssem, rsem = self.a
        whole(src.at[pl.ds(0, 44), :], ssem)
        pl.when(jnp.logical_not(self.owner))(lambda: whole(src.at[pl.ds(0, 4), :], ssem))


def step_kernel(ev_h, cur_h, hcur_h, prev_h, hprev_h, gm_h, scols_h, pot_h, wz_h, wy_h, wx_h, vx_h, vy_h,
                vz_h, hres_h, out,
                ev, cur, hcur, prev, hprev, gm, scols, pot, wz, wy, wx, vx, vy, vz, hres,
                res, kinr, gfour, liver, ghit, glhs, y, send, bsend,
                recv, brecv, shit, smask, sfour, slhs, potp, pm, tt, gg, gl, send2, recv2,
                qs, qcat, flat, esum, esend, egot, emid, erecv, z, zl, hsend, hrecv, la, lb,
                lsend, lgot, lmid, lrecv, fl, lrow, fsend, frecv, s1, r1, s3, r3, s4, s6, sems, load):
    pairs = [(ev_h, ev), (gm_h, gm), (scols_h, scols), (cur_h, cur), (hcur_h, hcur), (wz_h, wz), (prev_h, prev), (hprev_h, hprev),
             (pot_h, pot), (wy_h, wy), (wx_h, wx), (vx_h, vx), (vy_h, vy), (vz_h, vz)]
    loads = [pltpu.make_async_copy(a, b, load.at[i]) for i, (a, b) in enumerate(pairs)]
    for copy in loads:
        copy.start()
    greet_everyone()
    for copy in loads[:6]:
        copy.wait()
    x1 = FftExchange(send, recv, s1, r1)
    x2 = BandExchange(bsend, brecv, band_rows, sems.at[0], sems.at[1])
    x3 = FftExchange(send2, recv2, s3, r3)
    x4 = BandSum(esend, egot, emid, erecv, s4)
    x5 = BandExchange(hsend, hrecv, band_rows, sems.at[4], sems.at[5])
    x6 = BandSum(lsend, lgot, lmid, lrecv, s6)
    x8 = LateExchange(fl, lrow, sems.at[6], sems.at[7])
    x7 = FftExchange(fsend, frecv, sems.at[pl.ds(8, 1)], sems.at[pl.ds(9, 1)])
    residual(ev, cur, hcur, gm, scols, res, glhs, ghit, kinr, gfour, liver)
    sticks(glhs, ghit, wz, send, y)
    everyone_in()
    for g in range(3):
        x1.start(g)
    for copy in loads[6:]:
        copy.wait()
    basis_rows(cur, hcur, prev, hprev, res, liver, bsend)
    x2.start()
    plane_maps(scols, pot, shit, smask, sfour, potp)

    def plane(g, carry):
        x1.wait(g)
        place(g, recv, shit, smask, slhs, pm)
        along_y(pm, wy, tt)
        along_x(g, tt, potp, wx, vx, vy, gg)
        collect(g, gg, shit, sfour, gl, send2)
        x3.start(g)
        return carry

    lax.fori_loop(0, 3, plane, 0)
    x2.wait()
    row_side(brecv, qs)
    early_gram(brecv, qs, qcat, flat, esend)
    x4.first()
    x4.second()
    for g in range(3):
        x3.wait(g)
    term(recv2, res, ghit, gfour, kinr, liver, vz, hres, hsend, z, zl)
    x5.start()
    store = pltpu.make_async_copy(hres, hres_h, load.at[15])
    store.start()
    esum[...] = x4.total()
    fsend[...] = jnp.zeros((256, 128), F32)
    for f in range(NF):
        fsend[8 * f : 8 * f + 6, :] = esum[6 * f : 6 * f + 6, :]
    x7.start()
    fl[...] = jnp.zeros((8 * (F1 - F0), 128), F32)
    la[...] = jnp.zeros((80, 128), F32)
    lb[...] = jnp.zeros((80, 128), F32)
    x5.wait()
    late_gram(hrecv, qcat, flat, lsend, x6.first)
    x6.second()
    x7.wait()
    total = frecv[0:8, :]
    for d in range(1, NF):
        total = total + frecv[8 * d : 8 * d + 8, :]
    scale = 8.0 / float(L**3)
    out[...] = total * scale
    late_tiles(x6.total(), la, lb, fl)
    x8.start()
    x8.add(out, scale)
    store.wait()
    for g in range(3):
        x1.sent(g)
        x3.sent(g)
    for x in (x2, x4, x5, x6, x7, x8):
        x.sent()


def sds(*shape):
    return jax.ShapeDtypeStruct(shape, F32)


DMA = pltpu.SemaphoreType.DMA
BIG = 64 * 1024 * 1024


def local(current, h_current, previous, h_previous, eigen_values, potential, stick_cols, g_map):
    w = tables()
    gm = g_map.reshape(1, 3072)
    sc = stick_cols.reshape(NF, 128)
    vm = lambda *shape: pltpu.VMEM(shape, F32)
    v16 = lambda *shape: pltpu.VMEM(shape, BF16)
    vi = lambda *shape: pltpu.VMEM(shape, jnp.int32)
    hres, tile = pl.pallas_call(
        step_kernel, out_shape=(sds(2, 8, 3072), sds(8, 128)), in_specs=[HB] * 14, out_specs=(HB, VM),
        scratch_shapes=[
            pltpu.SMEM((8,), F32), vm(2, 8, 3072), vm(2, 8, 3072), vm(2, 8, 3072), vm(2, 8, 3072), vi(1, 3072), vi(NF, 128), vm(3, L, L),
            v16(384, 192), v16(384, 256), v16(192, 336), v16(112, 576), v16(256, 256), v16(128, 288),
            vm(2, 8, 3072),
            vm(16, 3072), vm(8, 3072), vi(8, 3072), vm(8, 3072), v16(256, 3072), v16(416, 3072), vm(512, 128),
            vm(768, 128), vm(8, 10, 8, 384),
            vm(768, 128), vm(10, 64, 384), v16(256, 2048), v16(208, 2048), vi(8, 2048), v16(416, 2048),
            vm(3, L, 128), vm(416, 128), vm(2, 448, 128), vm(448, 128), v16(208, 512), vm(768, 128), vm(768, 128),
            vm(512, 768), v16(512, 2304), vm(320, 768), vm(192, 128), vm(2, 4, 192, 128), vm(4, 192, 128), vm(4, 192, 128),
            vm(4, 192, 128), vm(512, 128),
            v16(208, 512), vm(8, 2, 8, 384), vm(2, 64, 384), vm(80, 128), vm(80, 128), vm(2, 4, 32, 128), vm(4, 32, 128), vm(4, 32, 128),
            vm(4, 32, 128), vm(96, 128), vm(256, 128),
            vm(256, 128), vm(256, 128), DMA((3,)), DMA((3,)), DMA((3,)), DMA((3,)), DMA((4,)), DMA((4,)), DMA((10,)), DMA((16,))],
        compiler_params=pltpu.CompilerParams(collective_id=0, has_side_effects=True, vmem_limit_bytes=BIG), name="step",
    )(eigen_values, current, h_current, previous, h_previous, gm, sc, potential,
      w["wz"], w["wy"], w["wx"], w["vx"], w["vy"], w["vz"])
    mats = jnp.transpose(tile[0:6].reshape(6, 4, 32)[:, :, 0:24], (1, 2, 0))
    return hres, mats[0:2], mats[2:4]


def solution(mesh):
    bf = P(None, "band", "fft")
    in_specs = (bf, bf, bf, bf, P("band"), P("fft", None, None), P(), P("fft"))
    return jax.shard_map(local, mesh=mesh, in_specs=in_specs, out_specs=(bf, bf, bf), check_vma=False)
```

```python
import math

import jax
import jax.numpy as jnp
import ml_dtypes
import numpy as np
from jax import lax
from jax.experimental import pallas as pl
from jax.experimental.pallas import tpu as pltpu
from jax.sharding import PartitionSpec as P

L = 96
CUT = 24
F32 = jnp.float32
BF16 = jnp.bfloat16
NF = 32
NBD = 8
GT = 24
NT = 13
MESH = pl.DeviceIdType.MESH
VM = pl.BlockSpec(memory_space=pltpu.VMEM)
HB = pl.BlockSpec(memory_space=pltpu.HBM)
SM = pl.BlockSpec(memory_space=pltpu.SMEM)


def split_np(table):
    high = table.astype(ml_dtypes.bfloat16)
    low = (table - high.astype(np.float64)).astype(ml_dtypes.bfloat16)
    return high, low


def tables():
    zout = (np.arange(NF)[None, :] * 3 + np.arange(3)[:, None]).reshape(-1)
    wz = np.zeros((2, 2, L, 2, 32))
    for par in range(2):
        zi = 2 * np.arange(32) + par
        ok = zi <= 2 * CUT
        ang = 2 * math.pi / L * ((zout[:, None] * (zi - CUT)[None, :]) % L)
        c, s = np.cos(ang) * ok, np.sin(ang) * ok
        wz[par, 0, :, 0], wz[par, 0, :, 1] = c, -s
        wz[par, 1, :, 0], wz[par, 1, :, 1] = s, c
    zh, zl = split_np(wz.reshape(384, 64))
    wz = np.concatenate([zh, zh, zl], axis=1)
    n = np.arange(L)
    k = np.arange(49) - CUT
    ang = 2 * math.pi / L * ((k[:, None] * n[None, :]) % L)
    c, s = np.cos(ang), np.sin(ang)
    wy = np.zeros((2, 64, 2, 128))
    wy[0, :49, 0, :L], wy[0, :49, 1, :L] = c, s
    wy[1, :49, 0, :L], wy[1, :49, 1, :L] = -s, c
    yh, yl = split_np(wy.reshape(128, 256))
    wy = np.concatenate([yh, yh, yl], axis=0)
    wx = np.zeros((2, L, 2, 56))
    wx[0, :, 0, :49], wx[0, :, 1, :49] = c.T, -s.T
    wx[1, :, 0, :49], wx[1, :, 1, :49] = s.T, c.T
    xh, xl = split_np(wx.reshape(192, 112))
    wx = np.concatenate([xh, xh, xl], axis=1)
    vx = np.zeros((2, 56, 2, L))
    vx[0, :49, 0], vx[0, :49, 1] = c, s
    vx[1, :49, 0], vx[1, :49, 1] = -s, c
    vh, vl = split_np(vx.reshape(112, 192))
    vx = np.concatenate([vh, vh, vl], axis=1)
    vy = np.zeros((2, 128, 2, 64))
    vy[0, :L, 0, :49], vy[0, :L, 1, :49] = c.T, -s.T
    vy[1, :L, 0, :49], vy[1, :L, 1, :49] = s.T, c.T
    vyh, vyl = split_np(vy.reshape(256, 128))
    vy = np.concatenate([vyh, vyl], axis=1)
    vz = np.zeros((2, 64, L))
    ang = 2 * math.pi / L * ((k[:, None] * zout[None, :]) % L)
    vz[0, :49], vz[1, :49] = np.cos(ang), np.sin(ang)
    zbh, zbl = split_np(vz.reshape(128, L))
    vz = np.concatenate([zbh, zbh, zbl], axis=1)
    return dict(wz=wz, wy=wy, wx=wx, vx=vx, vy=vy, vz=vz)


def dot(a, b):
    return jnp.dot(a, b, preferred_element_type=F32)


def dot_nt(a, b):
    return lax.dot_general(a, b, (((1,), (1,)), ((), ())), preferred_element_type=F32)


def halves(x):
    hi = x.astype(BF16)
    return hi, (x - hi.astype(F32)).astype(BF16)


def low_lanes(shape):
    return lax.broadcasted_iota(jnp.int32, shape, len(shape) - 1) < 64


def swap(x):
    return pltpu.roll(x, 64, 1)


def div96(v):
    return (v * 43691) >> 22


def signed(v):
    return jnp.where(v >= L // 2, v - L, v)


def lanes_of(x, index):
    return jnp.take_along_axis(x, index, axis=1, mode="promise_in_bounds")


def slot_facts(m, cols):
    live = m >= 0
    ms = jnp.maximum(m, 0)
    slot = div96(ms)
    z = signed(ms - slot * L)
    col = jnp.where(live, lanes_of(cols, slot), 0)
    xc = div96(col)
    x = signed(xc)
    y = signed(col - xc * L)
    norm = x * x + y * y + z * z
    kin = jnp.where(live, 64.0 * norm.astype(F32) / float(L * L), 0.0)
    zi = z + CUT
    four = jnp.where(live, zi >> 2, -1)
    lane = jnp.where(live, (zi & 3) * 64 + slot - 64, -1)
    return live, kin, four, lane


def one_hot_rows(key, rows):
    return jnp.where(jnp.broadcast_to(key, (256, 128)) == rows, 1.0, 0.0).astype(BF16)


def four_masks(four):
    wide = jnp.broadcast_to(four, (16, 128))
    return [jnp.where(wide == t, 1.0, 0.0).astype(BF16) for t in range(NT)]


def residual(ev, cur, hcur, gm, scols, res, lhs, hit, kinr, fourr, liver):
    me = lax.axis_index("fft")
    cols = jnp.broadcast_to(scols[pl.ds(me, 1), :], (8, 128))
    row = lax.broadcasted_iota(jnp.int32, (8, 128), 0)
    evc = jnp.zeros((8, 128), F32)
    for b in range(8):
        evc = jnp.where(row == b, ev[b], evc)
    rows = lax.broadcasted_iota(jnp.int32, (256, 128), 0)

    for k in range(GT):
        at = pl.ds(128 * k, 128)
        live, kin, four, lane = slot_facts(jnp.broadcast_to(gm[:, at], (8, 128)), cols)
        kinr[:, at] = kin
        fourr[:, at] = four
        liver[:, at] = live.astype(F32)
        den = 1.0 + kin
        r = jnp.concatenate(
            [jnp.where(live, (hcur[c, :, at] - evc * cur[c, :, at]) / den, 0.0) for c in range(2)], axis=0)
        res[:, at] = r
        hi, lo = halves(r)
        hit[:, at] = one_hot_rows(lane[:1], rows)
        for t, m in enumerate(four_masks(four[:1])):
            lhs[32 * t : 32 * t + 16, at] = hi * m
            lhs[32 * t + 16 : 32 * t + 32, at] = lo * m


def sticks(lhs, hit, wz, send, y):
    out = dot_nt(lhs[...], hit[...])
    y[416:512, :] = jnp.zeros((96, 128), F32)
    for t in range(NT):
        o = out[32 * t : 32 * t + 16] + out[32 * t + 16 : 32 * t + 32]
        for h in range(2):
            y[32 * t + 16 * h : 32 * t + 16 * h + 16, :] = o[:, 128 * h : 128 * h + 128]
    low = low_lanes((192, 128))
    low96 = low_lanes((96, 128))
    parts = []
    for b in range(8):
        x = jnp.concatenate([y[pl.ds(c * 8 + b, 32, stride=16), :] for c in range(2)], axis=0)
        hi, lo = halves(x)
        parts.append(jnp.concatenate([hi, lo, hi], axis=0))
    out = dot(wz[...], jnp.concatenate(parts, axis=1))
    for b in range(8):
        o = out[:, 128 * b : 128 * b + 128]
        w = jnp.where(low, o[:192], o[192:])
        w = w + swap(w)
        w = jnp.where(low96, w[:96], w[96:])
        for zl in range(3):
            send[pl.ds(256 * zl + b, 32, stride=8), :] = w[32 * zl : 32 * zl + 32]


def basis_rows(cur, hcur, prev, hprev, res, liver, bsend):
    def tile(d, carry):
        at = pl.ds(pl.multiple_of(384 * d, 128), 384)
        live = liver[:, at] > 0.0
        for c in range(2):
            bsend[d, c] = jnp.where(live, cur[c, :, at], 0.0)
            bsend[d, 2 + c] = res[8 * c : 8 * c + 8, at]
            bsend[d, 4 + c] = jnp.where(live, prev[c, :, at], 0.0)
            bsend[d, 6 + c] = jnp.where(live, hcur[c, :, at], 0.0)
            bsend[d, 8 + c] = jnp.where(live, hprev[c, :, at], 0.0)
        return carry

    lax.fori_loop(0, NBD, tile, 0)


def greet_everyone():
    f, b = lax.axis_index("fft"), lax.axis_index("band")
    barrier = pltpu.get_barrier_semaphore()

    def greet(i, c):
        pl.semaphore_signal(barrier, inc=1, device_id=(b, lax.rem(f + i, NF)), device_id_type=MESH)
        return c

    def greet_b(i, c):
        pl.semaphore_signal(barrier, inc=1, device_id=(lax.rem(b + i, NBD), f), device_id_type=MESH)
        return c

    lax.fori_loop(1, NF, greet, 0)
    lax.fori_loop(1, NBD, greet_b, 0)


def everyone_in():
    pl.semaphore_wait(pltpu.get_barrier_semaphore(), NF - 1 + NBD - 1)


FAR_FIRST = sorted(
    [(dx, dz) for dx in range(4) for dz in range(8) if dx or dz], key=lambda o: -min(o[0], 4 - o[0]) - min(o[1], 8 - o[1]))


def whole(ref, sem):
    pltpu.make_async_copy(ref, ref, sem).wait()


class FftExchange:
    def __init__(self, src, dst, ssem, rsem):
        self.a = (src, dst, ssem, rsem)

    def start(self, g=0):
        src, dst, ssem, rsem = self.a
        f, b = lax.axis_index("fft"), lax.axis_index("band")
        to_me = dst.at[pl.ds(pl.multiple_of(256 * g + 8 * f, 8), 8), :]

        for dx, dz in FAR_FIRST:
            to = lax.rem(f // 8 + dx, 4) * 8 + lax.rem(f + dz, 8)
            pltpu.make_async_remote_copy(
                src_ref=src.at[pl.ds(pl.multiple_of(256 * g + 8 * to, 8), 8), :], dst_ref=to_me,
                send_sem=ssem.at[g], recv_sem=rsem.at[g], device_id=(b, to), device_id_type=MESH).start()
        own = src.at[pl.ds(pl.multiple_of(256 * g + 8 * f, 8), 8), :]
        pltpu.make_async_copy(own, to_me, rsem.at[g]).start()

    def wait(self, g=0):
        src, dst, ssem, rsem = self.a
        whole(dst.at[pl.ds(256 * g, 256), :], rsem.at[g])

    def sent(self, g=0):
        src, dst, ssem, rsem = self.a
        whole(src.at[pl.ds(256 * g, 248), :], ssem.at[g])


class BandExchange:
    def __init__(self, src, dst, place, ssem, rsem):
        self.a = (src, dst, place, ssem, rsem)

    def start(self):
        src, dst, place, ssem, rsem = self.a
        f, b = lax.axis_index("fft"), lax.axis_index("band")
        for i in range(1, NBD):
            to = lax.rem(b + i, NBD)
            pltpu.make_async_remote_copy(
                src_ref=src.at[to], dst_ref=place(dst, b), send_sem=ssem, recv_sem=rsem,
                device_id=(to, f), device_id_type=MESH).start()
        pltpu.make_async_copy(src.at[b], place(dst, b), rsem).start()

    def wait(self):
        src, dst, place, ssem, rsem = self.a
        whole(dst, rsem)

    def sent(self):
        src, dst, place, ssem, rsem = self.a
        whole(src.at[pl.ds(0, NBD - 1)], ssem)


class BandSum:
    def __init__(self, src, got, mid, dst, sems):
        self.a = (src, got, mid, dst, sems)
        b = lax.axis_index("band")
        self.y, self.c = b // 2, lax.rem(b, 2)

    def first(self):
        src, got, mid, dst, sems = self.a
        pltpu.make_async_remote_copy(
            src_ref=src.at[1 - self.c], dst_ref=got, send_sem=sems.at[0], recv_sem=sems.at[1],
            device_id=(2 * self.y + 1 - self.c, lax.axis_index("fft")), device_id_type=MESH).start()

    def second(self):
        src, got, mid, dst, sems = self.a
        whole(got, sems.at[1])
        mid[...] = src[self.c] + got[...]
        for i in (2, 1, 3):
            to = lax.rem(self.y + i, 4)
            pltpu.make_async_remote_copy(
                src_ref=mid.at[to], dst_ref=dst.at[self.y], send_sem=sems.at[2], recv_sem=sems.at[3],
                device_id=(2 * to + self.c, lax.axis_index("fft")), device_id_type=MESH).start()
        pltpu.make_async_copy(mid.at[self.y], dst.at[self.y], sems.at[3]).start()

    def total(self):
        src, got, mid, dst, sems = self.a
        whole(dst, sems.at[3])
        return (dst[0] + dst[1]) + (dst[2] + dst[3])

    def sent(self):
        src, got, mid, dst, sems = self.a
        whole(got, sems.at[0])
        whole(mid.at[pl.ds(0, 3)], sems.at[2])


def band_rows(dst, frm):
    return dst.at[:, pl.ds(pl.multiple_of(frm * 8, 8), 8), :]


def plane_maps(scols, pot, hit, mask, fourr, potp):
    low1 = low_lanes((1, 128))
    rows = lax.broadcasted_iota(jnp.int32, (256, 128), 0)
    for k in range(16):
        col = jnp.where(low1, swap(scols[2 * k : 2 * k + 1, :]), scols[2 * k + 1 : 2 * k + 2, :])
        live = col >= 0
        colp = jnp.maximum(col, 0)
        xc = div96(colp)
        xi = signed(xc) + CUT
        yi = signed(colp - xc * L) + CUT
        four = jnp.where(live, xi >> 2, -1)
        at = pl.ds(128 * k, 128)
        fourr[:, at] = jnp.broadcast_to(four, (8, 128))
        hit[:, at] = one_hot_rows(jnp.where(live, (xi & 3) * 64 + yi, -1), rows)
        for t, m in enumerate(four_masks(four)):
            mask[16 * t : 16 * t + 16, at] = m
    potp[...] = jnp.zeros((3, L, 128), F32)
    potp[:, :, 0:L] = pot[...]


def place(g, recv, hit, mask, lhs, pm):
    low = low_lanes((8, 128))
    for k in range(16):
        at = pl.ds(128 * k, 128)
        base = 256 * g + 16 * k
        r0, r1 = recv[pl.ds(base, 8), :], recv[pl.ds(base + 8, 8), :]
        hi, lo = halves(jnp.concatenate([jnp.where(low, r0, swap(r1)), jnp.where(low, swap(r0), r1)], axis=0))
        for t in range(NT):
            m = mask[16 * t : 16 * t + 16, at]
            lhs[32 * t : 32 * t + 16, at] = hi * m
            lhs[32 * t + 16 : 32 * t + 32, at] = lo * m
    out = dot_nt(lhs[...], hit[...])
    for t in range(NT):
        o = out[32 * t : 32 * t + 16] + out[32 * t + 16 : 32 * t + 32]
        for h in range(2):
            re, im = o[:8, 128 * h : 128 * h + 128], o[8:, 128 * h : 128 * h + 128]
            base = 32 * t + 16 * h
            pm[base : base + 8, :] = jnp.where(low, re, swap(im))
            pm[base + 8 : base + 16, :] = jnp.where(low, swap(re), im)


def along_y(pm, wy, tt):
    hi, lo = halves(pm[0:416, :])
    out = dot(jnp.concatenate([hi, lo], axis=1), wy[0:256, :]) + dot(hi, wy[256:384, :])
    tt[0, 0:416, :] = out[:, 0:128]
    tt[1, 0:416, :] = out[:, 128:256]
    tt[:, 416:448, :] = jnp.zeros((2, 32, 128), F32)


def along_x(g, tt, potp, wx, vx, vy, gg):
    pv = potp[g]
    pv = jnp.concatenate([pv] * 8, axis=1)
    pv = jnp.concatenate([pv, pv], axis=0)
    his, los = [], []
    for b in range(8):
        hi, lo = halves(jnp.concatenate([tt[c, pl.ds(b, 56, stride=8), :] for c in range(2)], axis=0))
        his.append(hi)
        los.append(lo)
    hi = jnp.concatenate(his, axis=1)
    u = dot(wx[...], jnp.concatenate([hi, jnp.concatenate(los, axis=1), hi], axis=0))
    hi, lo = halves(u * pv)
    t = dot(vx[...], jnp.concatenate([hi, lo, hi], axis=0))
    hi, lo = halves(jnp.concatenate(
        [jnp.concatenate([t[56 * c : 56 * c + 56, 128 * b : 128 * b + 128] for c in range(2)], axis=1) for b in range(8)],
        axis=0))
    a = dot(hi, vy[...])
    q = a[:, 0:128] + a[:, 128:256] + dot(lo, vy[:, 0:128])
    for b in range(8):
        gg[pl.ds(b, 56, stride=8), :] = q[56 * b : 56 * b + 56]


def fours(src, low):
    blocks = []
    for t in range(NT):
        cols = []
        for h in range(2):
            base = 32 * t + 16 * h
            g0, g1 = src[base : base + 8, :], src[base + 8 : base + 16, :]
            cols.append(jnp.concatenate([jnp.where(low, g0, swap(g1)), jnp.where(low, swap(g0), g1)], axis=0))
        blocks.append(jnp.concatenate(cols, axis=1))
    hi, lo = halves(jnp.concatenate(blocks, axis=0))
    return jnp.concatenate([hi, lo], axis=1)


def pick(lhs, hit, fourr, n, width):
    at = pl.ds(n * width, width)
    d = hit[:, at]
    out = dot(lhs, jnp.concatenate([d, d], axis=0))
    f = fourr[:, at]
    f = jnp.concatenate([f, f], axis=0)
    acc = jnp.zeros((16, width), F32)
    for t in range(NT):
        acc = jnp.where(f == t, out[16 * t : 16 * t + 16], acc)
    return acc


def collect(g, gg, hit, fourr, gl, send):
    low = low_lanes((8, 128))
    gl[...] = fours(gg, low)
    for n in range(8):
        acc = pick(gl[...], hit, fourr, n, 256)
        for k in range(2):
            re, im = acc[0:8, 128 * k : 128 * k + 128], acc[8:16, 128 * k : 128 * k + 128]
            base = 256 * g + 32 * n + 16 * k
            send[pl.ds(base, 8), :] = jnp.where(low, re, swap(im))
            send[pl.ds(base + 8, 8), :] = jnp.where(low, swap(re), im)


def row_side(brecv, qs):
    zero = jnp.zeros((8, 768), F32)
    for d in range(NBD):
        for j in range(3):
            g8 = 3 * d + j
            ty, r0 = g8 // 8, (g8 % 8) * 8
            re, im = brecv[2 * ty, r0 : r0 + 8, :], brecv[2 * ty + 1, r0 : r0 + 8, :]
            o = 64 * (4 * (d % 2) + d // 2) + 8 * j
            qs[o : o + 8, 0:384] = re
            qs[o : o + 8, 384:768] = im
            qs[o + 32 : o + 40, 0:384] = -im
            qs[o + 32 : o + 40, 384:768] = re
        qs[64 * d + 24 : 64 * d + 32, :] = zero
        qs[64 * d + 56 : 64 * d + 64, :] = zero


def early_gram(brecv, qs, qcat, flat, esend):
    hi, lo = halves(qs[...])
    qcat[...] = jnp.concatenate([hi, hi, lo], axis=1)
    for i in range(5):
        flat[64 * i : 64 * i + 64, 0:384] = brecv[2 * i]
        flat[64 * i : 64 * i + 64, 384:768] = brecv[2 * i + 1]
    hi, lo = halves(flat[...])
    out = dot_nt(jnp.concatenate([hi, lo, hi], axis=1), qcat[...])
    low = low_lanes((192, 128))
    zero = jnp.zeros((64, 128), F32)
    for n in range(4):
        o = out[:, 128 * n : 128 * n + 128]
        c, h = o[0:192], jnp.concatenate([o[192:256], zero, o[256:320]], axis=0)
        esend[n // 2, 2 * (n % 2)] = jnp.where(low, c, swap(h))
        esend[n // 2, 2 * (n % 2) + 1] = jnp.where(low, swap(c), h)


def term(recv, res, hit, fourr, kinr, liver, vz, hres, hsend, z, zl_):
    his, los = [], []
    for b in range(8):
        hi, lo = halves(jnp.concatenate([recv[pl.ds(256 * zl + b, 32, stride=8), :] for zl in range(3)], axis=0))
        his.append(hi)
        los.append(lo)
    hi = jnp.concatenate(his, axis=1)
    out = dot(vz[...], jnp.concatenate([hi, jnp.concatenate(los, axis=1), hi], axis=0))
    low = low_lanes((64, 128))
    for b in range(8):
        o = out[:, 128 * b : 128 * b + 128]
        other = swap(o[64:128])
        z[pl.ds(b, 64, stride=8), :] = o[0:64] + jnp.where(low, other, -other)
    zl_[...] = fours(z, low_lanes((8, 128)))
    for n in range(12):
        at = pl.ds(256 * n, 256)
        acc = pick(zl_[...], hit, fourr, n, 256)
        live = liver[:, at] > 0.0
        for c in range(2):
            v = kinr[:, at] * res[8 * c : 8 * c + 8, at] + acc[8 * c : 8 * c + 8] * (1.0 / float(L**3))
            v = jnp.where(live, v, 0.0)
            hres[c, :, at] = v
            for k in range(2):
                q = 2 * n + k
                hsend[q // 3, c, :, (q % 3) * 128 : (q % 3) * 128 + 128] = v[:, 128 * k : 128 * k + 128]


F0, F1 = 10, 22


def late_gram(hrecv, qcat, flat, lsend, start):
    flat[0:64, 0:384] = hrecv[0]
    flat[0:64, 384:768] = hrecv[1]
    hi, lo = halves(flat[0:64, :])
    cat = jnp.concatenate([hi, lo, hi], axis=1)
    low = low_lanes((32, 128))
    mine = lax.rem(lax.axis_index("band"), 2)
    for core in (1 - mine, mine):
        out = dot_nt(cat, qcat[pl.ds(pl.multiple_of(256 * core, 256), 256), :])
        for n in range(2):
            a, b = out[0:32, 128 * n : 128 * n + 128], out[32:64, 128 * n : 128 * n + 128]
            lsend[core, 2 * n] = jnp.where(low, a, swap(b))
            lsend[core, 2 * n + 1] = jnp.where(low, swap(a), b)
        if core is not mine:
            start()


def late_tiles(total, la, lb, fl):
    other = swap(total)
    la[8:40, :], la[40:72, :] = total, other
    lb[8:40, :], lb[40:72, :] = other, total
    low = low_lanes((3, 128))
    for i in range(F1 - F0):
        r = 8 + 6 * (F0 + i) - 64
        fl[8 * i : 8 * i + 3, :] = jnp.where(low, la[r : r + 3, :], lb[r + 3 : r + 6, :])


class LateExchange:
    def __init__(self, src, dst, ssem, rsem):
        self.a = (src, dst, ssem, rsem)
        self.f = lax.axis_index("fft")
        self.owner = jnp.logical_and(self.f >= F0, self.f < F1)

    def start(self):
        src, dst, ssem, rsem = self.a
        f, b = self.f, lax.axis_index("band")
        to_me = dst.at[pl.ds(pl.multiple_of(8 * f, 8), 4), :]
        for i in range(F1 - F0):
            n = lax.rem(f + i, F1 - F0)
            part = src.at[pl.ds(pl.multiple_of(8 * n, 8), 4), :]

            @pl.when(n + F0 != f)
            def _():
                pltpu.make_async_remote_copy(
                    src_ref=part, dst_ref=to_me, send_sem=ssem, recv_sem=rsem, device_id=(b, n + F0),
                    device_id_type=MESH).start()

        @pl.when(self.owner)
        def _():
            own = src.at[pl.ds(pl.multiple_of(8 * (f - F0), 8), 4), :]
            pltpu.make_async_copy(own, to_me, rsem).start()

    def add(self, out, scale):
        src, dst, ssem, rsem = self.a

        @pl.when(self.owner)
        def _():
            whole(dst.at[pl.ds(0, 4 * NF), :], rsem)
            total = dst[0:4, :]
            for d in range(1, NF):
                total = total + dst[8 * d : 8 * d + 4, :]
            total = total[0:3] * scale
            low = low_lanes((3, 128))
            out[0:3, :] = out[0:3, :] + jnp.where(low, 0.0, swap(total))
            out[3:6, :] = out[3:6, :] + jnp.where(low, 0.0, total)

    def sent(self):
        src, dst, ssem, rsem = self.a
        whole(src.at[pl.ds(0, 44), :], ssem)
        pl.when(jnp.logical_not(self.owner))(lambda: whole(src.at[pl.ds(0, 4), :], ssem))


def step_kernel(ev_h, cur_h, hcur_h, prev_h, hprev_h, gm_h, scols_h, pot_h, wz_h, wy_h, wx_h, vx_h, vy_h,
                vz_h, hres_h, out,
                ev, cur, hcur, prev, hprev, gm, scols, pot, wz, wy, wx, vx, vy, vz, hres,
                res, kinr, gfour, liver, ghit, glhs, y, send, bsend,
                recv, brecv, shit, smask, sfour, slhs, potp, pm, pm2, tt, gg, gl, send2, recv2,
                qs, qcat, flat, esum, esend, egot, emid, erecv, z, zl, hsend, hrecv, la, lb,
                lsend, lgot, lmid, lrecv, fl, lrow, fsend, frecv, s1, r1, s3, r3, s4, s6, sems, load):
    pairs = [(ev_h, ev), (gm_h, gm), (scols_h, scols), (cur_h, cur), (hcur_h, hcur), (wz_h, wz), (prev_h, prev), (hprev_h, hprev),
             (pot_h, pot), (wy_h, wy), (wx_h, wx), (vx_h, vx), (vy_h, vy), (vz_h, vz)]
    loads = [pltpu.make_async_copy(a, b, load.at[i]) for i, (a, b) in enumerate(pairs)]
    for copy in loads[:6]:
        copy.start()
    greet_everyone()
    for copy in loads[:6]:
        copy.wait()
    x1 = FftExchange(send, recv, s1, r1)
    x2 = BandExchange(bsend, brecv, band_rows, sems.at[0], sems.at[1])
    x3 = FftExchange(send2, recv2, s3, r3)
    x4 = BandSum(esend, egot, emid, erecv, s4)
    x5 = BandExchange(hsend, hrecv, band_rows, sems.at[4], sems.at[5])
    x6 = BandSum(lsend, lgot, lmid, lrecv, s6)
    x8 = LateExchange(fl, lrow, sems.at[6], sems.at[7])
    x7 = FftExchange(fsend, frecv, sems.at[pl.ds(8, 1)], sems.at[pl.ds(9, 1)])
    residual(ev, cur, hcur, gm, scols, res, glhs, ghit, kinr, gfour, liver)
    for copy in loads[6:]:
        copy.start()
    sticks(glhs, ghit, wz, send, y)
    everyone_in()
    x1.start(0)
    for copy in loads[6:]:
        copy.wait()
    basis_rows(cur, hcur, prev, hprev, res, liver, bsend)
    x1.start(1)
    plane_maps(scols, pot, shit, smask, sfour, potp)
    x1.start(2)
    x2.start()

    pms = (pm, pm2)
    x1.wait(0)
    place(0, recv, shit, smask, slhs, pms[0])
    for g in range(3):
        if g < 2:
            x1.wait(g + 1)
        along_y(pms[g % 2], wy, tt)
        if g < 2:
            place(g + 1, recv, shit, smask, slhs, pms[(g + 1) % 2])
        along_x(g, tt, potp, wx, vx, vy, gg)
        collect(g, gg, shit, sfour, gl, send2)
        x3.start(g)
    x2.wait()
    row_side(brecv, qs)
    early_gram(brecv, qs, qcat, flat, esend)
    x4.first()
    x4.second()
    for g in range(3):
        x3.wait(g)
    term(recv2, res, ghit, gfour, kinr, liver, vz, hres, hsend, z, zl)
    x5.start()
    store = pltpu.make_async_copy(hres, hres_h, load.at[15])
    store.start()
    esum[...] = x4.total()
    fsend[...] = jnp.zeros((256, 128), F32)
    for f in range(NF):
        fsend[8 * f : 8 * f + 6, :] = esum[6 * f : 6 * f + 6, :]
    x7.start()
    fl[...] = jnp.zeros((8 * (F1 - F0), 128), F32)
    la[...] = jnp.zeros((80, 128), F32)
    lb[...] = jnp.zeros((80, 128), F32)
    x5.wait()
    late_gram(hrecv, qcat, flat, lsend, x6.first)
    x6.second()
    x7.wait()
    total = frecv[0:8, :]
    for d in range(1, NF):
        total = total + frecv[8 * d : 8 * d + 8, :]
    scale = 8.0 / float(L**3)
    out[...] = total * scale
    late_tiles(x6.total(), la, lb, fl)
    x8.start()
    x8.add(out, scale)
    store.wait()
    for g in range(3):
        x1.sent(g)
        x3.sent(g)
    for x in (x2, x4, x5, x6, x7, x8):
        x.sent()


def sds(*shape):
    return jax.ShapeDtypeStruct(shape, F32)


DMA = pltpu.SemaphoreType.DMA
BIG = 64 * 1024 * 1024


def local(current, h_current, previous, h_previous, eigen_values, potential, stick_cols, g_map):
    w = tables()
    gm = g_map.reshape(1, 3072)
    sc = stick_cols.reshape(NF, 128)
    vm = lambda *shape: pltpu.VMEM(shape, F32)
    v16 = lambda *shape: pltpu.VMEM(shape, BF16)
    vi = lambda *shape: pltpu.VMEM(shape, jnp.int32)
    hres, tile = pl.pallas_call(
        step_kernel, out_shape=(sds(2, 8, 3072), sds(8, 128)), in_specs=[HB] * 14, out_specs=(HB, VM),
        scratch_shapes=[
            pltpu.SMEM((8,), F32), vm(2, 8, 3072), vm(2, 8, 3072), vm(2, 8, 3072), vm(2, 8, 3072), vi(1, 3072), vi(NF, 128), vm(3, L, L),
            v16(384, 192), v16(384, 256), v16(192, 336), v16(112, 576), v16(256, 256), v16(128, 288),
            vm(2, 8, 3072),
            vm(16, 3072), vm(8, 3072), vi(8, 3072), vm(8, 3072), v16(256, 3072), v16(416, 3072), vm(512, 128),
            vm(768, 128), vm(8, 10, 8, 384),
            vm(768, 128), vm(10, 64, 384), v16(256, 2048), v16(208, 2048), vi(8, 2048), v16(416, 2048),
            vm(3, L, 128), vm(416, 128), vm(416, 128), vm(2, 448, 128), vm(448, 128), v16(208, 512), vm(768, 128), vm(768, 128),
            vm(512, 768), v16(512, 2304), vm(320, 768), vm(192, 128), vm(2, 4, 192, 128), vm(4, 192, 128), vm(4, 192, 128),
            vm(4, 192, 128), vm(512, 128),
            v16(208, 512), vm(8, 2, 8, 384), vm(2, 64, 384), vm(80, 128), vm(80, 128), vm(2, 4, 32, 128), vm(4, 32, 128), vm(4, 32, 128),
            vm(4, 32, 128), vm(96, 128), vm(256, 128),
            vm(256, 128), vm(256, 128), DMA((3,)), DMA((3,)), DMA((3,)), DMA((3,)), DMA((4,)), DMA((4,)), DMA((10,)), DMA((16,))],
        compiler_params=pltpu.CompilerParams(collective_id=0, has_side_effects=True, vmem_limit_bytes=BIG), name="step",
    )(eigen_values, current, h_current, previous, h_previous, gm, sc, potential,
      w["wz"], w["wy"], w["wx"], w["vx"], w["vy"], w["vz"])
    mats = jnp.transpose(tile[0:6].reshape(6, 4, 32)[:, :, 0:24], (1, 2, 0))
    return hres, mats[0:2], mats[2:4]


def solution(mesh):
    bf = P(None, "band", "fft")
    in_specs = (bf, bf, bf, bf, P("band"), P("fft", None, None), P(), P("fft"))
    return jax.shard_map(local, mesh=mesh, in_specs=in_specs, out_specs=(bf, bf, bf), check_vma=False)
```

```python
import math

import jax
import jax.numpy as jnp
import ml_dtypes
import numpy as np
from jax import lax
from jax.experimental import pallas as pl
from jax.experimental.pallas import tpu as pltpu
from jax.sharding import PartitionSpec as P

L = 96
CUT = 24
F32 = jnp.float32
BF16 = jnp.bfloat16
NF = 32
NBD = 8
GT = 24
NT = 13
MESH = pl.DeviceIdType.MESH
VM = pl.BlockSpec(memory_space=pltpu.VMEM)
HB = pl.BlockSpec(memory_space=pltpu.HBM)
SM = pl.BlockSpec(memory_space=pltpu.SMEM)


def split_np(table):
    high = table.astype(ml_dtypes.bfloat16)
    low = (table - high.astype(np.float64)).astype(ml_dtypes.bfloat16)
    return high, low


def tables():
    zout = (np.arange(NF)[None, :] * 3 + np.arange(3)[:, None]).reshape(-1)
    wz = np.zeros((2, 2, L, 2, 32))
    for par in range(2):
        zi = 2 * np.arange(32) + par
        ok = zi <= 2 * CUT
        ang = 2 * math.pi / L * ((zout[:, None] * (zi - CUT)[None, :]) % L)
        c, s = np.cos(ang) * ok, np.sin(ang) * ok
        wz[par, 0, :, 0], wz[par, 0, :, 1] = c, -s
        wz[par, 1, :, 0], wz[par, 1, :, 1] = s, c
    zh, zl = split_np(wz.reshape(384, 64))
    wz = np.concatenate([zh, zh, zl], axis=1)
    n = np.arange(L)
    k = np.arange(49) - CUT
    ang = 2 * math.pi / L * ((k[:, None] * n[None, :]) % L)
    c, s = np.cos(ang), np.sin(ang)
    wy = np.zeros((2, 64, 2, 128))
    wy[0, :49, 0, :L], wy[0, :49, 1, :L] = c, s
    wy[1, :49, 0, :L], wy[1, :49, 1, :L] = -s, c
    yh, yl = split_np(wy.reshape(128, 256))
    wy = np.concatenate([yh, yh, yl], axis=0)
    wx = np.zeros((2, L, 2, 56))
    wx[0, :, 0, :49], wx[0, :, 1, :49] = c.T, -s.T
    wx[1, :, 0, :49], wx[1, :, 1, :49] = s.T, c.T
    xh, xl = split_np(wx.reshape(192, 112))
    wx = np.concatenate([xh, xh, xl], axis=1)
    vx = np.zeros((2, 56, 2, L))
    vx[0, :49, 0], vx[0, :49, 1] = c, s
    vx[1, :49, 0], vx[1, :49, 1] = -s, c
    vh, vl = split_np(vx.reshape(112, 192))
    vx = np.concatenate([vh, vh, vl], axis=1)
    vy = np.zeros((2, 128, 2, 64))
    vy[0, :L, 0, :49], vy[0, :L, 1, :49] = c.T, -s.T
    vy[1, :L, 0, :49], vy[1, :L, 1, :49] = s.T, c.T
    vyh, vyl = split_np(vy.reshape(256, 128))
    vy = np.concatenate([vyh, vyl], axis=1)
    vz = np.zeros((2, 64, L))
    ang = 2 * math.pi / L * ((k[:, None] * zout[None, :]) % L)
    vz[0, :49], vz[1, :49] = np.cos(ang), np.sin(ang)
    zbh, zbl = split_np(vz.reshape(128, L))
    vz = np.concatenate([zbh, zbh, zbl], axis=1)
    return dict(wz=wz, wy=wy, wx=wx, vx=vx, vy=vy, vz=vz)


def dot(a, b):
    return jnp.dot(a, b, preferred_element_type=F32)


def dot_nt(a, b):
    return lax.dot_general(a, b, (((1,), (1,)), ((), ())), preferred_element_type=F32)


def halves(x):
    hi = x.astype(BF16)
    return hi, (x - hi.astype(F32)).astype(BF16)


def low_lanes(shape):
    return lax.broadcasted_iota(jnp.int32, shape, len(shape) - 1) < 64


def swap(x):
    return pltpu.roll(x, 64, 1)


def div96(v):
    return (v * 43691) >> 22


def signed(v):
    return jnp.where(v >= L // 2, v - L, v)


def lanes_of(x, index):
    return jnp.take_along_axis(x, index, axis=1, mode="promise_in_bounds")


def slot_facts(m, cols):
    live = m >= 0
    ms = jnp.maximum(m, 0)
    slot = div96(ms)
    z = signed(ms - slot * L)
    col = jnp.where(live, lanes_of(cols, slot), 0)
    xc = div96(col)
    x = signed(xc)
    y = signed(col - xc * L)
    norm = x * x + y * y + z * z
    kin = jnp.where(live, 64.0 * norm.astype(F32) / float(L * L), 0.0)
    zi = z + CUT
    four = jnp.where(live, zi >> 2, -1)
    lane = jnp.where(live, (zi & 3) * 64 + slot - 64, -1)
    return live, kin, four, lane


def one_hot_rows(key, rows):
    return jnp.where(jnp.broadcast_to(key, (256, 128)) == rows, 1.0, 0.0).astype(BF16)


def four_masks(four):
    wide = jnp.broadcast_to(four, (16, 128))
    return [jnp.where(wide == t, 1.0, 0.0).astype(BF16) for t in range(NT)]


def residual(ev, cur, hcur, gm, scols, res, lhs, hit, kinr, fourr, liver):
    me = lax.axis_index("fft")
    cols = jnp.broadcast_to(scols[pl.ds(me, 1), :], (8, 128))
    row = lax.broadcasted_iota(jnp.int32, (8, 128), 0)
    evc = jnp.zeros((8, 128), F32)
    for b in range(8):
        evc = jnp.where(row == b, ev[b], evc)
    rows = lax.broadcasted_iota(jnp.int32, (256, 128), 0)

    for k in range(GT):
        at = pl.ds(128 * k, 128)
        live, kin, four, lane = slot_facts(jnp.broadcast_to(gm[:, at], (8, 128)), cols)
        kinr[:, at] = kin
        fourr[:, at] = four
        liver[:, at] = live.astype(F32)
        den = 1.0 + kin
        r = jnp.concatenate(
            [jnp.where(live, (hcur[c, :, at] - evc * cur[c, :, at]) / den, 0.0) for c in range(2)], axis=0)
        res[:, at] = r
        hi, lo = halves(r)
        hit[:, at] = one_hot_rows(lane[:1], rows)
        for t, m in enumerate(four_masks(four[:1])):
            lhs[32 * t : 32 * t + 16, at] = hi * m
            lhs[32 * t + 16 : 32 * t + 32, at] = lo * m


def sticks(lhs, hit, wz, send, y):
    out = dot_nt(lhs[...], hit[...])
    y[416:512, :] = jnp.zeros((96, 128), F32)
    for t in range(NT):
        o = out[32 * t : 32 * t + 16] + out[32 * t + 16 : 32 * t + 32]
        for h in range(2):
            y[32 * t + 16 * h : 32 * t + 16 * h + 16, :] = o[:, 128 * h : 128 * h + 128]
    low = low_lanes((192, 128))
    low96 = low_lanes((96, 128))
    parts = []
    for b in range(8):
        x = jnp.concatenate([y[pl.ds(c * 8 + b, 32, stride=16), :] for c in range(2)], axis=0)
        hi, lo = halves(x)
        parts.append(jnp.concatenate([hi, lo, hi], axis=0))
    out = dot(wz[...], jnp.concatenate(parts, axis=1))
    for b in range(8):
        o = out[:, 128 * b : 128 * b + 128]
        w = jnp.where(low, o[:192], o[192:])
        w = w + swap(w)
        w = jnp.where(low96, w[:96], w[96:])
        for zl in range(3):
            send[pl.ds(256 * zl + b, 32, stride=8), :] = w[32 * zl : 32 * zl + 32]


def basis_rows(cur, hcur, prev, hprev, res, liver, bsend):
    def tile(d, carry):
        at = pl.ds(pl.multiple_of(384 * d, 128), 384)
        live = liver[:, at] > 0.0
        for c in range(2):
            bsend[d, c] = jnp.where(live, cur[c, :, at], 0.0)
            bsend[d, 2 + c] = res[8 * c : 8 * c + 8, at]
            bsend[d, 4 + c] = jnp.where(live, prev[c, :, at], 0.0)
            bsend[d, 6 + c] = jnp.where(live, hcur[c, :, at], 0.0)
            bsend[d, 8 + c] = jnp.where(live, hprev[c, :, at], 0.0)
        return carry

    lax.fori_loop(0, NBD, tile, 0)


def greet_everyone():
    f, b = lax.axis_index("fft"), lax.axis_index("band")
    barrier = pltpu.get_barrier_semaphore()

    def greet(i, c):
        pl.semaphore_signal(barrier, inc=1, device_id=(b, lax.rem(f + i, NF)), device_id_type=MESH)
        return c

    def greet_b(i, c):
        pl.semaphore_signal(barrier, inc=1, device_id=(lax.rem(b + i, NBD), f), device_id_type=MESH)
        return c

    lax.fori_loop(1, NF, greet, 0)
    lax.fori_loop(1, NBD, greet_b, 0)


def everyone_in():
    pl.semaphore_wait(pltpu.get_barrier_semaphore(), NF - 1 + NBD - 1)


FAR_FIRST = sorted(
    [(dx, dz) for dx in range(4) for dz in range(8) if dx or dz], key=lambda o: -min(o[0], 4 - o[0]) - min(o[1], 8 - o[1]))


def whole(ref, sem):
    pltpu.make_async_copy(ref, ref, sem).wait()


class FftExchange:
    def __init__(self, src, dst, ssem, rsem):
        self.a = (src, dst, ssem, rsem)

    def start(self, g=0):
        src, dst, ssem, rsem = self.a
        f, b = lax.axis_index("fft"), lax.axis_index("band")
        to_me = dst.at[pl.ds(pl.multiple_of(256 * g + 8 * f, 8), 8), :]

        for dx, dz in FAR_FIRST:
            to = lax.rem(f // 8 + dx, 4) * 8 + lax.rem(f + dz, 8)
            pltpu.make_async_remote_copy(
                src_ref=src.at[pl.ds(pl.multiple_of(256 * g + 8 * to, 8), 8), :], dst_ref=to_me,
                send_sem=ssem.at[g], recv_sem=rsem.at[g], device_id=(b, to), device_id_type=MESH).start()
        own = src.at[pl.ds(pl.multiple_of(256 * g + 8 * f, 8), 8), :]
        pltpu.make_async_copy(own, to_me, rsem.at[g]).start()

    def wait(self, g=0):
        src, dst, ssem, rsem = self.a
        whole(dst.at[pl.ds(256 * g, 256), :], rsem.at[g])

    def sent(self, g=0):
        src, dst, ssem, rsem = self.a
        whole(src.at[pl.ds(256 * g, 248), :], ssem.at[g])


class BandExchange:
    def __init__(self, src, dst, place, ssem, rsem):
        self.a = (src, dst, place, ssem, rsem)

    def start(self):
        src, dst, place, ssem, rsem = self.a
        f, b = lax.axis_index("fft"), lax.axis_index("band")
        for i in range(1, NBD):
            to = lax.rem(b + i, NBD)
            pltpu.make_async_remote_copy(
                src_ref=src.at[to], dst_ref=place(dst, b), send_sem=ssem, recv_sem=rsem,
                device_id=(to, f), device_id_type=MESH).start()
        pltpu.make_async_copy(src.at[b], place(dst, b), rsem).start()

    def wait(self):
        src, dst, place, ssem, rsem = self.a
        whole(dst, rsem)

    def sent(self):
        src, dst, place, ssem, rsem = self.a
        whole(src.at[pl.ds(0, NBD - 1)], ssem)


class BandSum:
    def __init__(self, src, got, mid, dst, sems):
        self.a = (src, got, mid, dst, sems)
        b = lax.axis_index("band")
        self.y, self.c = b // 2, lax.rem(b, 2)

    def first(self):
        src, got, mid, dst, sems = self.a
        pltpu.make_async_remote_copy(
            src_ref=src.at[1 - self.c], dst_ref=got, send_sem=sems.at[0], recv_sem=sems.at[1],
            device_id=(2 * self.y + 1 - self.c, lax.axis_index("fft")), device_id_type=MESH).start()

    def second(self):
        src, got, mid, dst, sems = self.a
        whole(got, sems.at[1])
        mid[...] = src[self.c] + got[...]
        for i in (2, 1, 3):
            to = lax.rem(self.y + i, 4)
            pltpu.make_async_remote_copy(
                src_ref=mid.at[to], dst_ref=dst.at[self.y], send_sem=sems.at[2], recv_sem=sems.at[3],
                device_id=(2 * to + self.c, lax.axis_index("fft")), device_id_type=MESH).start()
        pltpu.make_async_copy(mid.at[self.y], dst.at[self.y], sems.at[3]).start()

    def total(self):
        src, got, mid, dst, sems = self.a
        whole(dst, sems.at[3])
        return (dst[0] + dst[1]) + (dst[2] + dst[3])

    def sent(self):
        src, got, mid, dst, sems = self.a
        whole(got, sems.at[0])
        whole(mid.at[pl.ds(0, 3)], sems.at[2])


class LateSum:
    def __init__(self, src, dst, sems):
        self.a = (src, dst, sems)

    def start(self, core, mine):
        src, dst, sems = self.a
        f, b = lax.axis_index("fft"), lax.axis_index("band")
        y = b // 2
        for i in (2, 1, 3, 0):
            to = lax.rem(y + i, 4)
            if mine and i == 0:
                pltpu.make_async_copy(src.at[core, to], dst.at[b], sems.at[1]).start()
            else:
                pltpu.make_async_remote_copy(
                    src_ref=src.at[core, to], dst_ref=dst.at[b], send_sem=sems.at[0], recv_sem=sems.at[1],
                    device_id=(2 * to + core, f), device_id_type=MESH).start()

    def total(self):
        src, dst, sems = self.a
        whole(dst, sems.at[1])
        return ((dst[0] + dst[1]) + (dst[2] + dst[3])) + ((dst[4] + dst[5]) + (dst[6] + dst[7]))

    def sent(self):
        src, dst, sems = self.a
        whole(dst.at[pl.ds(0, NBD - 1)], sems.at[0])


def band_rows(dst, frm):
    return dst.at[:, pl.ds(pl.multiple_of(frm * 8, 8), 8), :]


def plane_maps(scols, pot, hit, mask, fourr, potp):
    low1 = low_lanes((1, 128))
    rows = lax.broadcasted_iota(jnp.int32, (256, 128), 0)
    for k in range(16):
        col = jnp.where(low1, swap(scols[2 * k : 2 * k + 1, :]), scols[2 * k + 1 : 2 * k + 2, :])
        live = col >= 0
        colp = jnp.maximum(col, 0)
        xc = div96(colp)
        xi = signed(xc) + CUT
        yi = signed(colp - xc * L) + CUT
        four = jnp.where(live, xi >> 2, -1)
        at = pl.ds(128 * k, 128)
        fourr[:, at] = jnp.broadcast_to(four, (8, 128))
        hit[:, at] = one_hot_rows(jnp.where(live, (xi & 3) * 64 + yi, -1), rows)
        for t, m in enumerate(four_masks(four)):
            mask[16 * t : 16 * t + 16, at] = m
    potp[...] = jnp.zeros((3, L, 128), F32)
    potp[:, :, 0:L] = pot[...]


def place(g, recv, hit, mask, lhs, pm):
    low = low_lanes((8, 128))
    for k in range(16):
        at = pl.ds(128 * k, 128)
        base = 256 * g + 16 * k
        r0, r1 = recv[pl.ds(base, 8), :], recv[pl.ds(base + 8, 8), :]
        hi, lo = halves(jnp.concatenate([jnp.where(low, r0, swap(r1)), jnp.where(low, swap(r0), r1)], axis=0))
        for t in range(NT):
            m = mask[16 * t : 16 * t + 16, at]
            lhs[32 * t : 32 * t + 16, at] = hi * m
            lhs[32 * t + 16 : 32 * t + 32, at] = lo * m
    out = dot_nt(lhs[...], hit[...])
    for t in range(NT):
        o = out[32 * t : 32 * t + 16] + out[32 * t + 16 : 32 * t + 32]
        for h in range(2):
            re, im = o[:8, 128 * h : 128 * h + 128], o[8:, 128 * h : 128 * h + 128]
            base = 32 * t + 16 * h
            pm[base : base + 8, :] = jnp.where(low, re, swap(im))
            pm[base + 8 : base + 16, :] = jnp.where(low, swap(re), im)


def along_y(pm, wy, tt):
    hi, lo = halves(pm[0:416, :])
    out = dot(jnp.concatenate([hi, lo], axis=1), wy[0:256, :]) + dot(hi, wy[256:384, :])
    tt[0, 0:416, :] = out[:, 0:128]
    tt[1, 0:416, :] = out[:, 128:256]
    tt[:, 416:448, :] = jnp.zeros((2, 32, 128), F32)


def along_x(g, tt, potp, wx, vx, vy, gg):
    pv = potp[g]
    pv = jnp.concatenate([pv] * 8, axis=1)
    pv = jnp.concatenate([pv, pv], axis=0)
    his, los = [], []
    for b in range(8):
        hi, lo = halves(jnp.concatenate([tt[c, pl.ds(b, 56, stride=8), :] for c in range(2)], axis=0))
        his.append(hi)
        los.append(lo)
    hi = jnp.concatenate(his, axis=1)
    u = dot(wx[...], jnp.concatenate([hi, jnp.concatenate(los, axis=1), hi], axis=0))
    hi, lo = halves(u * pv)
    t = dot(vx[...], jnp.concatenate([hi, lo, hi], axis=0))
    hi, lo = halves(jnp.concatenate(
        [jnp.concatenate([t[56 * c : 56 * c + 56, 128 * b : 128 * b + 128] for c in range(2)], axis=1) for b in range(8)],
        axis=0))
    a = dot(hi, vy[...])
    q = a[:, 0:128] + a[:, 128:256] + dot(lo, vy[:, 0:128])
    for b in range(8):
        gg[pl.ds(b, 56, stride=8), :] = q[56 * b : 56 * b + 56]


def fours(src, low):
    blocks = []
    for t in range(NT):
        cols = []
        for h in range(2):
            base = 32 * t + 16 * h
            g0, g1 = src[base : base + 8, :], src[base + 8 : base + 16, :]
            cols.append(jnp.concatenate([jnp.where(low, g0, swap(g1)), jnp.where(low, swap(g0), g1)], axis=0))
        blocks.append(jnp.concatenate(cols, axis=1))
    hi, lo = halves(jnp.concatenate(blocks, axis=0))
    return jnp.concatenate([hi, lo], axis=1)


def pick(lhs, hit, fourr, n, width):
    at = pl.ds(n * width, width)
    d = hit[:, at]
    out = dot(lhs, jnp.concatenate([d, d], axis=0))
    f = fourr[:, at]
    f = jnp.concatenate([f, f], axis=0)
    acc = jnp.zeros((16, width), F32)
    for t in range(NT):
        acc = jnp.where(f == t, out[16 * t : 16 * t + 16], acc)
    return acc


def collect(g, gg, hit, fourr, gl, send):
    low = low_lanes((8, 128))
    gl[...] = fours(gg, low)
    for n in range(8):
        acc = pick(gl[...], hit, fourr, n, 256)
        for k in range(2):
            re, im = acc[0:8, 128 * k : 128 * k + 128], acc[8:16, 128 * k : 128 * k + 128]
            base = 256 * g + 32 * n + 16 * k
            send[pl.ds(base, 8), :] = jnp.where(low, re, swap(im))
            send[pl.ds(base + 8, 8), :] = jnp.where(low, swap(re), im)


def row_side(brecv, qs):
    zero = jnp.zeros((8, 768), F32)
    for d in range(NBD):
        for j in range(3):
            g8 = 3 * d + j
            ty, r0 = g8 // 8, (g8 % 8) * 8
            re, im = brecv[2 * ty, r0 : r0 + 8, :], brecv[2 * ty + 1, r0 : r0 + 8, :]
            o = 64 * (4 * (d % 2) + d // 2) + 8 * j
            qs[o : o + 8, 0:384] = re
            qs[o : o + 8, 384:768] = im
            qs[o + 32 : o + 40, 0:384] = -im
            qs[o + 32 : o + 40, 384:768] = re
        qs[64 * d + 24 : 64 * d + 32, :] = zero
        qs[64 * d + 56 : 64 * d + 64, :] = zero


def early_gram(brecv, qs, qcat, flat, esend):
    hi, lo = halves(qs[...])
    qcat[...] = jnp.concatenate([hi, hi, lo], axis=1)
    for i in range(5):
        flat[64 * i : 64 * i + 64, 0:384] = brecv[2 * i]
        flat[64 * i : 64 * i + 64, 384:768] = brecv[2 * i + 1]
    hi, lo = halves(flat[...])
    out = dot_nt(jnp.concatenate([hi, lo, hi], axis=1), qcat[...])
    low = low_lanes((192, 128))
    zero = jnp.zeros((64, 128), F32)
    for n in range(4):
        o = out[:, 128 * n : 128 * n + 128]
        c, h = o[0:192], jnp.concatenate([o[192:256], zero, o[256:320]], axis=0)
        esend[n // 2, 2 * (n % 2)] = jnp.where(low, c, swap(h))
        esend[n // 2, 2 * (n % 2) + 1] = jnp.where(low, swap(c), h)


def term(recv, res, hit, fourr, kinr, liver, vz, hres, hsend, z, zl_):
    his, los = [], []
    for b in range(8):
        hi, lo = halves(jnp.concatenate([recv[pl.ds(256 * zl + b, 32, stride=8), :] for zl in range(3)], axis=0))
        his.append(hi)
        los.append(lo)
    hi = jnp.concatenate(his, axis=1)
    out = dot(vz[...], jnp.concatenate([hi, jnp.concatenate(los, axis=1), hi], axis=0))
    low = low_lanes((64, 128))
    for b in range(8):
        o = out[:, 128 * b : 128 * b + 128]
        other = swap(o[64:128])
        z[pl.ds(b, 64, stride=8), :] = o[0:64] + jnp.where(low, other, -other)
    zl_[...] = fours(z, low_lanes((8, 128)))
    for n in range(12):
        at = pl.ds(256 * n, 256)
        acc = pick(zl_[...], hit, fourr, n, 256)
        live = liver[:, at] > 0.0
        for c in range(2):
            v = kinr[:, at] * res[8 * c : 8 * c + 8, at] + acc[8 * c : 8 * c + 8] * (1.0 / float(L**3))
            v = jnp.where(live, v, 0.0)
            hres[c, :, at] = v
            for k in range(2):
                q = 2 * n + k
                hsend[q // 3, c, :, (q % 3) * 128 : (q % 3) * 128 + 128] = v[:, 128 * k : 128 * k + 128]


F0, F1 = 10, 22


def late_gram(hrecv, qcat, flat, lsend, start):
    flat[0:64, 0:384] = hrecv[0]
    flat[0:64, 384:768] = hrecv[1]
    hi, lo = halves(flat[0:64, :])
    cat = jnp.concatenate([hi, lo, hi], axis=1)
    low = low_lanes((32, 128))
    mine = lax.rem(lax.axis_index("band"), 2)
    for core in (1 - mine, mine):
        out = dot_nt(cat, qcat[pl.ds(pl.multiple_of(256 * core, 256), 256), :])
        for n in range(2):
            a, b = out[0:32, 128 * n : 128 * n + 128], out[32:64, 128 * n : 128 * n + 128]
            lsend[core, 2 * n] = jnp.where(low, a, swap(b))
            lsend[core, 2 * n + 1] = jnp.where(low, swap(a), b)
        start(core, core is mine)


def late_tiles(total, la, lb, fl):
    other = swap(total)
    la[8:40, :], la[40:72, :] = total, other
    lb[8:40, :], lb[40:72, :] = other, total
    low = low_lanes((3, 128))
    for i in range(F1 - F0):
        r = 8 + 6 * (F0 + i) - 64
        fl[8 * i : 8 * i + 3, :] = jnp.where(low, la[r : r + 3, :], lb[r + 3 : r + 6, :])


class LateExchange:
    def __init__(self, src, dst, ssem, rsem):
        self.a = (src, dst, ssem, rsem)
        self.f = lax.axis_index("fft")
        self.owner = jnp.logical_and(self.f >= F0, self.f < F1)

    def start(self):
        src, dst, ssem, rsem = self.a
        f, b = self.f, lax.axis_index("band")
        to_me = dst.at[pl.ds(pl.multiple_of(8 * f, 8), 4), :]
        for i in range(F1 - F0):
            n = lax.rem(f + i, F1 - F0)
            part = src.at[pl.ds(pl.multiple_of(8 * n, 8), 4), :]

            @pl.when(n + F0 != f)
            def _():
                pltpu.make_async_remote_copy(
                    src_ref=part, dst_ref=to_me, send_sem=ssem, recv_sem=rsem, device_id=(b, n + F0),
                    device_id_type=MESH).start()

        @pl.when(self.owner)
        def _():
            own = src.at[pl.ds(pl.multiple_of(8 * (f - F0), 8), 4), :]
            pltpu.make_async_copy(own, to_me, rsem).start()

    def add(self, out, scale):
        src, dst, ssem, rsem = self.a

        @pl.when(self.owner)
        def _():
            whole(dst.at[pl.ds(0, 4 * NF), :], rsem)
            total = dst[0:4, :]
            for d in range(1, NF):
                total = total + dst[8 * d : 8 * d + 4, :]
            total = total * scale
            both = jnp.concatenate([swap(total)[0:3], total[0:3], jnp.zeros((2, 128), F32)], axis=0)
            out[...] = out[...] + jnp.where(low_lanes((8, 128)), 0.0, both)

    def sent(self):
        src, dst, ssem, rsem = self.a
        whole(src.at[pl.ds(0, 44), :], ssem)
        pl.when(jnp.logical_not(self.owner))(lambda: whole(src.at[pl.ds(0, 4), :], ssem))


def step_kernel(ev_h, cur_h, hcur_h, prev_h, hprev_h, gm_h, scols_h, pot_h, wz_h, wy_h, wx_h, vx_h, vy_h,
                vz_h, hres_h, out,
                ev, cur, hcur, prev, hprev, gm, scols, pot, wz, wy, wx, vx, vy, vz, hres,
                res, kinr, gfour, liver, ghit, glhs, y, send, bsend,
                recv, brecv, shit, smask, sfour, slhs, potp, pm, pm2, tt, gg, gl, send2, recv2,
                qs, qcat, flat, esum, esend, egot, emid, erecv, z, zl, hsend, hrecv, la, lb,
                lsend, lrecv, fl, lrow, fsend, frecv, s1, r1, s3, r3, s4, s6, sems, load):
    pairs = [(ev_h, ev), (gm_h, gm), (scols_h, scols.at[pl.ds(0, NF), :]), (cur_h, cur), (hcur_h, hcur), (wz_h, wz), (prev_h, prev), (hprev_h, hprev),
             (pot_h, pot), (wy_h, wy), (wx_h, wx), (vx_h, vx), (vy_h, vy), (vz_h, vz)]
    loads = [pltpu.make_async_copy(a, b, load.at[i]) for i, (a, b) in enumerate(pairs)]
    for copy in loads[:6]:
        copy.start()
    greet_everyone()
    for copy in loads[:6]:
        copy.wait()
    x1 = FftExchange(send, recv, s1, r1)
    x2 = BandExchange(bsend, brecv, band_rows, sems.at[0], sems.at[1])
    x3 = FftExchange(send2, recv2, s3, r3)
    x4 = BandSum(esend, egot, emid, erecv, s4)
    x5 = BandExchange(hsend, hrecv, band_rows, sems.at[4], sems.at[5])
    x6 = LateSum(lsend, lrecv, s6)
    x8 = LateExchange(fl, lrow, sems.at[6], sems.at[7])
    x7 = FftExchange(fsend, frecv, sems.at[pl.ds(8, 1)], sems.at[pl.ds(9, 1)])
    residual(ev, cur, hcur, gm, scols, res, glhs, ghit, kinr, gfour, liver)
    for copy in loads[6:]:
        copy.start()
    sticks(glhs, ghit, wz, send, y)
    everyone_in()
    x1.start(0)
    for copy in loads[6:]:
        copy.wait()
    basis_rows(cur, hcur, prev, hprev, res, liver, bsend)
    x1.start(1)
    plane_maps(scols, pot, shit, smask, sfour, potp)
    x1.start(2)
    x2.start()

    pms = (pm, pm2)
    x1.wait(0)
    place(0, recv, shit, smask, slhs, pms[0])
    for g in range(3):
        if g < 2:
            x1.wait(g + 1)
        along_y(pms[g % 2], wy, tt)
        if g < 2:
            place(g + 1, recv, shit, smask, slhs, pms[(g + 1) % 2])
        along_x(g, tt, potp, wx, vx, vy, gg)
        collect(g, gg, shit, sfour, gl, send2)
        x3.start(g)
    x2.wait()
    row_side(brecv, qs)
    early_gram(brecv, qs, qcat, flat, esend)
    x4.first()
    x4.second()
    for g in range(3):
        x3.wait(g)
    term(recv2, res, ghit, gfour, kinr, liver, vz, hres, hsend, z, zl)
    x5.start()
    store = pltpu.make_async_copy(hres, hres_h, load.at[15])
    store.start()
    esum[0:192, :] = x4.total()
    fsend[...] = jnp.zeros((256, 128), F32)
    for f in range(NF):
        fsend[8 * f : 8 * f + 6, :] = esum[6 * f : 6 * f + 6, :]
    x7.start()
    fl[...] = jnp.zeros((8 * (F1 - F0), 128), F32)
    la[...] = jnp.zeros((88, 128), F32)
    lb[...] = jnp.zeros((88, 128), F32)
    x5.wait()
    late_gram(hrecv, qcat, flat, lsend, x6.start)
    x7.wait()
    total = frecv[0:8, :]
    for d in range(1, NF):
        total = total + frecv[8 * d : 8 * d + 8, :]
    scale = 8.0 / float(L**3)
    out[...] = total * scale
    late_tiles(x6.total(), la, lb, fl)
    x8.start()
    x8.add(out, scale)
    store.wait()
    for g in range(3):
        x1.sent(g)
        x3.sent(g)
    for x in (x2, x4, x5, x6, x7, x8):
        x.sent()


def sds(*shape):
    return jax.ShapeDtypeStruct(shape, F32)


DMA = pltpu.SemaphoreType.DMA
BIG = 64 * 1024 * 1024


def local(current, h_current, previous, h_previous, eigen_values, potential, stick_cols, g_map):
    w = tables()
    gm = g_map.reshape(1, 3072)
    sc = stick_cols.reshape(NF, 128)
    vm = lambda *shape: pltpu.VMEM(shape, F32)
    v16 = lambda *shape: pltpu.VMEM(shape, BF16)
    vi = lambda *shape: pltpu.VMEM(shape, jnp.int32)
    hres, tile = pl.pallas_call(
        step_kernel, out_shape=(sds(2, 8, 3072), sds(8, 128)), in_specs=[HB] * 14, out_specs=(HB, VM),
        scratch_shapes=[
            pltpu.SMEM((8,), F32), vm(2, 8, 3072), vm(2, 8, 3072), vm(2, 8, 3072), vm(2, 8, 3072), vi(1, 3072), vi(NF + 8, 128), vm(3, L, L),
            v16(384, 192), v16(384, 256), v16(192, 336), v16(112, 576), v16(256, 256), v16(128, 288),
            vm(2, 8, 3072),
            vm(16, 3072), vm(8, 3072), vi(8, 3072), vm(8, 3072), v16(256, 3072), v16(416, 3072), vm(512, 128),
            vm(768, 128), vm(8, 10, 8, 384),
            vm(768, 128), vm(10, 64, 384), v16(256, 2048), v16(208, 2048), vi(8, 2048), v16(416, 2048),
            vm(3, L, 128), vm(416, 128), vm(416, 128), vm(2, 448, 128), vm(448, 128), v16(208, 512), vm(768, 128), vm(768, 128),
            vm(512, 768), v16(512, 2304), vm(320, 768), vm(200, 128), vm(2, 4, 192, 128), vm(4, 192, 128), vm(4, 192, 128),
            vm(4, 192, 128), vm(512, 128),
            v16(208, 512), vm(8, 2, 8, 384), vm(2, 64, 384), vm(88, 128), vm(88, 128), vm(2, 4, 32, 128), vm(8, 32, 128), vm(96, 128), vm(256, 128),
            vm(256, 128), vm(256, 128), DMA((3,)), DMA((3,)), DMA((3,)), DMA((3,)), DMA((4,)), DMA((4,)), DMA((10,)), DMA((16,))],
        compiler_params=pltpu.CompilerParams(collective_id=0, has_side_effects=True, vmem_limit_bytes=BIG), name="step",
    )(eigen_values, current, h_current, previous, h_previous, gm, sc, potential,
      w["wz"], w["wy"], w["wx"], w["vx"], w["vy"], w["vz"])
    mats = jnp.transpose(tile[0:6].reshape(6, 4, 32)[:, :, 0:24], (1, 2, 0))
    return hres, mats[0:2], mats[2:4]


def solution(mesh):
    bf = P(None, "band", "fft")
    in_specs = (bf, bf, bf, bf, P("band"), P("fft", None, None), P(), P("fft"))
    return jax.shard_map(local, mesh=mesh, in_specs=in_specs, out_specs=(bf, bf, bf), check_vma=False)
```

```python
import math

import jax
import jax.numpy as jnp
import ml_dtypes
import numpy as np
from jax import lax
from jax.experimental import pallas as pl
from jax.experimental.pallas import tpu as pltpu
from jax.sharding import PartitionSpec as P

L = 96
CUT = 24
F32 = jnp.float32
BF16 = jnp.bfloat16
NF = 32
NBD = 8
GT = 24
NT = 13
MESH = pl.DeviceIdType.MESH
VM = pl.BlockSpec(memory_space=pltpu.VMEM)
HB = pl.BlockSpec(memory_space=pltpu.HBM)
SM = pl.BlockSpec(memory_space=pltpu.SMEM)


def split_np(table):
    high = table.astype(ml_dtypes.bfloat16)
    low = (table - high.astype(np.float64)).astype(ml_dtypes.bfloat16)
    return high, low


def tables():
    zout = (np.arange(NF)[None, :] * 3 + np.arange(3)[:, None]).reshape(-1)
    wz = np.zeros((2, 2, L, 2, 32))
    for par in range(2):
        zi = 2 * np.arange(32) + par
        ok = zi <= 2 * CUT
        ang = 2 * math.pi / L * ((zout[:, None] * (zi - CUT)[None, :]) % L)
        c, s = np.cos(ang) * ok, np.sin(ang) * ok
        wz[par, 0, :, 0], wz[par, 0, :, 1] = c, -s
        wz[par, 1, :, 0], wz[par, 1, :, 1] = s, c
    zh, zl = split_np(wz.reshape(384, 64))
    wz = np.concatenate([zh, zh, zl], axis=1)
    n = np.arange(L)
    k = np.arange(49) - CUT
    ang = 2 * math.pi / L * ((k[:, None] * n[None, :]) % L)
    c, s = np.cos(ang), np.sin(ang)
    wy = np.zeros((2, 64, 2, 128))
    wy[0, :49, 0, :L], wy[0, :49, 1, :L] = c, s
    wy[1, :49, 0, :L], wy[1, :49, 1, :L] = -s, c
    yh, yl = split_np(wy.reshape(128, 256))
    wy = np.concatenate([yh, yh, yl], axis=0)
    wx = np.zeros((2, L, 2, 56))
    wx[0, :, 0, :49], wx[0, :, 1, :49] = c.T, -s.T
    wx[1, :, 0, :49], wx[1, :, 1, :49] = s.T, c.T
    xh, xl = split_np(wx.reshape(192, 112))
    wx = np.concatenate([xh, xh, xl], axis=1)
    vx = np.zeros((2, 56, 2, L))
    vx[0, :49, 0], vx[0, :49, 1] = c, s
    vx[1, :49, 0], vx[1, :49, 1] = -s, c
    vh, vl = split_np(vx.reshape(112, 192))
    vx = np.concatenate([vh, vh, vl], axis=1)
    vy = np.zeros((2, 128, 2, 64))
    vy[0, :L, 0, :49], vy[0, :L, 1, :49] = c.T, -s.T
    vy[1, :L, 0, :49], vy[1, :L, 1, :49] = s.T, c.T
    vyh, vyl = split_np(vy.reshape(256, 128))
    vy = np.concatenate([vyh, vyl], axis=1)
    vz = np.zeros((2, 64, L))
    ang = 2 * math.pi / L * ((k[:, None] * zout[None, :]) % L)
    vz[0, :49], vz[1, :49] = np.cos(ang), np.sin(ang)
    zbh, zbl = split_np(vz.reshape(128, L))
    vz = np.concatenate([zbh, zbh, zbl], axis=1)
    return dict(wz=wz, wy=wy, wx=wx, vx=vx, vy=vy, vz=vz)


def dot(a, b):
    return jnp.dot(a, b, preferred_element_type=F32)


def dot_nt(a, b):
    return lax.dot_general(a, b, (((1,), (1,)), ((), ())), preferred_element_type=F32)


def halves(x):
    hi = x.astype(BF16)
    return hi, (x - hi.astype(F32)).astype(BF16)


def low_lanes(shape):
    return lax.broadcasted_iota(jnp.int32, shape, len(shape) - 1) < 64


def swap(x):
    return pltpu.roll(x, 64, 1)


def div96(v):
    return (v * 43691) >> 22


def signed(v):
    return jnp.where(v >= L // 2, v - L, v)


def lanes_of(x, index):
    return jnp.take_along_axis(x, index, axis=1, mode="promise_in_bounds")


def slot_facts(m, cols):
    live = m >= 0
    ms = jnp.maximum(m, 0)
    slot = div96(ms)
    z = signed(ms - slot * L)
    col = jnp.where(live, lanes_of(cols, slot), 0)
    xc = div96(col)
    x = signed(xc)
    y = signed(col - xc * L)
    norm = x * x + y * y + z * z
    kin = jnp.where(live, 64.0 * norm.astype(F32) / float(L * L), 0.0)
    zi = z + CUT
    four = jnp.where(live, zi >> 2, -1)
    lane = jnp.where(live, (zi & 3) * 64 + slot - 64, -1)
    return live, kin, four, lane


def one_hot_rows(key, rows):
    return jnp.where(jnp.broadcast_to(key, (256, 128)) == rows, 1.0, 0.0).astype(BF16)


def four_masks(four):
    wide = jnp.broadcast_to(four, (16, 128))
    return [jnp.where(wide == t, 1.0, 0.0).astype(BF16) for t in range(NT)]


def residual(ev, cur, hcur, gm, scols, res, lhs, hit, kinr, fourr, liver):
    me = lax.axis_index("fft")
    cols = jnp.broadcast_to(scols[pl.ds(me, 1), :], (8, 128))
    row = lax.broadcasted_iota(jnp.int32, (8, 128), 0)
    evc = jnp.zeros((8, 128), F32)
    for b in range(8):
        evc = jnp.where(row == b, ev[b], evc)
    rows = lax.broadcasted_iota(jnp.int32, (256, 128), 0)

    for k in range(GT):
        at = pl.ds(128 * k, 128)
        live, kin, four, lane = slot_facts(jnp.broadcast_to(gm[:, at], (8, 128)), cols)
        kinr[:, at] = kin
        fourr[:, at] = four
        liver[:, at] = live.astype(F32)
        den = 1.0 + kin
        r = jnp.concatenate(
            [jnp.where(live, (hcur[c, :, at] - evc * cur[c, :, at]) / den, 0.0) for c in range(2)], axis=0)
        res[:, at] = r
        hi, lo = halves(r)
        hit[:, at] = one_hot_rows(lane[:1], rows)
        for t, m in enumerate(four_masks(four[:1])):
            lhs[32 * t : 32 * t + 16, at] = hi * m
            lhs[32 * t + 16 : 32 * t + 32, at] = lo * m


def sticks(lhs, hit, wz, send, y):
    out = dot_nt(lhs[...], hit[...])
    y[416:512, :] = jnp.zeros((96, 128), F32)
    for t in range(NT):
        o = out[32 * t : 32 * t + 16] + out[32 * t + 16 : 32 * t + 32]
        for h in range(2):
            y[32 * t + 16 * h : 32 * t + 16 * h + 16, :] = o[:, 128 * h : 128 * h + 128]
    low = low_lanes((192, 128))
    low96 = low_lanes((96, 128))
    parts = []
    for b in range(8):
        x = jnp.concatenate([y[pl.ds(c * 8 + b, 32, stride=16), :] for c in range(2)], axis=0)
        hi, lo = halves(x)
        parts.append(jnp.concatenate([hi, lo, hi], axis=0))
    out = dot(wz[...], jnp.concatenate(parts, axis=1))
    for b in range(8):
        o = out[:, 128 * b : 128 * b + 128]
        w = jnp.where(low, o[:192], o[192:])
        w = w + swap(w)
        w = jnp.where(low96, w[:96], w[96:])
        for zl in range(3):
            send[pl.ds(256 * zl + b, 32, stride=8), :] = w[32 * zl : 32 * zl + 32]


def basis_rows(cur, hcur, prev, hprev, res, liver, bsend):
    def tile(d, carry):
        at = pl.ds(pl.multiple_of(384 * d, 128), 384)
        live = liver[:, at] > 0.0
        for c in range(2):
            bsend[d, c] = jnp.where(live, cur[c, :, at], 0.0)
            bsend[d, 2 + c] = res[8 * c : 8 * c + 8, at]
            bsend[d, 4 + c] = jnp.where(live, prev[c, :, at], 0.0)
            bsend[d, 6 + c] = jnp.where(live, hcur[c, :, at], 0.0)
            bsend[d, 8 + c] = jnp.where(live, hprev[c, :, at], 0.0)
        return carry

    lax.fori_loop(0, NBD, tile, 0)


def greet_everyone():
    f, b = lax.axis_index("fft"), lax.axis_index("band")
    barrier = pltpu.get_barrier_semaphore()

    def greet(i, c):
        pl.semaphore_signal(barrier, inc=1, device_id=(b, lax.rem(f + i, NF)), device_id_type=MESH)
        return c

    def greet_b(i, c):
        pl.semaphore_signal(barrier, inc=1, device_id=(lax.rem(b + i, NBD), f), device_id_type=MESH)
        return c

    lax.fori_loop(1, NF, greet, 0)
    lax.fori_loop(1, NBD, greet_b, 0)


def everyone_in():
    pl.semaphore_wait(pltpu.get_barrier_semaphore(), NF - 1 + NBD - 1)


FAR_FIRST = sorted(
    [(dx, dz) for dx in range(4) for dz in range(8) if dx or dz], key=lambda o: -min(o[0], 4 - o[0]) - min(o[1], 8 - o[1]))


def whole(ref, sem):
    pltpu.make_async_copy(ref, ref, sem).wait()


class FftExchange:
    def __init__(self, src, dst, ssem, rsem):
        self.a = (src, dst, ssem, rsem)

    def start(self, g=0):
        src, dst, ssem, rsem = self.a
        f, b = lax.axis_index("fft"), lax.axis_index("band")
        to_me = dst.at[pl.ds(pl.multiple_of(256 * g + 8 * f, 8), 8), :]

        for dx, dz in FAR_FIRST:
            to = lax.rem(f // 8 + dx, 4) * 8 + lax.rem(f + dz, 8)
            pltpu.make_async_remote_copy(
                src_ref=src.at[pl.ds(pl.multiple_of(256 * g + 8 * to, 8), 8), :], dst_ref=to_me,
                send_sem=ssem.at[g], recv_sem=rsem.at[g], device_id=(b, to), device_id_type=MESH).start()
        own = src.at[pl.ds(pl.multiple_of(256 * g + 8 * f, 8), 8), :]
        pltpu.make_async_copy(own, to_me, rsem.at[g]).start()

    def wait(self, g=0):
        src, dst, ssem, rsem = self.a
        whole(dst.at[pl.ds(256 * g, 256), :], rsem.at[g])

    def sent(self, g=0):
        src, dst, ssem, rsem = self.a
        whole(src.at[pl.ds(256 * g, 248), :], ssem.at[g])


class BandExchange:
    def __init__(self, src, dst, place, ssem, rsem):
        self.a = (src, dst, place, ssem, rsem)

    def start(self):
        src, dst, place, ssem, rsem = self.a
        f, b = lax.axis_index("fft"), lax.axis_index("band")
        for i in range(1, NBD):
            to = lax.rem(b + i, NBD)
            pltpu.make_async_remote_copy(
                src_ref=src.at[to], dst_ref=place(dst, b), send_sem=ssem, recv_sem=rsem,
                device_id=(to, f), device_id_type=MESH).start()
        pltpu.make_async_copy(src.at[b], place(dst, b), rsem).start()

    def wait(self):
        src, dst, place, ssem, rsem = self.a
        whole(dst, rsem)

    def sent(self):
        src, dst, place, ssem, rsem = self.a
        whole(src.at[pl.ds(0, NBD - 1)], ssem)


class BandSum:
    def __init__(self, src, got, mid, dst, sems):
        self.a = (src, got, mid, dst, sems)
        b = lax.axis_index("band")
        self.y, self.c = b // 2, lax.rem(b, 2)

    def first(self):
        src, got, mid, dst, sems = self.a
        pltpu.make_async_remote_copy(
            src_ref=src.at[1 - self.c], dst_ref=got, send_sem=sems.at[0], recv_sem=sems.at[1],
            device_id=(2 * self.y + 1 - self.c, lax.axis_index("fft")), device_id_type=MESH).start()

    def second(self):
        src, got, mid, dst, sems = self.a
        whole(got, sems.at[1])
        mid[...] = src[self.c] + got[...]
        for i in (2, 1, 3):
            to = lax.rem(self.y + i, 4)
            pltpu.make_async_remote_copy(
                src_ref=mid.at[to], dst_ref=dst.at[self.y], send_sem=sems.at[2], recv_sem=sems.at[3],
                device_id=(2 * to + self.c, lax.axis_index("fft")), device_id_type=MESH).start()
        pltpu.make_async_copy(mid.at[self.y], dst.at[self.y], sems.at[3]).start()

    def total(self):
        src, got, mid, dst, sems = self.a
        whole(dst, sems.at[3])
        return (dst[0] + dst[1]) + (dst[2] + dst[3])

    def sent(self):
        src, got, mid, dst, sems = self.a
        whole(got, sems.at[0])
        whole(mid.at[pl.ds(0, 3)], sems.at[2])


class LateSum:
    def __init__(self, src, dst, sems):
        self.a = (src, dst, sems)

    def start(self, core, mine):
        src, dst, sems = self.a
        f, b = lax.axis_index("fft"), lax.axis_index("band")
        y = b // 2
        for i in (2, 1, 3, 0):
            to = lax.rem(y + i, 4)
            if mine and i == 0:
                pltpu.make_async_copy(src.at[core, to], dst.at[b], sems.at[1]).start()
            else:
                pltpu.make_async_remote_copy(
                    src_ref=src.at[core, to], dst_ref=dst.at[b], send_sem=sems.at[0], recv_sem=sems.at[1],
                    device_id=(2 * to + core, f), device_id_type=MESH).start()

    def total(self):
        src, dst, sems = self.a
        whole(dst, sems.at[1])
        return ((dst[0] + dst[1]) + (dst[2] + dst[3])) + ((dst[4] + dst[5]) + (dst[6] + dst[7]))

    def sent(self):
        src, dst, sems = self.a
        whole(dst.at[pl.ds(0, NBD - 1)], sems.at[0])


def band_rows(dst, frm):
    return dst.at[:, pl.ds(pl.multiple_of(frm * 8, 8), 8), :]


def plane_maps(scols, pot, hit, mask, fourr, potp):
    low1 = low_lanes((1, 128))
    rows = lax.broadcasted_iota(jnp.int32, (256, 128), 0)
    for k in range(16):
        col = jnp.where(low1, swap(scols[2 * k : 2 * k + 1, :]), scols[2 * k + 1 : 2 * k + 2, :])
        live = col >= 0
        colp = jnp.maximum(col, 0)
        xc = div96(colp)
        xi = signed(xc) + CUT
        yi = signed(colp - xc * L) + CUT
        four = jnp.where(live, xi >> 2, -1)
        at = pl.ds(128 * k, 128)
        fourr[:, at] = jnp.broadcast_to(four, (8, 128))
        hit[:, at] = one_hot_rows(jnp.where(live, (xi & 3) * 64 + yi, -1), rows)
        for t, m in enumerate(four_masks(four)):
            mask[16 * t : 16 * t + 16, at] = m
    potp[...] = jnp.zeros((3, L, 128), F32)
    potp[:, :, 0:L] = pot[...]


def place(g, recv, hit, mask, lhs, pm):
    low = low_lanes((8, 128))
    for k in range(16):
        at = pl.ds(128 * k, 128)
        base = 256 * g + 16 * k
        r0, r1 = recv[pl.ds(base, 8), :], recv[pl.ds(base + 8, 8), :]
        hi, lo = halves(jnp.concatenate([jnp.where(low, r0, swap(r1)), jnp.where(low, swap(r0), r1)], axis=0))
        for t in range(NT):
            m = mask[16 * t : 16 * t + 16, at]
            lhs[32 * t : 32 * t + 16, at] = hi * m
            lhs[32 * t + 16 : 32 * t + 32, at] = lo * m
    out = dot_nt(lhs[...], hit[...])
    for t in range(NT):
        o = out[32 * t : 32 * t + 16] + out[32 * t + 16 : 32 * t + 32]
        for h in range(2):
            re, im = o[:8, 128 * h : 128 * h + 128], o[8:, 128 * h : 128 * h + 128]
            base = 32 * t + 16 * h
            pm[base : base + 8, :] = jnp.where(low, re, swap(im))
            pm[base + 8 : base + 16, :] = jnp.where(low, swap(re), im)


def along_y(pm, wy, tt):
    hi, lo = halves(pm[0:416, :])
    out = dot(jnp.concatenate([hi, lo], axis=1), wy[0:256, :]) + dot(hi, wy[256:384, :])
    tt[0, 0:416, :] = out[:, 0:128]
    tt[1, 0:416, :] = out[:, 128:256]
    tt[:, 416:448, :] = jnp.zeros((2, 32, 128), F32)


def along_x(g, tt, potp, wx, vx, vy, gg):
    pv = potp[g]
    pv = jnp.concatenate([pv] * 8, axis=1)
    pv = jnp.concatenate([pv, pv], axis=0)
    his, los = [], []
    for b in range(8):
        hi, lo = halves(jnp.concatenate([tt[c, pl.ds(b, 56, stride=8), :] for c in range(2)], axis=0))
        his.append(hi)
        los.append(lo)
    hi = jnp.concatenate(his, axis=1)
    u = dot(wx[...], jnp.concatenate([hi, jnp.concatenate(los, axis=1), hi], axis=0))
    hi, lo = halves(u * pv)
    t = dot(vx[...], jnp.concatenate([hi, lo, hi], axis=0))
    hi, lo = halves(jnp.concatenate(
        [jnp.concatenate([t[56 * c : 56 * c + 56, 128 * b : 128 * b + 128] for c in range(2)], axis=1) for b in range(8)],
        axis=0))
    a = dot(hi, vy[...])
    q = a[:, 0:128] + a[:, 128:256] + dot(lo, vy[:, 0:128])
    for b in range(8):
        gg[pl.ds(b, 56, stride=8), :] = q[56 * b : 56 * b + 56]


def fours(src, low):
    blocks = []
    for t in range(NT):
        cols = []
        for h in range(2):
            base = 32 * t + 16 * h
            g0, g1 = src[base : base + 8, :], src[base + 8 : base + 16, :]
            cols.append(jnp.concatenate([jnp.where(low, g0, swap(g1)), jnp.where(low, swap(g0), g1)], axis=0))
        blocks.append(jnp.concatenate(cols, axis=1))
    hi, lo = halves(jnp.concatenate(blocks, axis=0))
    return jnp.concatenate([hi, lo], axis=1)


def pick(lhs, hit, fourr, n, width):
    at = pl.ds(n * width, width)
    d = hit[:, at]
    out = dot(lhs, jnp.concatenate([d, d], axis=0))
    f = fourr[:, at]
    f = jnp.concatenate([f, f], axis=0)
    acc = jnp.zeros((16, width), F32)
    for t in range(NT):
        acc = jnp.where(f == t, out[16 * t : 16 * t + 16], acc)
    return acc


def collect(g, gg, hit, fourr, gl, send):
    low = low_lanes((8, 128))
    gl[...] = fours(gg, low)
    for n in range(8):
        acc = pick(gl[...], hit, fourr, n, 256)
        for k in range(2):
            re, im = acc[0:8, 128 * k : 128 * k + 128], acc[8:16, 128 * k : 128 * k + 128]
            base = 256 * g + 32 * n + 16 * k
            send[pl.ds(base, 8), :] = jnp.where(low, re, swap(im))
            send[pl.ds(base + 8, 8), :] = jnp.where(low, swap(re), im)


def row_side(brecv, qs):
    zero = jnp.zeros((8, 768), F32)
    for d in range(NBD):
        for j in range(3):
            g8 = 3 * d + j
            ty, r0 = g8 // 8, (g8 % 8) * 8
            re, im = brecv[2 * ty, r0 : r0 + 8, :], brecv[2 * ty + 1, r0 : r0 + 8, :]
            o = 64 * (4 * (d % 2) + d // 2) + 8 * j
            qs[o : o + 8, 0:384] = re
            qs[o : o + 8, 384:768] = im
            qs[o + 32 : o + 40, 0:384] = -im
            qs[o + 32 : o + 40, 384:768] = re
        qs[64 * d + 24 : 64 * d + 32, :] = zero
        qs[64 * d + 56 : 64 * d + 64, :] = zero


def early_gram(brecv, qs, qcat, flat, esend):
    hi, lo = halves(qs[...])
    qcat[...] = jnp.concatenate([hi, hi, lo], axis=1)
    for i in range(5):
        flat[64 * i : 64 * i + 64, 0:384] = brecv[2 * i]
        flat[64 * i : 64 * i + 64, 384:768] = brecv[2 * i + 1]
    hi, lo = halves(flat[...])
    out = dot_nt(jnp.concatenate([hi, lo, hi], axis=1), qcat[...])
    low = low_lanes((192, 128))
    zero = jnp.zeros((64, 128), F32)
    for n in range(4):
        o = out[:, 128 * n : 128 * n + 128]
        c, h = o[0:192], jnp.concatenate([o[192:256], zero, o[256:320]], axis=0)
        esend[n // 2, 2 * (n % 2)] = jnp.where(low, c, swap(h))
        esend[n // 2, 2 * (n % 2) + 1] = jnp.where(low, swap(c), h)


def term(recv, res, hit, fourr, kinr, liver, vz, hres, hsend, z, zl_):
    his, los = [], []
    for b in range(8):
        hi, lo = halves(jnp.concatenate([recv[pl.ds(256 * zl + b, 32, stride=8), :] for zl in range(3)], axis=0))
        his.append(hi)
        los.append(lo)
    hi = jnp.concatenate(his, axis=1)
    out = dot(vz[...], jnp.concatenate([hi, jnp.concatenate(los, axis=1), hi], axis=0))
    low = low_lanes((64, 128))
    for b in range(8):
        o = out[:, 128 * b : 128 * b + 128]
        other = swap(o[64:128])
        z[pl.ds(b, 64, stride=8), :] = o[0:64] + jnp.where(low, other, -other)
    zl_[...] = fours(z, low_lanes((8, 128)))
    for n in range(12):
        at = pl.ds(256 * n, 256)
        acc = pick(zl_[...], hit, fourr, n, 256)
        live = liver[:, at] > 0.0
        for c in range(2):
            v = kinr[:, at] * res[8 * c : 8 * c + 8, at] + acc[8 * c : 8 * c + 8] * (1.0 / float(L**3))
            v = jnp.where(live, v, 0.0)
            hres[c, :, at] = v
            for k in range(2):
                q = 2 * n + k
                hsend[q // 3, c, :, (q % 3) * 128 : (q % 3) * 128 + 128] = v[:, 128 * k : 128 * k + 128]


F0, F1 = 10, 22


def late_gram(hrecv, qcat, lsend, start):
    hi, lo = halves(jnp.concatenate([hrecv[0], hrecv[1]], axis=1))
    cat = jnp.concatenate([hi, lo, hi], axis=1)
    low = low_lanes((32, 128))
    mine = lax.rem(lax.axis_index("band"), 2)
    for core in (1 - mine, mine):
        out = dot_nt(cat, qcat[pl.ds(pl.multiple_of(256 * core, 256), 256), :])
        for n in range(2):
            a, b = out[0:32, 128 * n : 128 * n + 128], out[32:64, 128 * n : 128 * n + 128]
            lsend[core, 2 * n] = jnp.where(low, a, swap(b))
            lsend[core, 2 * n + 1] = jnp.where(low, swap(a), b)
        start(core, core is mine)


def late_tiles(total, la, lb, fl):
    other = swap(total)
    la[8:40, :], la[40:72, :] = total, other
    lb[8:40, :], lb[40:72, :] = other, total
    low = low_lanes((3, 128))
    for i in range(F1 - F0):
        r = 8 + 6 * (F0 + i) - 64
        fl[8 * i : 8 * i + 3, :] = jnp.where(low, la[r : r + 3, :], lb[r + 3 : r + 6, :])


class LateExchange:
    def __init__(self, src, dst, ssem, rsem):
        self.a = (src, dst, ssem, rsem)
        self.f = lax.axis_index("fft")
        self.owner = jnp.logical_and(self.f >= F0, self.f < F1)

    def start(self):
        src, dst, ssem, rsem = self.a
        f, b = self.f, lax.axis_index("band")
        to_me = dst.at[pl.ds(pl.multiple_of(8 * f, 8), 4), :]
        for i in range(F1 - F0):
            n = lax.rem(f + i, F1 - F0)
            part = src.at[pl.ds(pl.multiple_of(8 * n, 8), 4), :]

            @pl.when(n + F0 != f)
            def _():
                pltpu.make_async_remote_copy(
                    src_ref=part, dst_ref=to_me, send_sem=ssem, recv_sem=rsem, device_id=(b, n + F0),
                    device_id_type=MESH).start()

        @pl.when(self.owner)
        def _():
            own = src.at[pl.ds(pl.multiple_of(8 * (f - F0), 8), 4), :]
            pltpu.make_async_copy(own, to_me, rsem).start()

    def add(self, out, scale):
        src, dst, ssem, rsem = self.a

        @pl.when(self.owner)
        def _():
            whole(dst.at[pl.ds(0, 4 * NF), :], rsem)
            parts = [dst[8 * d : 8 * d + 4, :] for d in range(NF)]
            while len(parts) > 1:
                parts = [a + b for a, b in zip(parts[::2], parts[1::2])]
            total = parts[0] * scale
            both = jnp.concatenate([swap(total)[0:3], total[0:3], jnp.zeros((2, 128), F32)], axis=0)
            out[...] = out[...] + jnp.where(low_lanes((8, 128)), 0.0, both)

    def sent(self):
        src, dst, ssem, rsem = self.a
        whole(src.at[pl.ds(0, 44), :], ssem)
        pl.when(jnp.logical_not(self.owner))(lambda: whole(src.at[pl.ds(0, 4), :], ssem))


def step_kernel(ev_h, cur_h, hcur_h, prev_h, hprev_h, gm_h, scols_h, pot_h, wz_h, wy_h, wx_h, vx_h, vy_h,
                vz_h, hres_h, out,
                ev, cur, hcur, prev, hprev, gm, scols, pot, wz, wy, wx, vx, vy, vz, hres,
                res, kinr, gfour, liver, ghit, glhs, y, send, bsend,
                recv, brecv, shit, smask, sfour, slhs, potp, pm, pm2, tt, gg, gl, send2, recv2,
                qs, qcat, flat, esum, esend, egot, emid, erecv, z, zl, hsend, hrecv, la, lb,
                lsend, lrecv, fl, lrow, fsend, frecv, s1, r1, s3, r3, s4, s6, sems, load):
    pairs = [(ev_h, ev), (gm_h, gm), (scols_h, scols.at[pl.ds(0, NF), :]), (cur_h, cur), (hcur_h, hcur), (wz_h, wz), (prev_h, prev), (hprev_h, hprev),
             (pot_h, pot), (wy_h, wy), (wx_h, wx), (vx_h, vx), (vy_h, vy), (vz_h, vz)]
    loads = [pltpu.make_async_copy(a, b, load.at[i]) for i, (a, b) in enumerate(pairs)]
    for copy in loads[:6]:
        copy.start()
    greet_everyone()
    for copy in loads[:6]:
        copy.wait()
    x1 = FftExchange(send, recv, s1, r1)
    x2 = BandExchange(bsend, brecv, band_rows, sems.at[0], sems.at[1])
    x3 = FftExchange(send2, recv2, s3, r3)
    x4 = BandSum(esend, egot, emid, erecv, s4)
    x5 = BandExchange(hsend, hrecv, band_rows, sems.at[4], sems.at[5])
    x6 = LateSum(lsend, lrecv, s6)
    x8 = LateExchange(fl, lrow, sems.at[6], sems.at[7])
    x7 = FftExchange(fsend, frecv, sems.at[pl.ds(8, 1)], sems.at[pl.ds(9, 1)])
    residual(ev, cur, hcur, gm, scols, res, glhs, ghit, kinr, gfour, liver)
    for copy in loads[6:]:
        copy.start()
    sticks(glhs, ghit, wz, send, y)
    everyone_in()
    x1.start(0)
    for copy in loads[6:]:
        copy.wait()
    basis_rows(cur, hcur, prev, hprev, res, liver, bsend)
    x1.start(1)
    plane_maps(scols, pot, shit, smask, sfour, potp)
    x1.start(2)
    x2.start()

    pms = (pm, pm2)
    x1.wait(0)
    place(0, recv, shit, smask, slhs, pms[0])
    for g in range(3):
        if g < 2:
            x1.wait(g + 1)
        along_y(pms[g % 2], wy, tt)
        if g < 2:
            place(g + 1, recv, shit, smask, slhs, pms[(g + 1) % 2])
        along_x(g, tt, potp, wx, vx, vy, gg)
        collect(g, gg, shit, sfour, gl, send2)
        x3.start(g)
    x2.wait()
    row_side(brecv, qs)
    early_gram(brecv, qs, qcat, flat, esend)
    x4.first()
    x4.second()
    for g in range(3):
        x3.wait(g)
    term(recv2, res, ghit, gfour, kinr, liver, vz, hres, hsend, z, zl)
    x5.start()
    store = pltpu.make_async_copy(hres, hres_h, load.at[15])
    store.start()
    esum[0:192, :] = x4.total()
    fsend[...] = jnp.zeros((256, 128), F32)
    for f in range(NF):
        fsend[8 * f : 8 * f + 6, :] = esum[6 * f : 6 * f + 6, :]
    x7.start()
    fl[...] = jnp.zeros((8 * (F1 - F0), 128), F32)
    la[...] = jnp.zeros((88, 128), F32)
    lb[...] = jnp.zeros((88, 128), F32)
    x5.wait()
    late_gram(hrecv, qcat, lsend, x6.start)
    x7.wait()
    total = frecv[0:8, :]
    for d in range(1, NF):
        total = total + frecv[8 * d : 8 * d + 8, :]
    scale = 8.0 / float(L**3)
    out[...] = total * scale
    late_tiles(x6.total(), la, lb, fl)
    x8.start()
    x8.add(out, scale)
    store.wait()
    for g in range(3):
        x1.sent(g)
        x3.sent(g)
    for x in (x2, x4, x5, x6, x7, x8):
        x.sent()


def sds(*shape):
    return jax.ShapeDtypeStruct(shape, F32)


DMA = pltpu.SemaphoreType.DMA
BIG = 64 * 1024 * 1024


def local(current, h_current, previous, h_previous, eigen_values, potential, stick_cols, g_map):
    w = tables()
    gm = g_map.reshape(1, 3072)
    sc = stick_cols.reshape(NF, 128)
    vm = lambda *shape: pltpu.VMEM(shape, F32)
    v16 = lambda *shape: pltpu.VMEM(shape, BF16)
    vi = lambda *shape: pltpu.VMEM(shape, jnp.int32)
    hres, tile = pl.pallas_call(
        step_kernel, out_shape=(sds(2, 8, 3072), sds(8, 128)), in_specs=[HB] * 14, out_specs=(HB, VM),
        scratch_shapes=[
            pltpu.SMEM((8,), F32), vm(2, 8, 3072), vm(2, 8, 3072), vm(2, 8, 3072), vm(2, 8, 3072), vi(1, 3072), vi(NF + 8, 128), vm(3, L, L),
            v16(384, 192), v16(384, 256), v16(192, 336), v16(112, 576), v16(256, 256), v16(128, 288),
            vm(2, 8, 3072),
            vm(16, 3072), vm(8, 3072), vi(8, 3072), vm(8, 3072), v16(256, 3072), v16(416, 3072), vm(512, 128),
            vm(768, 128), vm(8, 10, 8, 384),
            vm(768, 128), vm(10, 64, 384), v16(256, 2048), v16(208, 2048), vi(8, 2048), v16(416, 2048),
            vm(3, L, 128), vm(416, 128), vm(416, 128), vm(2, 448, 128), vm(448, 128), v16(208, 512), vm(768, 128), vm(768, 128),
            vm(512, 768), v16(512, 2304), vm(320, 768), vm(200, 128), vm(2, 4, 192, 128), vm(4, 192, 128), vm(4, 192, 128),
            vm(4, 192, 128), vm(512, 128),
            v16(208, 512), vm(8, 2, 8, 384), vm(2, 64, 384), vm(88, 128), vm(88, 128), vm(2, 4, 32, 128), vm(8, 32, 128), vm(96, 128), vm(256, 128),
            vm(256, 128), vm(256, 128), DMA((3,)), DMA((3,)), DMA((3,)), DMA((3,)), DMA((4,)), DMA((4,)), DMA((10,)), DMA((16,))],
        compiler_params=pltpu.CompilerParams(collective_id=0, has_side_effects=True, vmem_limit_bytes=BIG), name="step",
    )(eigen_values, current, h_current, previous, h_previous, gm, sc, potential,
      w["wz"], w["wy"], w["wx"], w["vx"], w["vy"], w["vz"])
    mats = jnp.transpose(tile[0:6].reshape(6, 4, 32)[:, :, 0:24], (1, 2, 0))
    return hres, mats[0:2], mats[2:4]


def solution(mesh):
    bf = P(None, "band", "fft")
    in_specs = (bf, bf, bf, bf, P("band"), P("fft", None, None), P(), P("fft"))
    return jax.shard_map(local, mesh=mesh, in_specs=in_specs, out_specs=(bf, bf, bf), check_vma=False)
```
